32 devices in a mesh: dp: 8 (over z, y), seq: 4 (over x, core).
Axes of the slice: x: 2, y: 2, z: 4, core: 2. Of those that a mesh axis runs over, the one named last changes fastest.
Arguments:
- token_ids: int32 [32, 2, 512], P('dp', None, 'seq'), may hold values from 0 to 30719
- lengths: int32 [32, 2], P('dp'), may hold values from 64 to 512, as said below
- labeled: int32 [32], P('dp'), may hold values 0 or 1
- gold: float32 [32], P('dp'), may hold values from 0 to 1
- embed: float32 [30720, 768], P(('dp', 'seq')), may hold values from -0.3 to 0.3
- position: float32 [512, 768], P(None, ('dp', 'seq')), may hold values from -0.3 to 0.3
- attn_in: float32 [768, 2304], P(('dp', 'seq')), may hold values from -0.21875 to 0.21875
- attn_out: float32 [768, 768], P(('dp', 'seq')), may hold values from -0.875 to 0.875
- ff_in: float32 [768, 3072], P(('dp', 'seq')), may hold values from -0.21875 to 0.21875
- ff_out: float32 [3072, 768], P(('dp', 'seq')), may hold values from -0.109375 to 0.109375
- vectors: float32 [14, 768], P(None, ('dp', 'seq'))
- mom_embed: float32 [30720, 768], P(('dp', 'seq')), may hold values from -2.670288e-05 to 2.670288e-05
- mom_position: float32 [512, 768], P(None, ('dp', 'seq')), may hold values from -2.670288e-05 to 2.670288e-05
- mom_attn_in: float32 [768, 2304], P(('dp', 'seq')), may hold values from -2.670288e-05 to 2.670288e-05
- mom_attn_out: float32 [768, 768], P(('dp', 'seq')), may hold values from -2.670288e-05 to 2.670288e-05
- mom_ff_in: float32 [768, 3072], P(('dp', 'seq')), may hold values from -2.670288e-05 to 2.670288e-05
- mom_ff_out: float32 [3072, 768], P(('dp', 'seq')), may hold values from -2.670288e-05 to 2.670288e-05
- mom_vectors: float32 [14, 768], P(None, ('dp', 'seq')), may hold values from -0.00010681152 to 0.00010681152
- avg_embed: float32 [30720, 768], P(('dp', 'seq')), may hold values from -0.3 to 0.3
- avg_position: float32 [512, 768], P(None, ('dp', 'seq')), may hold values from -0.3 to 0.3
- avg_attn_in: float32 [768, 2304], P(('dp', 'seq')), may hold values from -0.21875 to 0.21875
- avg_attn_out: float32 [768, 768], P(('dp', 'seq')), may hold values from -0.875 to 0.875
- avg_ff_in: float32 [768, 3072], P(('dp', 'seq')), may hold values from -0.21875 to 0.21875
- avg_ff_out: float32 [3072, 768], P(('dp', 'seq')), may hold values from -0.109375 to 0.109375
- avg_vectors: float32 [14, 768], P(None, ('dp', 'seq')), may hold values from 0.5 to 1.5
Outputs:
- loss_sum: float32 [], replicated
- loss_count: float32 [], replicated
- grad_norm: float32 [], replicated
- new_embed: float32 [30720, 768], P(('dp', 'seq'))
- new_position: float32 [512, 768], P(None, ('dp', 'seq'))
- new_attn_in: float32 [768, 2304], P(('dp', 'seq'))
- new_attn_out: float32 [768, 768], P(('dp', 'seq'))
- new_ff_in: float32 [768, 3072], P(('dp', 'seq'))
- new_ff_out: float32 [3072, 768], P(('dp', 'seq'))
- new_vectors: float32 [14, 768], P(None, ('dp', 'seq'))
- next_mom_embed: float32 [30720, 768], P(('dp', 'seq'))
- next_mom_position: float32 [512, 768], P(None, ('dp', 'seq'))
- next_mom_attn_in: float32 [768, 2304], P(('dp', 'seq'))
- next_mom_attn_out: float32 [768, 768], P(('dp', 'seq'))
- next_mom_ff_in: float32 [768, 3072], P(('dp', 'seq'))
- next_mom_ff_out: float32 [3072, 768], P(('dp', 'seq'))
- next_mom_vectors: float32 [14, 768], P(None, ('dp', 'seq'))
- next_avg_embed: float32 [30720, 768], P(('dp', 'seq'))
- next_avg_position: float32 [512, 768], P(None, ('dp', 'seq'))
- next_avg_attn_in: float32 [768, 2304], P(('dp', 'seq'))
- next_avg_attn_out: float32 [768, 768], P(('dp', 'seq'))
- next_avg_ff_in: float32 [768, 3072], P(('dp', 'seq'))
- next_avg_ff_out: float32 [3072, 768], P(('dp', 'seq'))
- next_avg_vectors: float32 [14, 768], P(None, ('dp', 'seq'))
The draws below stay inside these ranges and needn't reach their ends.
Inputs may be any that keep to these rules, and one draw needn't show every extreme that they name: `lengths`: each group of the 8 sentences of one index of dp holds at least one sentence of exactly 512 tokens, which one drawn.
All inputs are finite; a program needn't handle non-finite values. No bound on the sum of `labeled` on one device may be relied on, other than what follows from the above.
Results may differ from the reference program's by a relative error of at most 0.012.
Values may be sent and summed in bfloat16 or wider, within the bound.
No kernel may reach another device: no remote copies, remote signals or barrier semaphores. Data moves between devices by JAX's collectives and lax.ppermute only.
A program may use at most 320 MiB of HBM per device.

```python
import math
import jax
import jax.numpy as jnp
import numpy as np
from jax import lax

HEADS = 12
HEAD_DIM = 64
D = 768
FF = 3072
VOCAB = 30720
LENGTH = 512
NVEC = 14
PAIRS_DEV = 4
PAIRS = 32


def draw_lengths(key, part):
    key = jax.random.fold_in(key, 7)
    first, second = jax.random.split(key)
    sents = PAIRS * 2
    group_size = PAIRS_DEV * 2
    lens = jax.random.randint(first, (sents,), LENGTH // 8, LENGTH + 1)
    chosen = jax.random.randint(second, (sents // group_size,), 0, group_size)
    slots = jnp.arange(sents)
    owner = jnp.repeat(chosen, group_size)
    lens = jnp.where(slots % group_size == owner, LENGTH, lens)
    return lens.reshape(PAIRS, 2).astype(jnp.int32)


def draw_vectors(key, part):
    key = jax.random.fold_in(key, 11)
    noise = jax.random.normal(key, (NVEC, D), jnp.float32)
    ramp = 0.6 + 1.2 * jnp.arange(D).astype(jnp.float32) / D
    rows = jnp.arange(NVEC)[:, None]
    is_gain = (rows == 0) | (rows == 5) | (rows == NVEC - 2)
    return jnp.where(is_gain, ramp * (1.0 + 0.1 * noise), 0.1 * noise).astype(jnp.float32)


def with_ends(result, own_key, low, largest):
    shape = result.shape
    index_at = [jax.random.randint(jax.random.fold_in(own_key, axis), (), 0, shape[axis]) for axis in range(len(shape))]
    result = result.at[tuple(index_at)].set(low)
    longest = shape.index(max(shape))
    index_at[longest] = (index_at[longest] + 1) % shape[longest]
    return result.at[tuple(index_at)].set(largest)


def block_scale(own_key, dims, cuts, smallest, high):
    def one(dim, shards_of):
        heights = jax.random.uniform(jax.random.fold_in(jax.random.fold_in(own_key, 6), dim), (shards_of,), jnp.float32, smallest / len(cuts), high / len(cuts))
        return jnp.repeat(jnp.exp(heights), dims[dim] // shards_of).reshape((-1,) + (1,) * (len(dims) - dim - 1))

    level = one(*cuts[0])
    for cut in cuts[1:]:
        level = level * one(*cut)
    return level


def cumulative_ranks(count, lean):
    portions = [(1 << 20) // math.isqrt(standing ** lean) + 1 for standing in range(1, count + 1)]
    deviation = 1 + sum(portions) // (1 << 30)
    return np.cumsum(np.array([max(1, weight // deviation) for weight in portions]))


def ranked_ids(stream_key, extent, number_of, lean):
    grid = cumulative_ranks(number_of, lean)
    pick = jax.random.randint(jax.random.fold_in(stream_key, 1), extent, 0, int(grid[number_of - 1]))
    grade = jnp.searchsorted(jnp.asarray(grid, jnp.int32), pick, side="right")
    return jax.random.permutation(jax.random.fold_in(stream_key, 2), number_of)[grade].astype(jnp.int32)


def centred(stream_key, dims, scale, reach, cuts=(), kind=jnp.bfloat16):
    level = block_scale(stream_key, dims, cuts, -0.22, 0.18) if cuts else 1.0
    array = jax.random.normal(stream_key, dims, jnp.float32) * scale * level
    return jnp.minimum(jnp.maximum(array, -reach), reach).astype(kind)


def setup_inputs(seed: int = 0) -> dict:
    seeds = jax.random.split(jax.random.key(seed), 26)
    return {
        "token_ids": with_ends(ranked_ids(seeds[0], (PAIRS, 2, LENGTH), VOCAB, 2), jax.random.fold_in(seeds[0], 3), 0, VOCAB - 1).astype(jnp.int32),
        "lengths": draw_lengths(jax.random.fold_in(seeds[25], 71), 0),
        "labeled": with_ends((jax.random.randint(seeds[2], (PAIRS,), 0, 4) < 3).astype(jnp.int32), jax.random.fold_in(seeds[2], 1), 0, 1),
        "gold": jnp.clip(1.0 * jax.random.uniform(seeds[3], (PAIRS,), jnp.float32) ** block_scale(seeds[3], (PAIRS,), ((0, 8),), -0.2, 0.2), 0.0, 1.0),
        "embed": centred(seeds[4], (VOCAB, D), 0.05, 0.3, ((0, 32),), jnp.float32),
        "position": centred(seeds[5], (LENGTH, D), 0.05, 0.3, ((1, 32),), jnp.float32),
        "attn_in": centred(seeds[6], (D, 3 * D), D ** -0.5, 0.21875, ((0, 32),), jnp.float32),
        "attn_out": centred(seeds[7], (D, D), (D // 16) ** -0.5, 0.875, ((0, 32),), jnp.float32),
        "ff_in": centred(seeds[8], (D, FF), D ** -0.5, 0.21875, ((0, 32),), jnp.float32),
        "ff_out": centred(seeds[9], (FF, D), FF ** -0.5, 0.109375, ((0, 32),), jnp.float32),
        "vectors": draw_vectors(jax.random.fold_in(seeds[25], 71), 0),
        "mom_embed": centred(seeds[11], (VOCAB, D), (0.01 * ((VOCAB + LENGTH + 4 * D + 2 * FF) * D) ** -0.5), 2.6702880859375e-05, ((0, 32),), jnp.float32),
        "mom_position": centred(seeds[12], (LENGTH, D), (0.01 * ((VOCAB + LENGTH + 4 * D + 2 * FF) * D) ** -0.5), 2.6702880859375e-05, ((1, 32),), jnp.float32),
        "mom_attn_in": centred(seeds[13], (D, 3 * D), (0.01 * ((VOCAB + LENGTH + 4 * D + 2 * FF) * D) ** -0.5), 2.6702880859375e-05, ((0, 32),), jnp.float32),
        "mom_attn_out": centred(seeds[14], (D, D), (0.01 * ((VOCAB + LENGTH + 4 * D + 2 * FF) * D) ** -0.5), 2.6702880859375e-05, ((0, 32),), jnp.float32),
        "mom_ff_in": centred(seeds[15], (D, FF), (0.01 * ((VOCAB + LENGTH + 4 * D + 2 * FF) * D) ** -0.5), 2.6702880859375e-05, ((0, 32),), jnp.float32),
        "mom_ff_out": centred(seeds[16], (FF, D), (0.01 * ((VOCAB + LENGTH + 4 * D + 2 * FF) * D) ** -0.5), 2.6702880859375e-05, ((0, 32),), jnp.float32),
        "mom_vectors": centred(seeds[17], (NVEC, D), (0.04 * ((VOCAB + LENGTH + 4 * D + 2 * FF) * D) ** -0.5), 0.00010681152, ((1, 32),), jnp.float32),
        "avg_embed": centred(seeds[18], (VOCAB, D), 0.05, 0.3, ((0, 32),), jnp.float32),
        "avg_position": centred(seeds[19], (LENGTH, D), 0.05, 0.3, ((1, 32),), jnp.float32),
        "avg_attn_in": centred(seeds[20], (D, 3 * D), D ** -0.5, 0.21875, ((0, 32),), jnp.float32),
        "avg_attn_out": centred(seeds[21], (D, D), (D // 16) ** -0.5, 0.875, ((0, 32),), jnp.float32),
        "avg_ff_in": centred(seeds[22], (D, FF), D ** -0.5, 0.21875, ((0, 32),), jnp.float32),
        "avg_ff_out": centred(seeds[23], (FF, D), FF ** -0.5, 0.109375, ((0, 32),), jnp.float32),
        "avg_vectors": jnp.clip(1.0 + 0.1 * jax.random.normal(seeds[24], (NVEC, D), jnp.float32), 0.5, 1.5),
    }


EPS = 1e-06
HIGH = lax.Precision.HIGHEST
RATE = 10000.0
MOMENT = 0.5
DECAY = 0.5
CLIP = 0.01

@jax.custom_vjp
def low(v):
    return lax.optimization_barrier(v.astype(jnp.bfloat16)).astype(jnp.float32)

@jax.custom_vjp
def low_back(v):
    return v

def low_keep(v):
    return (low(v), None)

def low_pass(kept, grad):
    return (grad,)

def back_keep(v):
    return (v, None)

def back_low(kept, grad):
    return (low(grad),)
low.defvjp(low_keep, low_pass)
low_back.defvjp(back_keep, back_low)

def rounded(v):
    return low_back(low(v))

def layer_norm(v, gain, bias):
    center = v - lax.optimization_barrier(jnp.mean(v, axis=-1, keepdims=True))
    spread = lax.optimization_barrier(jnp.mean(center * center, axis=-1, keepdims=True))
    return center * lax.rsqrt(spread + EPS) * gain + bias

def matmul(left, right):
    return jnp.dot(left, right, precision=HIGH)

def encode(used, ids, lens):
    embed, position, attn_in, attn_out, ff_in, ff_out, vec = used
    count = ids.shape[0]
    width = HEADS * HEAD_DIM
    h0 = layer_norm(embed[ids] + position[None], vec[0], vec[1])
    bias = jnp.concatenate([vec[2], jnp.zeros_like(vec[2]), vec[3]])
    proj = rounded(matmul(low(h0), attn_in) + bias)
    query = proj[..., :width].reshape(count, LENGTH, HEADS, HEAD_DIM)
    keys = proj[..., width:2 * width].reshape(count, LENGTH, HEADS, HEAD_DIM)
    values = proj[..., 2 * width:].reshape(count, LENGTH, HEADS, HEAD_DIM)
    score = low_back(jnp.einsum('sqhd,skhd->shqk', query, keys, precision=HIGH) * 0.125)
    live = jnp.arange(LENGTH)[None, :] < lens[:, None]
    score = jnp.where(live[:, None, None, :], score, -1e+30)
    prob = jax.nn.softmax(score, axis=-1)
    out = jnp.einsum('shqk,skhd->sqhd', low(prob), values, precision=HIGH).reshape(count, LENGTH, width)
    out = rounded(out)
    branch = low_back(matmul(out, attn_out) + vec[4])
    h1 = layer_norm(h0 + branch, vec[5], vec[6])
    hidden = low_back(matmul(low(h1), ff_in) + vec[7:7 + FF // width].reshape(-1))
    act = low(jax.nn.gelu(hidden, approximate=False))
    mixed = low_back(matmul(act, ff_out) + vec[7 + FF // width])
    h2 = layer_norm(h1 + mixed, vec[8 + FF // width], vec[9 + FF // width])
    keep = live.astype(jnp.float32)
    return lax.optimization_barrier(jnp.sum(h2 * keep[:, :, None], axis=1)) / lens[:, None].astype(jnp.float32)

def reference(token_ids, lengths, labeled, gold, embed, position, attn_in, attn_out, ff_in, ff_out, vectors, mom_embed, mom_position, mom_attn_in, mom_attn_out, mom_ff_in, mom_ff_out, mom_vectors, avg_embed, avg_position, avg_attn_in, avg_attn_out, avg_ff_in, avg_ff_out, avg_vectors):
    weights = (embed, position, attn_in, attn_out, ff_in, ff_out, vectors)
    groups = token_ids.reshape(PAIRS // PAIRS_DEV, 2 * PAIRS_DEV, LENGTH)
    group_lens = lengths.reshape(PAIRS // PAIRS_DEV, 2 * PAIRS_DEV)
    lab = labeled.astype(jnp.float32)

    def loss_fn(params):
        used = tuple((low(w) for w in params))
        pooled = lax.map(jax.checkpoint(lambda item: encode(used, item[0], item[1])), (groups, group_lens))
        pooled = pooled.reshape(PAIRS, 2, HEADS * HEAD_DIM)
        first, second = (pooled[:, 0], pooled[:, 1])
        cos = lax.optimization_barrier(jnp.sum(first * second, axis=-1)) * lax.rsqrt(lax.optimization_barrier(jnp.sum(first * first, axis=-1)) + EPS) * lax.rsqrt(lax.optimization_barrier(jnp.sum(second * second, axis=-1)) + EPS)
        miss = cos - gold
        total = jnp.sum(lab * miss * miss)
        count = jnp.maximum(jnp.sum(lab), 1.0)
        return (total / count, (total, count))
    value, pull, aux = jax.vjp(loss_fn, weights, has_aux=True)
    grads = pull(jnp.ones_like(value))[0]
    squares = sum((jnp.sum(g * g) for g in grads))
    norm = jnp.sqrt(squares)
    scale = jnp.minimum(1.0, CLIP / (norm + 1e-06))
    moms = (mom_embed, mom_position, mom_attn_in, mom_attn_out, mom_ff_in, mom_ff_out, mom_vectors)
    avgs = (avg_embed, avg_position, avg_attn_in, avg_attn_out, avg_ff_in, avg_ff_out, avg_vectors)
    news, next_moms, next_avgs = ([], [], [])
    for weight, grad, mom, avg in zip(weights, grads, moms, avgs):
        clipped = grad * scale
        moment = MOMENT * mom + clipped
        fresh = weight - RATE * (clipped + MOMENT * moment)
        news.append(fresh)
        next_moms.append(moment)
        next_avgs.append(DECAY * avg + (1.0 - DECAY) * fresh)
    return (aux[0], aux[1], norm, news[0], news[1], news[2], news[3], news[4], news[5], news[6], next_moms[0], next_moms[1], next_moms[2], next_moms[3], next_moms[4], next_moms[5], next_moms[6], next_avgs[0], next_avgs[1], next_avgs[2], next_avgs[3], next_avgs[4], next_avgs[5], next_avgs[6])
```

```python
import jax
import jax.numpy as jnp
from jax import lax
from jax.sharding import PartitionSpec as P

HEADS = 12
HEAD_DIM = 64
EPS = 1e-06
RATE = 10000.0
MOMENT = 0.5
DECAY = 0.5
CLIP = 0.01
SLOTS = 32
AXES = ("dp", "seq")
bf = jnp.bfloat16
f32 = jnp.float32


def layer_norm(v, gain, bias):
    center = v - jnp.mean(v, axis=-1, keepdims=True)
    spread = jnp.mean(center * center, axis=-1, keepdims=True)
    return center * lax.rsqrt(spread + EPS) * gain + bias


def exact_gelu(v):
    return jax.nn.gelu(v, approximate=False)


def mm(left, right):
    return jnp.dot(left, right, preferred_element_type=f32)


def mm_left(left, right):
    return lax.dot_general(left, right, (((0,), (0,)), ((), ())), preferred_element_type=f32)


def mm_right(left, right):
    return lax.dot_general(left, right, (((1,), (1,)), ((), ())), preferred_element_type=f32)


def exchange(v):
    return lax.all_to_all(v, AXES, 0, 0, tiled=True)


def route(ids, valid, per_owner):
    count = ids.shape[0]
    spot = jnp.arange(count, dtype=jnp.int32)
    owner = ids // per_owner
    local = ids - owner * per_owner
    key = jnp.where(valid, ids, -1 - spot)
    alike = key[:, None] == key[None, :]
    first_at = jnp.min(jnp.where(alike, spot[None, :], count), axis=1)
    first = (first_at == spot) & valid
    before = (owner[:, None] == owner[None, :]) & first[None, :] & (spot[None, :] < first_at[:, None])
    rank = jnp.sum(before.astype(jnp.int32), axis=1)
    return owner, local, first, rank


def requests(owner, local, first, rank, start, devices):
    slot = jnp.where(first & (rank >= start) & (rank < start + SLOTS), owner * SLOTS + rank - start, -1)
    line = jnp.arange(devices * SLOTS, dtype=jnp.int32)
    hit = slot[None, :] == line[:, None]
    return jnp.max(jnp.where(hit, local[None, :], -1), axis=1)


def token_slots(owner, valid, rank, start):
    return jnp.where(valid & (rank >= start) & (rank < start + SLOTS), owner * SLOTS + rank - start, -1)


def one_hot(index, size):
    return (index[:, None] == jnp.arange(size, dtype=jnp.int32)[None, :]).astype(bf)


def forward_backward(summed, weights, vec, lens, labeled, gold, count):
    w_qkv, w_out, w_in, w_back = weights
    sents, length, width = summed.shape
    rows = sents * length
    hidden_rows = w_in.shape[1] // width
    h0, back_embed = jax.vjp(layer_norm, summed.reshape(rows, width), vec[0], vec[1])
    hin = h0.astype(bf)
    bias = jnp.concatenate([vec[2], jnp.zeros_like(vec[2]), vec[3]])
    proj = (mm(hin, w_qkv) + bias).astype(bf).reshape(sents, length, 3, HEADS, HEAD_DIM)
    query, keys, values = (proj[:, :, i].transpose(0, 2, 1, 3) for i in range(3))
    live = (jnp.arange(length)[None, :] < lens[:, None])
    mask = live[:, None, None, :]
    raw = jnp.einsum("shqd,shkd->shqk", query, keys, preferred_element_type=f32) * 0.125
    raw = jnp.where(mask, raw, -1e30)
    top = jnp.max(raw, axis=-1, keepdims=True)
    power = jnp.exp(raw - top)
    prob = power / jnp.sum(power, axis=-1, keepdims=True)
    prob_b = prob.astype(bf)
    out = jnp.einsum("shqk,shkd->shqd", prob_b, values, preferred_element_type=f32).astype(bf)
    out_b = out.transpose(0, 2, 1, 3).reshape(rows, width)
    branch = mm(out_b, w_out) + vec[4]
    h1, back_one = jax.vjp(layer_norm, h0 + branch, vec[5], vec[6])
    h1_b = h1.astype(bf)
    hidden = mm(h1_b, w_in) + vec[7 : 7 + hidden_rows].reshape(-1)
    act, back_act = jax.vjp(exact_gelu, hidden)
    act_b = act.astype(bf)
    mixed = mm(act_b, w_back) + vec[7 + hidden_rows]
    h2, back_two = jax.vjp(layer_norm, h1 + mixed, vec[8 + hidden_rows], vec[9 + hidden_rows])
    keep = live.astype(f32)
    pooled_sum = jnp.sum(h2.reshape(sents, length, width) * keep[:, :, None], axis=1)

    def head(total):
        pooled = (total / lens.astype(f32)[:, None]).reshape(sents // 2, 2, width)
        first, second = pooled[:, 0], pooled[:, 1]
        cos = (
            jnp.sum(first * second, axis=-1)
            * lax.rsqrt(jnp.sum(first * first, axis=-1) + EPS)
            * lax.rsqrt(jnp.sum(second * second, axis=-1) + EPS)
        )
        miss = cos - gold
        return jnp.sum(labeled * miss * miss)

    loss, back_head = jax.vjp(head, pooled_sum)
    d_pooled = back_head(1.0 / count)[0]
    d_h2 = (keep[:, :, None] * d_pooled[:, None, :]).reshape(rows, width)

    d_r2, d_g2, d_b2n = back_two(d_h2)
    d_y = d_r2.astype(bf)
    g_ff_out = mm_left(act_b, d_y)
    d_f = back_act(mm_right(d_y, w_back))[0].astype(bf)
    g_ff_in = mm_left(h1_b, d_f)
    d_r1, d_g1, d_b1 = back_one(d_r2 + mm_right(d_f, w_in))
    d_a = d_r1.astype(bf)
    g_attn_out = mm_left(out_b, d_a)
    d_out = mm_right(d_a, w_out).astype(bf).reshape(sents, length, HEADS, HEAD_DIM).transpose(0, 2, 1, 3)
    d_value = jnp.einsum("shqk,shqd->shkd", prob_b, d_out, preferred_element_type=f32)
    d_prob = jnp.einsum("shqd,shkd->shqk", d_out, values, preferred_element_type=f32)
    d_score = (prob * (d_prob - jnp.sum(prob * d_prob, axis=-1, keepdims=True))).astype(bf)
    d_query = jnp.einsum("shqk,shkd->shqd", d_score, keys, preferred_element_type=f32) * 0.125
    d_key = jnp.einsum("shqk,shqd->shkd", d_score, query, preferred_element_type=f32) * 0.125
    d_proj = jnp.concatenate(
        [d.astype(bf).transpose(0, 2, 1, 3).reshape(rows, width) for d in (d_query, d_key, d_value)], axis=1
    )
    g_attn_in = mm_left(hin, d_proj)
    d_h0 = d_r1 + mm_right(d_proj, w_qkv)
    bias_sums = jnp.sum(d_proj.astype(f32), axis=0)
    d_x, d_ge, d_be = back_embed(d_h0)
    g_vectors = jnp.concatenate(
        [
            jnp.stack([d_ge, d_be, bias_sums[:width], bias_sums[2 * width :], jnp.sum(d_a.astype(f32), axis=0), d_g1, d_b1]),
            jnp.sum(d_f.astype(f32), axis=0).reshape(hidden_rows, width),
            jnp.stack([jnp.sum(d_y.astype(f32), axis=0), d_g2, d_b2n]),
        ],
        axis=0,
    )
    return loss, (g_attn_in, g_attn_out, g_ff_in, g_ff_out), g_vectors, d_x


def body(
    token_ids, lengths, labeled, gold,
    embed, position, attn_in, attn_out, ff_in, ff_out, vectors,
    mom_embed, mom_position, mom_attn_in, mom_attn_out, mom_ff_in, mom_ff_out, mom_vectors,
    avg_embed, avg_position, avg_attn_in, avg_attn_out, avg_ff_in, avg_ff_out, avg_vectors,
):
    pairs_here, _, local = token_ids.shape
    seq = lax.axis_size("seq")
    devices = lax.axis_size("dp") * seq
    length = local * seq
    per_owner, width = embed.shape
    depth = attn_in.shape[0]
    hidden = ff_in.shape[1]
    nvec = vectors.shape[0]
    turns = ff_out.shape[0] // depth
    mine = pairs_here // seq
    sents = 2 * mine
    rows = sents * length
    spare = 128 - nvec

    shard = jnp.concatenate(
        [attn_in, attn_out, ff_in]
        + [ff_out[i * depth : (i + 1) * depth] for i in range(turns)]
        + [position.T, vectors.T, jnp.zeros((depth, spare), f32)],
        axis=1,
    ).astype(bf)
    full = lax.all_gather(shard, AXES, axis=0, tiled=True)

    ids = lax.all_to_all(token_ids, "seq", 0, 2, tiled=True).reshape(rows)
    turn = lax.axis_index("seq") * mine
    lens = lax.dynamic_slice_in_dim(lengths, turn, mine, 0).reshape(sents)
    lab = lax.dynamic_slice_in_dim(labeled, turn, mine, 0)
    goal = lax.dynamic_slice_in_dim(gold, turn, mine, 0)
    lab_f = lab.astype(f32)
    used = (jnp.arange(length)[None, :] < lens[:, None]) & (jnp.repeat(lab, 2) > 0)[:, None]
    used = used.reshape(rows)
    owner, place, first, rank = route(ids, used, per_owner)
    most = jnp.max(jnp.where(used, rank + 1, 0))
    asked = requests(owner, place, first, rank, 0, devices).reshape(devices, SLOTS)
    note = jnp.stack([most, jnp.sum(lab)])[None, :]
    note = jnp.broadcast_to(note, (devices, 2))
    got = exchange(jnp.concatenate([asked, note, jnp.zeros((devices, 126 - SLOTS), jnp.int32)], axis=1))
    rounds = (jnp.max(got[:, SLOTS]) + SLOTS - 1) // SLOTS
    count = jnp.maximum(jnp.sum(got[:, SLOTS + 1]).astype(f32), 1.0)

    table = embed.astype(bf)

    def fetch(wanted, start):
        picked = mm(one_hot(wanted, per_owner), table).astype(bf).reshape(devices, SLOTS, width)
        back = exchange(picked).reshape(devices * SLOTS, width)
        return mm(one_hot(token_slots(owner, used, rank, start), devices * SLOTS), back)

    wanted_first = got[:, :SLOTS].reshape(-1)
    found = fetch(wanted_first, 0)

    def more(state):
        step, total = state
        start = step * SLOTS
        wanted = exchange(requests(owner, place, first, rank, start, devices).reshape(devices, SLOTS)).reshape(-1)
        return step + 1, total + fetch(wanted, start)

    _, found = lax.while_loop(lambda state: state[0] < rounds, more, (jnp.int32(1), found))

    at = 3 * width
    w_qkv, w_out, w_in = full[:, :at], full[:, at : at + width], full[:, at + width : at + width + hidden]
    at = at + width + hidden
    w_back = (
        full[:, at : at + turns * width].reshape(devices, depth, turns, width).transpose(0, 2, 1, 3).reshape(hidden, width)
    )
    at = at + turns * width
    pos = full[:, at : at + length].T.astype(f32)
    vec = full[:, at + length : at + length + nvec].T.astype(f32)

    summed = found.reshape(sents, length, width) + pos[None]
    loss, mats, g_vec, d_x = forward_backward(summed, (w_qkv, w_out, w_in, w_back), vec, lens, lab_f, goal, count)

    scatter = lambda g: lax.psum_scatter(g.astype(bf), AXES, scatter_dimension=0, tiled=True).astype(f32)
    g_ff_out = scatter(mats[3])
    g_ff_in = scatter(mats[2])
    d_xb = d_x.astype(bf)
    g_rest = scatter(
        jnp.concatenate(
            [mats[0], mats[1], jnp.sum(d_x.reshape(sents, length, width), axis=0).T, g_vec.T, jnp.zeros((width, spare), f32)],
            axis=1,
        )
    )
    g_attn_in, g_attn_out = g_rest[:, : 3 * width], g_rest[:, 3 * width : 4 * width]
    g_position = g_rest[:, 4 * width : 4 * width + length].T
    g_vectors = g_rest[:, 4 * width + length : 4 * width + length + nvec].T

    def give(wanted, start):
        sums = mm_left(one_hot(token_slots(owner, used, rank, start), devices * SLOTS), d_xb).astype(bf)
        back = exchange(sums.reshape(devices, SLOTS, width)).reshape(devices * SLOTS, width)
        return mm_left(one_hot(wanted, per_owner), back)

    g_embed = give(wanted_first, 0)

    def more_back(state):
        step, total = state
        start = step * SLOTS
        wanted = exchange(requests(owner, place, first, rank, start, devices).reshape(devices, SLOTS)).reshape(-1)
        return step + 1, total + give(wanted, start)

    _, g_embed = lax.while_loop(lambda state: state[0] < rounds, more_back, (jnp.int32(1), g_embed))

    grads = (g_embed, g_position, g_attn_in, g_attn_out, g_ff_in, g_ff_out, g_vectors)
    squares = sum(jnp.sum(g * g) for g in grads)
    sums = exchange(jnp.broadcast_to(jnp.stack([squares, loss])[None, :], (devices, 2)))
    sums = jnp.sum(sums, axis=0)
    norm = jnp.sqrt(sums[0])
    loss_sum = sums[1]
    scale = jnp.minimum(1.0, CLIP / (norm + 1e-06))
    weights = (embed, position, attn_in, attn_out, ff_in, ff_out, vectors)
    moms = (mom_embed, mom_position, mom_attn_in, mom_attn_out, mom_ff_in, mom_ff_out, mom_vectors)
    avgs = (avg_embed, avg_position, avg_attn_in, avg_attn_out, avg_ff_in, avg_ff_out, avg_vectors)
    news, next_moms, next_avgs = [], [], []
    for weight, grad, mom, avg in zip(weights, grads, moms, avgs):
        clipped = grad * scale
        moment = MOMENT * mom + clipped
        fresh = weight - RATE * (clipped + MOMENT * moment)
        news.append(fresh)
        next_moms.append(moment)
        next_avgs.append(DECAY * avg + (1.0 - DECAY) * fresh)
    return (loss_sum, count, norm, *news, *next_moms, *next_avgs)


def solution(mesh):
    whole = (
        P(AXES, None),
        P(None, AXES),
        P(AXES, None),
        P(AXES, None),
        P(AXES, None),
        P(AXES, None),
        P(None, AXES),
    )
    return jax.shard_map(
        body,
        mesh=mesh,
        in_specs=(P("dp", None, "seq"), P("dp", None), P("dp"), P("dp")) + whole * 3,
        out_specs=(P(), P(), P()) + whole * 3,
        check_vma=False,
    )
```

```python
import functools

import jax
import jax.numpy as jnp
from jax import lax
from jax.experimental import pallas as pl
from jax.experimental.pallas import tpu as pltpu
from jax.sharding import PartitionSpec as P

HEADS = 12
HEAD_DIM = 64
EPS = 1e-06
RATE = 10000.0
MOMENT = 0.5
DECAY = 0.5
CLIP = 0.01
SLOTS = 32
GROUP = 128
ROWS = 256
AXES = ("dp", "seq")
bf = jnp.bfloat16
f32 = jnp.float32


def mm(left, right):
    return jnp.dot(left, right, preferred_element_type=f32)


def mm_left(left, right):
    return lax.dot_general(left, right, (((0,), (0,)), ((), ())), preferred_element_type=f32)


def mm_right(left, right):
    return lax.dot_general(left, right, (((1,), (1,)), ((), ())), preferred_element_type=f32)


def exchange(v):
    return lax.all_to_all(v, AXES, 0, 0, tiled=True)


def route(ids, valid, per_owner):
    count = ids.shape[0]
    spot = jnp.arange(count, dtype=jnp.int32)
    owner = ids // per_owner
    local = ids - owner * per_owner
    key = jnp.where(valid, ids, -1 - spot)
    alike = key[:, None] == key[None, :]
    first_at = jnp.min(jnp.where(alike, spot[None, :], count), axis=1)
    first = (first_at == spot) & valid
    before = (owner[:, None] == owner[None, :]) & first[None, :] & (spot[None, :] < first_at[:, None])
    rank = jnp.sum(before.astype(jnp.int32), axis=1)
    return owner, local, first, rank


def requests(owner, local, first, rank, start, devices):
    slot = jnp.where(first & (rank >= start) & (rank < start + SLOTS), owner * SLOTS + rank - start, -1)
    line = jnp.arange(devices * SLOTS, dtype=jnp.int32)
    hit = slot[None, :] == line[:, None]
    return jnp.max(jnp.where(hit, local[None, :], -1), axis=1)


def token_slots(owner, valid, rank, start):
    return jnp.where(valid & (rank >= start) & (rank < start + SLOTS), owner * SLOTS + rank - start, -1)


def one_hot(index, size):
    return (index[:, None] == jnp.arange(size, dtype=jnp.int32)[None, :]).astype(bf)


NEAR = 0.3
TAIL = (
    0.11962924781130464, 0.12075473126046088, 0.09990870957740686, 0.12857719637511858,
    -0.05371263258867769, 0.2063844888355699, -0.15722075016774184, 0.03567893567949022,
)


def dot(left, right):
    return jnp.dot(left, right, preferred_element_type=f32)


def dot_nt(left, right):
    return lax.dot_general(left, right, (((1,), (1,)), ((), ())), preferred_element_type=f32)


def dot_tn(left, right):
    return lax.dot_general(left, right, (((0,), (0,)), ((), ())), preferred_element_type=f32)


def iota(shape, axis):
    return lax.broadcasted_iota(jnp.int32, shape, axis)


def normal(v):
    center = v - jnp.mean(v, axis=-1, keepdims=True)
    scale = lax.rsqrt(jnp.mean(center * center, axis=-1, keepdims=True) + EPS)
    return center * scale, scale


def normal_back(grad, unit, scale):
    inner = jnp.mean(grad * unit, axis=-1, keepdims=True)
    return scale * (grad - jnp.mean(grad, axis=-1, keepdims=True) - unit * inner)


def column_sums(v):
    return dot(jnp.full((8, v.shape[0]), 1.0, bf), v)[:1]


def gelu_pair(v):
    bell = jnp.exp(v * v * -0.5)
    t = 1.0 / (1.0 + NEAR * jnp.abs(v))
    poly = TAIL[-1]
    for c in TAIL[-2::-1]:
        poly = poly * t + c
    tail = poly * t * bell
    area = jnp.where(v < 0, tail, 1.0 - tail)
    return v * area, area + v * bell * 0.3989422804014327


def params(limit, **more):
    return pltpu.CompilerParams(vmem_limit_bytes=limit << 20, **more)


def fixed(shape, index):
    return pl.BlockSpec(shape, lambda *_: index, pipeline_mode=pl.Buffered(1))


def spread_kernel(depth, turns, width, src, out):
    tall = src[...].astype(f32)
    parts = []
    for e in range(2):
        for j in range(turns):
            parts.append(tall[e * depth : (e + 1) * depth, j * width : (j + 1) * width])
    out[...] = jnp.concatenate(parts, axis=0).astype(bf)


def first_kernel(slot, back, extra, w_qkv, pos_t, vec_t, x_out, hin_out, qkv_out, vec_out):
    rows, width = x_out.shape
    length = pos_t.shape[1]
    vec = dot_nt((iota((16, 128), 0) == iota((16, 128), 1)).astype(f32).astype(bf), vec_t[...])
    vec_out[...] = vec
    where = jnp.where(slot[...] == iota((rows, back.shape[0]), 1), 1.0, 0.0).astype(bf)
    begin = lax.rem(pl.program_id(0), length // rows) * rows
    line = jnp.where(iota((rows, length), 0) + begin == iota((rows, length), 1), 1.0, 0.0).astype(bf)
    x = dot(where, back[...]) + extra[...].astype(f32) + dot_nt(line, pos_t[...])
    x_out[...] = x
    unit, _ = normal(x)
    hin = (unit * vec[0:1] + vec[1:2]).astype(bf)
    hin_out[...] = hin
    qkv_out[:, :width] = (dot(hin, w_qkv[:, :width]) + vec[2:3]).astype(bf)
    qkv_out[:, width : 2 * width] = dot(hin, w_qkv[:, width : 2 * width]).astype(bf)
    qkv_out[:, 2 * width :] = (dot(hin, w_qkv[:, 2 * width :]) + vec[3:4]).astype(bf)


def head_parts(lens, query, keys, half):
    length = query.shape[0]
    lane = iota((length, GROUP), 1)
    inside = (lane // HEAD_DIM) == half
    spare = lane == (1 - half) * HEAD_DIM
    dead = iota((length, GROUP), 0) >= lens
    key = jnp.where(inside, keys.astype(f32), jnp.where(spare & dead, -1e30, 0.0)).astype(bf)
    ask = jnp.where(inside, query.astype(f32) * 0.125, jnp.where(spare, 1.0, 0.0)).astype(bf)
    return inside, ask, key


def attend_kernel(lens, query, keys, values, out):
    size = lens[pl.program_id(0)]
    total = None
    for half in range(2):
        inside, ask, key = head_parts(size, query[...], keys[...], half)
        score = dot_nt(ask, key)
        power = jnp.exp(score - jnp.max(score, axis=1, keepdims=True))
        prob = (power * (1.0 / jnp.sum(power, axis=1, keepdims=True))).astype(bf)
        part = dot(prob, jnp.where(inside, values[...].astype(f32), 0.0).astype(bf))
        total = part if total is None else total + part
    out[...] = total.astype(bf)


def attend_back_kernel(lens, query, keys, values, d_out, d_proj):
    size = lens[pl.program_id(0)]
    d_query, d_key, d_value = None, None, None
    add = lambda a, b: b if a is None else a + b
    for half in range(2):
        inside, ask, key = head_parts(size, query[...], keys[...], half)
        clean = lambda v: jnp.where(inside, v.astype(f32), 0.0).astype(bf)
        score = dot_nt(key, ask)
        power = jnp.exp(score - jnp.max(score, axis=0, keepdims=True))
        prob = power * (1.0 / jnp.sum(power, axis=0, keepdims=True))
        grad = clean(d_out[...])
        d_value = add(d_value, dot(prob.astype(bf), grad))
        d_prob = dot_nt(values[...], grad)
        inner = jnp.sum(prob * d_prob, axis=0, keepdims=True)
        d_score = (prob * (d_prob - inner)).astype(bf)
        d_key = add(d_key, dot(d_score, clean(ask)))
        d_query = add(d_query, dot_tn(d_score, clean(key)))
    d_proj[0] = (d_query * 0.125).astype(bf)
    d_proj[1] = d_key.astype(bf)
    d_proj[2] = d_value.astype(bf)


def middle_kernel(per_sent, lens, x, mixed, w_out, w_in, w_back, vec, vec_ff, z1_out, h1_out, act_out, slope_out, z2_out, pooled):
    rows, width = x.shape
    step = pl.program_id(0)
    unit, _ = normal(x[...])
    h0 = unit * vec[0:1] + vec[1:2]
    z1 = h0 + dot(mixed[...], w_out[...]) + vec[4:5]
    z1_out[...] = z1
    unit, _ = normal(z1)
    h1 = unit * vec[5:6] + vec[6:7]
    h1_b = h1.astype(bf)
    h1_out[...] = h1_b
    turns = w_in.shape[1] // width
    y = None
    for j in range(turns):
        at = slice(j * width, (j + 1) * width)
        hidden = dot(h1_b, w_in[:, at]) + vec_ff[:, at]
        act, slope = gelu_pair(hidden)
        act = act.astype(bf)
        act_out[:, at] = act
        slope_out[:, at] = slope.astype(bf)
        part = dot(act, w_back[at, :])
        y = part if y is None else y + part
    z2 = h1 + y + vec[7 + turns : 8 + turns]
    z2_out[...] = z2
    unit, _ = normal(z2)
    h2 = unit * vec[8 + turns : 9 + turns] + vec[9 + turns : 10 + turns]
    sent = step // per_sent
    begin = lax.rem(step, per_sent) * rows
    keep = iota((rows, width), 0) + begin < lens[sent]
    sums = jnp.sum(jnp.where(keep, h2, 0.0), axis=0, keepdims=True)

    @pl.when(step == 0)
    def _():
        pooled[...] = jnp.zeros_like(pooled)

    pooled[...] += jnp.where(iota(pooled.shape, 0) == sent, sums, 0.0)


def back_kernel(per_sent, lens, facts, pooled, z1, slope, z2, w_out, w_in, w_back, vec, d_y_out, d_f_out, d_r1_out, d_a_out, d_o_out, sums, sums_ff, loss):
    rows, width = z1.shape
    step = pl.program_id(0)
    sent = step // per_sent
    labeled, gold, count = facts[0], facts[1], facts[2]
    size = [lens[i].astype(f32) for i in range(2)]
    side = [pooled[i : i + 1] / size[i] for i in range(2)]
    total = lambda a, b: jnp.sum(a * b, axis=1, keepdims=True)
    cross = total(side[0], side[1])
    root = [lax.rsqrt(total(s, s) + EPS) for s in side]
    miss = cross * root[0] * root[1] - gold
    loss[...] = jnp.broadcast_to(labeled * miss * miss, loss.shape)
    push = 2.0 * labeled * miss / count
    grads = [
        push * (side[1 - i] * root[0] * root[1] - cross * root[i] * root[i] * root[i] * root[1 - i] * side[i]) / size[i]
        for i in range(2)
    ]
    d_pooled = jnp.where(sent == 0, grads[0], grads[1])
    begin = lax.rem(step, per_sent) * rows
    keep = iota((rows, width), 0) + begin < lens[sent]
    d_h2 = jnp.where(keep, d_pooled, 0.0)
    turns = w_in.shape[1] // width

    unit, scale = normal(z2[...])
    d_g2 = jnp.sum(d_h2 * unit, axis=0, keepdims=True)
    d_b2n = jnp.sum(d_h2, axis=0, keepdims=True)
    d_r2 = normal_back(d_h2 * vec[8 + turns : 9 + turns], unit, scale)
    d_y = d_r2.astype(bf)
    d_y_out[...] = d_y
    d_h1 = d_r2
    ff = []
    for j in range(turns):
        at = slice(j * width, (j + 1) * width)
        d_f = (dot_nt(d_y, w_back[at, :]) * slope[:, at].astype(f32)).astype(bf)
        d_f_out[:, at] = d_f
        ff.append(column_sums(d_f))
        d_h1 = d_h1 + dot_nt(d_f, w_in[:, at])
    unit, scale = normal(z1[...])
    d_g1 = jnp.sum(d_h1 * unit, axis=0, keepdims=True)
    d_b1 = jnp.sum(d_h1, axis=0, keepdims=True)
    d_r1 = normal_back(d_h1 * vec[5:6], unit, scale)
    d_r1_out[...] = d_r1
    d_a = d_r1.astype(bf)
    d_a_out[...] = d_a
    d_o_out[...] = dot_nt(d_a, w_out[...]).astype(bf)
    fresh = jnp.concatenate([column_sums(d_a), d_g1, d_b1, column_sums(d_y), d_g2, d_b2n, d_g2, d_b2n], axis=0)

    @pl.when(step == 0)
    def _():
        sums[...] = jnp.zeros_like(sums)
        sums_ff[...] = jnp.zeros_like(sums_ff)

    sums[...] += fresh
    sums_ff[...] += jnp.concatenate(ff, axis=0)


def last_kernel(slot, x, d_r1, d_proj, hin, w_qkv, vec, d_x_out, sums, rows_out, total):
    rows, width = x.shape
    step = pl.program_id(0)
    d_h0 = d_r1[...]
    for i in range(3):
        d_h0 = d_h0 + dot_nt(d_proj[i], w_qkv[:, i * width : (i + 1) * width])
    unit, scale = normal(x[...])
    d_ge = jnp.sum(d_h0 * unit, axis=0, keepdims=True)
    d_be = jnp.sum(d_h0, axis=0, keepdims=True)
    d_x = normal_back(d_h0 * vec[0:1], unit, scale)
    d_xb = d_x.astype(bf)
    d_x_out[...] = d_xb
    bias_q, bias_v = column_sums(d_proj[0]), column_sums(d_proj[2])
    fresh = jnp.concatenate([d_ge, d_be, bias_q, bias_v, d_ge, d_be, bias_q, bias_v], axis=0)
    hit = jnp.where(slot[...] == iota((rows_out.shape[0], rows), 0), 1.0, 0.0).astype(bf)

    @pl.when(step == 0)
    def _():
        sums[...] = jnp.zeros_like(sums)
        total[...] = jnp.zeros_like(total)

    sums[...] += fresh
    total[...] += dot(hit, d_xb)

    @pl.when(step == pl.num_programs(0) - 1)
    def _():
        rows_out[...] = total[...].astype(bf)


def blocks(v, depth):
    return v.reshape(v.shape[0] // depth, depth, v.shape[1])


def dense_grads_kernel(depth, turns, act, d_y, h1, d_f, mixed, d_a, out):
    width = d_y.shape[1]
    g = dot_tn(act[...], d_y[...])
    g = g.reshape(out.shape[0], turns, depth, width)
    for j in range(turns):
        out[:, j] = g[:, j].astype(bf)
    for j in range(turns):
        out[:, turns + j] = blocks(dot_tn(h1[...], d_f[:, j * width : (j + 1) * width]), depth).astype(bf)
    out[:, 2 * turns] = blocks(dot_tn(mixed[...], d_a[...]), depth).astype(bf)


def rest_grads_kernel(depth, length, core, hin, d_proj, d_x, sums_0, sums, sums_ff, keep, send):
    rows, width = d_proj.shape[1], d_proj.shape[2]
    part = hin.shape[1]
    mine = core[0]

    def put(kind, g):
        g = g.reshape(part // (2 * depth), 2, depth, width)
        even, odd = g[:, 0], g[:, 1]
        keep[:, kind] = jnp.where(mine == 0, even, odd).astype(bf)
        send[:, kind] = jnp.where(mine == 0, odd, even).astype(bf)

    for i in range(3):
        put(i, dot_tn(hin[...], d_proj[i]))
    g_pos = None
    for i in range(rows // length):
        line = jnp.where(iota((length, length), 0) == iota((length, length), 1), 1.0, 0.0).astype(bf)
        g = dot_tn(d_x[i * length : (i + 1) * length], line)
        g_pos = g if g_pos is None else g_pos + g
    turns = sums_ff.shape[0]
    vec = jnp.concatenate([sums_0[:4], sums[:3], sums_ff[...], sums[3:6]], axis=0)
    vec = jnp.concatenate([vec, jnp.zeros((128 - vec.shape[0], part), f32)], axis=0)
    put(3, jnp.concatenate([g_pos, vec.T, jnp.zeros((part, width - length - 128), f32)], axis=1))


def cost(flops, nbytes):
    return pl.CostEstimate(flops=int(flops), bytes_accessed=int(nbytes), transcendentals=0)


def run_forward_backward(full, back, extra, slots, lens, facts, core, devices, depth, length, hidden):
    width = back.shape[1]
    rows = slots.shape[0]
    sents = rows // length
    steps = rows // ROWS
    per_sent = length // ROWS
    turns = hidden // width
    pairs = width // GROUP
    shape = jax.ShapeDtypeStruct
    row = lambda cols, kind=None: pl.BlockSpec((ROWS, cols), lambda i, *_: (i, 0))
    column = lambda block: fixed((width, width), (0, block))
    at_back = 4 * width + hidden

    if depth % 8 == 0:
        w_back = pl.pallas_call(
            functools.partial(spread_kernel, depth, turns, width),
            grid=(devices // 2,),
            in_specs=[pl.BlockSpec((2 * depth, turns * width), lambda i: (i, at_back // (turns * width)))],
            out_specs=pl.BlockSpec((2 * depth * turns, width), lambda i: (i, 0)),
            out_shape=shape((hidden, width), bf),
            name="spread",
        )(full)
    else:
        w_back = full[:, at_back : at_back + turns * width].reshape(devices, depth, turns, width)
        w_back = w_back.transpose(0, 2, 1, 3).reshape(hidden, width)

    at_pos = at_back + turns * width
    at_vec = at_pos + length
    w_qkv_spec = fixed((width, 3 * width), (0, 0))
    w_out_spec = column(3)
    w_in_spec = fixed((width, hidden), (0, 4 * width // hidden))
    vec_spec = fixed((16, width), (0, 0))

    x, hin, qkv, vec = pl.pallas_call(
        first_kernel,
        grid=(steps,),
        in_specs=[
            pl.BlockSpec((ROWS, 1), lambda i: (i, 0)),
            fixed(back.shape, (0, 0)),
            row(width),
            w_qkv_spec,
            fixed((width, length), (0, at_pos // length)),
            fixed((width, 128), (0, at_vec // 128)),
        ],
        out_specs=[row(width), row(width), row(3 * width), pl.BlockSpec((16, width), lambda i: (0, 0))],
        out_shape=[shape((rows, width), f32), shape((rows, width), bf), shape((rows, 3 * width), bf), shape((16, width), f32)],
        compiler_params=params(56),
        name="first",
    )(slots[:, None], back, extra, full, full, full)

    block = lambda part: pl.BlockSpec((length, GROUP), lambda s, p, *_: (s, part * pairs + p))
    mixed = pl.pallas_call(
        attend_kernel,
        grid_spec=pltpu.PrefetchScalarGridSpec(
            num_scalar_prefetch=1,
            grid=(sents, pairs),
            in_specs=[block(0), block(1), block(2)],
            out_specs=block(0),
        ),
        out_shape=shape((rows, width), bf),
        compiler_params=params(56),
        name="attend",
    )(lens, qkv, qkv, qkv)

    vec_ff = vec[7 : 7 + turns].reshape(1, hidden)
    z1, h1, act, slope, z2, pooled = pl.pallas_call(
        functools.partial(middle_kernel, per_sent),
        grid_spec=pltpu.PrefetchScalarGridSpec(
            num_scalar_prefetch=1,
            grid=(steps,),
            in_specs=[
                row(width), row(width), w_out_spec, w_in_spec, fixed((hidden, width), (0, 0)), vec_spec, fixed((1, hidden), (0, 0)),
            ],
            out_specs=[row(width), row(width), row(hidden), row(hidden), row(width), pl.BlockSpec((8, width), lambda i, *_: (0, 0))],
        ),
        out_shape=[
            shape((rows, width), f32), shape((rows, width), bf), shape((rows, hidden), bf), shape((rows, hidden), bf),
            shape((rows, width), f32), shape((8, width), f32),
        ],
        compiler_params=params(60),
        name="middle",
    )(lens, x, mixed, full, full, w_back, vec, vec_ff)

    d_y, d_f, d_r1, d_a, d_o, sums, sums_ff, loss = pl.pallas_call(
        functools.partial(back_kernel, per_sent),
        grid_spec=pltpu.PrefetchScalarGridSpec(
            num_scalar_prefetch=2,
            grid=(steps,),
            in_specs=[
                fixed((8, width), (0, 0)), row(width), row(hidden), row(width), w_out_spec, w_in_spec, fixed((hidden, width), (0, 0)), vec_spec,
            ],
            out_specs=[
                row(width), row(hidden), row(width), row(width), row(width),
                pl.BlockSpec((8, width), lambda i, *_: (0, 0)),
                pl.BlockSpec((turns, width), lambda i, *_: (0, 0)),
                pl.BlockSpec((8, 128), lambda i, *_: (0, 0)),
            ],
        ),
        out_shape=[
            shape((rows, width), bf), shape((rows, hidden), bf), shape((rows, width), f32), shape((rows, width), bf), shape((rows, width), bf),
            shape((8, width), f32), shape((turns, width), f32), shape((8, 128), f32),
        ],
        compiler_params=params(60),
        name="back",
    )(lens, facts, pooled, z1, slope, z2, full, full, w_back, vec)

    tall = depth % 8 == 0
    half = devices // 2
    part = width // 2
    halves = lambda cols: pl.BlockSpec((rows, cols), lambda i, *_: (0, i))
    if tall:
        dense = pl.pallas_call(
            functools.partial(dense_grads_kernel, depth, turns),
            grid=(2,),
            in_specs=[
                halves(hidden // 2), fixed((rows, width), (0, 0)), halves(part), fixed((rows, hidden), (0, 0)), halves(part),
                fixed((rows, width), (0, 0)),
            ],
            out_specs=pl.BlockSpec((half, 2 * turns + 1, depth, width), lambda i: (i, 0, 0, 0)),
            out_shape=shape((devices, 2 * turns + 1, depth, width), bf),
            compiler_params=params(60),
            name="dense_grads",
        )(act, d_y, h1, d_f, mixed, d_a)
    else:
        cut = lambda g: g.astype(bf).reshape(devices, depth, -1, width).transpose(0, 2, 1, 3)
        g_out = dot_tn(act, d_y).astype(bf).reshape(devices, turns, depth, width)
        dense = jnp.concatenate([g_out, cut(dot_tn(h1, d_f)), cut(dot_tn(mixed, d_a))], axis=1)
    d_o, dense = lax.optimization_barrier((d_o, dense))

    d_proj = pl.pallas_call(
        attend_back_kernel,
        grid_spec=pltpu.PrefetchScalarGridSpec(
            num_scalar_prefetch=1,
            grid=(sents, pairs),
            in_specs=[block(0), block(1), block(2), block(0)],
            out_specs=pl.BlockSpec((3, length, GROUP), lambda s, p, *_: (0, s, p)),
        ),
        out_shape=shape((3, rows, width), bf),
        compiler_params=params(56),
        name="attend_back",
    )(lens, qkv, qkv, qkv, d_o)

    d_xb, sums_0, give_rows = pl.pallas_call(
        last_kernel,
        grid=(steps,),
        in_specs=[
            pl.BlockSpec((1, ROWS), lambda i: (0, i)), row(width), row(width),
            pl.BlockSpec((3, ROWS, width), lambda i: (0, i, 0)), row(width), w_qkv_spec, vec_spec,
        ],
        out_specs=[
            row(width), pl.BlockSpec((8, width), lambda i: (0, 0)),
            pl.BlockSpec(back.shape, lambda i: (0, 0)),
        ],
        out_shape=[shape((rows, width), bf), shape((8, width), f32), shape(back.shape, bf)],
        scratch_shapes=[pltpu.VMEM(back.shape, f32)],
        compiler_params=params(60),
        name="last",
    )(slots[None, :], x, d_r1, d_proj, hin, full, vec)

    if tall:
        quarter = pl.BlockSpec((half // 2, 4, depth, width), lambda i, *_: (i, 0, 0, 0))
        rest = pl.pallas_call(
            functools.partial(rest_grads_kernel, depth, length),
            grid_spec=pltpu.PrefetchScalarGridSpec(
                num_scalar_prefetch=1,
                grid=(2,),
                in_specs=[
                    halves(part), fixed((3, rows, width), (0, 0, 0)), halves(part),
                    pl.BlockSpec((8, part), lambda i, *_: (0, i)), pl.BlockSpec((8, part), lambda i, *_: (0, i)),
                    pl.BlockSpec((turns, part), lambda i, *_: (0, i)),
                ],
                out_specs=[quarter, quarter],
            ),
            out_shape=[shape((half, 4, depth, width), bf)] * 2,
            compiler_params=params(60),
            name="rest_grads",
        )(core, hin, d_proj, d_xb, sums_0, sums, sums_ff)
    else:
        g_vec = jnp.concatenate([sums_0[:4], sums[:3], sums_ff, sums[3:6]], axis=0)
        g_pos = jnp.sum(d_xb.astype(f32).reshape(sents, length, width), axis=0).T
        spare = jnp.zeros((width, width - length - g_vec.shape[0]), f32)
        rest = [dot_tn(hin, d_proj[i]) for i in range(3)] + [jnp.concatenate([g_pos, g_vec.T, spare], axis=1)]
        rest = jnp.stack([g.astype(bf).reshape(devices, depth, width) for g in rest], axis=1)
    return loss[0, 0], dense, rest, d_xb, give_rows


def swap(v, bit, devices):
    return lax.ppermute(v, AXES, [(i, i ^ bit) for i in range(devices)])


def add(a, b):
    return (a.astype(f32) + b.astype(f32)).astype(bf)


def gather_sums(keep, send):
    devices = 32
    x = lax.axis_index("seq") // 2
    y = lax.rem(lax.axis_index("dp"), 2)
    kinds = keep.shape[1]
    view = lambda v: v.reshape((4, 2, 2) + v.shape[1:])
    keep, send = view(keep), view(send)
    pick = lambda v, axis, index: lax.dynamic_index_in_dim(v, index, axis, keepdims=False)
    cut = kinds // 2
    one = add(keep[:, :, :, :cut], swap(send[:, :, :, :cut], 1, devices))
    two = add(keep[:, :, :, cut:], swap(send[:, :, :, cut:], 1, devices))
    one = add(pick(one, 2, x), swap(pick(one, 2, 1 - x), 2, devices))
    two = add(pick(two, 1, y), swap(pick(two, 1, 1 - y), 4, devices))
    one = add(pick(one, 1, y), swap(pick(one, 1, 1 - y), 4, devices))
    two = add(pick(two, 1, x), swap(pick(two, 1, 1 - x), 2, devices))
    both = jnp.concatenate([one, two], axis=1)
    groups = [[low + 8 * z for z in range(4)] for low in range(8)]
    both = lax.all_to_all(both, AXES, 0, 0, tiled=True, axis_index_groups=groups)
    return jnp.sum(both.astype(f32), axis=0)


def body(
    token_ids, lengths, labeled, gold,
    embed, position, attn_in, attn_out, ff_in, ff_out, vectors,
    mom_embed, mom_position, mom_attn_in, mom_attn_out, mom_ff_in, mom_ff_out, mom_vectors,
    avg_embed, avg_position, avg_attn_in, avg_attn_out, avg_ff_in, avg_ff_out, avg_vectors,
):
    pairs_here, _, local = token_ids.shape
    seq = lax.axis_size("seq")
    devices = lax.axis_size("dp") * seq
    length = local * seq
    per_owner, width = embed.shape
    depth = attn_in.shape[0]
    hidden = ff_in.shape[1]
    nvec = vectors.shape[0]
    turns = ff_out.shape[0] // depth
    mine = pairs_here // seq
    sents = 2 * mine
    rows = sents * length
    spare = 128 - nvec

    shard = jnp.concatenate(
        [attn_in, attn_out, ff_in]
        + [ff_out[i * depth : (i + 1) * depth] for i in range(turns)]
        + [position.T, vectors.T, jnp.zeros((depth, spare), f32)],
        axis=1,
    ).astype(bf)
    full = lax.all_gather(shard, AXES, axis=0, tiled=True)

    ids = lax.all_to_all(token_ids, "seq", 0, 2, tiled=True).reshape(rows)
    turn = lax.axis_index("seq") * mine
    lens = lax.dynamic_slice_in_dim(lengths, turn, mine, 0).reshape(sents)
    lab = lax.dynamic_slice_in_dim(labeled, turn, mine, 0)
    goal = lax.dynamic_slice_in_dim(gold, turn, mine, 0)
    lab_f = lab.astype(f32)
    used = (jnp.arange(length)[None, :] < lens[:, None]) & (jnp.repeat(lab, 2) > 0)[:, None]
    used = used.reshape(rows)
    owner, place, first, rank = route(ids, used, per_owner)
    most = jnp.max(jnp.where(used, rank + 1, 0))
    asked = requests(owner, place, first, rank, 0, devices).reshape(devices, SLOTS)
    note = jnp.stack([most, jnp.sum(lab)])[None, :]
    note = jnp.broadcast_to(note, (devices, 2))
    got = exchange(jnp.concatenate([asked, note, jnp.zeros((devices, 126 - SLOTS), jnp.int32)], axis=1))
    rounds = (jnp.max(got[:, SLOTS]) + SLOTS - 1) // SLOTS
    count = jnp.maximum(jnp.sum(got[:, SLOTS + 1]).astype(f32), 1.0)

    table = embed.astype(bf)
    slots = token_slots(owner, used, rank, 0)
    wanted_first = got[:, :SLOTS].reshape(-1)

    def pick(wanted):
        picked = mm(one_hot(wanted, per_owner), table).astype(bf).reshape(devices, SLOTS, width)
        return exchange(picked).reshape(devices * SLOTS, width)

    back = pick(wanted_first)

    def ask_again(start):
        return exchange(requests(owner, place, first, rank, start, devices).reshape(devices, SLOTS)).reshape(-1)

    def more(state):
        step, total = state
        start = step * SLOTS
        there = one_hot(token_slots(owner, used, rank, start), devices * SLOTS)
        return step + 1, total + mm(there, pick(ask_again(start))).astype(bf)

    _, extra = lax.while_loop(lambda state: state[0] < rounds, more, (jnp.int32(1), jnp.zeros((rows, width), bf)))
    facts = jnp.stack([lab_f[0], goal[0], count, count])
    core = lax.rem(lax.axis_index("seq"), 2)[None]
    loss, dense, rest, d_xb, give_rows = run_forward_backward(
        full, back, extra, slots, lens, facts, core, devices, depth, length, hidden
    )

    scatter = lambda g: lax.psum_scatter(g, AXES, scatter_dimension=0, tiled=True).astype(f32)[0]
    dense = scatter(dense)
    if not isinstance(rest, list | tuple):
        rest = scatter(rest)
    elif (seq, devices) == (4, 32):
        rest = gather_sums(*rest)
    else:
        keep, send = rest
        both = jnp.stack([jnp.where(core[0] == 0, keep, send), jnp.where(core[0] == 0, send, keep)], axis=1)
        rest = scatter(both.reshape((devices,) + keep.shape[1:]))
    beside = lambda v: jnp.concatenate(list(v), axis=1)
    g_ff_out = dense[:turns].reshape(turns * depth, width)
    g_ff_in = beside(dense[turns : 2 * turns])
    g_attn_out = dense[2 * turns]
    g_attn_in = beside(rest[:3])
    g_position = rest[3, :, :length].T
    g_vectors = rest[3, :, length : length + nvec].T

    def give(wanted, sums):
        there = exchange(sums.reshape(devices, SLOTS, width)).reshape(devices * SLOTS, width)
        return mm_left(one_hot(wanted, per_owner), there)

    def more_back(state):
        step, total = state
        start = step * SLOTS
        sums = mm_left(one_hot(token_slots(owner, used, rank, start), devices * SLOTS), d_xb).astype(bf)
        return step + 1, total + give(ask_again(start), sums)

    _, g_embed = lax.while_loop(lambda state: state[0] < rounds, more_back, (jnp.int32(1), give(wanted_first, give_rows)))

    grads = (g_embed, g_position, g_attn_in, g_attn_out, g_ff_in, g_ff_out, g_vectors)
    squares = sum(jnp.sum(g * g) for g in grads)
    sums = exchange(jnp.broadcast_to(jnp.stack([squares, loss])[None, :], (devices, 2)))
    sums = jnp.sum(sums, axis=0)
    norm = jnp.sqrt(sums[0])
    loss_sum = sums[1]
    scale = jnp.minimum(1.0, CLIP / (norm + 1e-06))
    weights = (embed, position, attn_in, attn_out, ff_in, ff_out, vectors)
    moms = (mom_embed, mom_position, mom_attn_in, mom_attn_out, mom_ff_in, mom_ff_out, mom_vectors)
    avgs = (avg_embed, avg_position, avg_attn_in, avg_attn_out, avg_ff_in, avg_ff_out, avg_vectors)
    news, next_moms, next_avgs = [], [], []
    for weight, grad, mom, avg in zip(weights, grads, moms, avgs):
        clipped = grad * scale
        moment = MOMENT * mom + clipped
        fresh = weight - RATE * (clipped + MOMENT * moment)
        news.append(fresh)
        next_moms.append(moment)
        next_avgs.append(DECAY * avg + (1.0 - DECAY) * fresh)
    return (loss_sum, count, norm, *news, *next_moms, *next_avgs)


def solution(mesh):
    whole = (
        P(AXES, None),
        P(None, AXES),
        P(AXES, None),
        P(AXES, None),
        P(AXES, None),
        P(AXES, None),
        P(None, AXES),
    )
    return jax.shard_map(
        body,
        mesh=mesh,
        in_specs=(P("dp", None, "seq"), P("dp", None), P("dp"), P("dp")) + whole * 3,
        out_specs=(P(), P(), P()) + whole * 3,
        check_vma=False,
    )
```

```python
import functools

import jax
import jax.numpy as jnp
from jax import lax
from jax.experimental import pallas as pl
from jax.experimental.pallas import tpu as pltpu
from jax.sharding import PartitionSpec as P

HEADS = 12
HEAD_DIM = 64
EPS = 1e-06
RATE = 10000.0
MOMENT = 0.5
DECAY = 0.5
CLIP = 0.01
SLOTS = 32
GROUP = 128
ROWS = 256
AXES = ("dp", "seq")
bf = jnp.bfloat16
f32 = jnp.float32


def mm(left, right):
    return jnp.dot(left, right, preferred_element_type=f32)


def mm_left(left, right):
    return lax.dot_general(left, right, (((0,), (0,)), ((), ())), preferred_element_type=f32)


def mm_right(left, right):
    return lax.dot_general(left, right, (((1,), (1,)), ((), ())), preferred_element_type=f32)


def exchange(v):
    return lax.all_to_all(v, AXES, 0, 0, tiled=True)


def route(ids, valid, per_owner):
    count = ids.shape[0]
    spot = jnp.arange(count, dtype=jnp.int32)
    owner = ids // per_owner
    local = ids - owner * per_owner
    key = jnp.where(valid, ids, -1 - spot)
    alike = key[:, None] == key[None, :]
    first_at = jnp.min(jnp.where(alike, spot[None, :], count), axis=1)
    first = (first_at == spot) & valid
    before = (owner[:, None] == owner[None, :]) & first[None, :] & (spot[None, :] < first_at[:, None])
    rank = jnp.sum(before.astype(jnp.int32), axis=1)
    return owner, local, first, rank


def requests(owner, local, first, rank, start, devices):
    slot = jnp.where(first & (rank >= start) & (rank < start + SLOTS), owner * SLOTS + rank - start, -1)
    line = jnp.arange(devices * SLOTS, dtype=jnp.int32)
    hit = slot[None, :] == line[:, None]
    return jnp.max(jnp.where(hit, local[None, :], -1), axis=1)


def token_slots(owner, valid, rank, start):
    return jnp.where(valid & (rank >= start) & (rank < start + SLOTS), owner * SLOTS + rank - start, -1)


def one_hot(index, size):
    return (index[:, None] == jnp.arange(size, dtype=jnp.int32)[None, :]).astype(bf)


NEAR = 0.3
TAIL = (
    0.11962924781130464, 0.12075473126046088, 0.09990870957740686, 0.12857719637511858,
    -0.05371263258867769, 0.2063844888355699, -0.15722075016774184, 0.03567893567949022,
)


def dot(left, right):
    return jnp.dot(left, right, preferred_element_type=f32)


def dot_nt(left, right):
    return lax.dot_general(left, right, (((1,), (1,)), ((), ())), preferred_element_type=f32)


def dot_tn(left, right):
    return lax.dot_general(left, right, (((0,), (0,)), ((), ())), preferred_element_type=f32)


def iota(shape, axis):
    return lax.broadcasted_iota(jnp.int32, shape, axis)


def normal(v):
    center = v - jnp.mean(v, axis=-1, keepdims=True)
    scale = lax.rsqrt(jnp.mean(center * center, axis=-1, keepdims=True) + EPS)
    return center * scale, scale


def normal_back(grad, unit, scale):
    inner = jnp.mean(grad * unit, axis=-1, keepdims=True)
    return scale * (grad - jnp.mean(grad, axis=-1, keepdims=True) - unit * inner)


def column_sums(v):
    return dot(jnp.full((8, v.shape[0]), 1.0, bf), v)[:1]


def gelu_pair(v):
    bell = jnp.exp(v * v * -0.5)
    t = 1.0 / (1.0 + NEAR * jnp.abs(v))
    poly = TAIL[-1]
    for c in TAIL[-2::-1]:
        poly = poly * t + c
    tail = poly * t * bell
    area = jnp.where(v < 0, tail, 1.0 - tail)
    return v * area, area + v * bell * 0.3989422804014327


def params(limit, **more):
    return pltpu.CompilerParams(vmem_limit_bytes=limit << 20, **more)


def fixed(shape, index):
    return pl.BlockSpec(shape, lambda *_: index, pipeline_mode=pl.Buffered(1))


def spread_kernel(depth, turns, width, src, out):
    tall = src[...].astype(f32)
    parts = []
    for e in range(2):
        for j in range(turns):
            parts.append(tall[e * depth : (e + 1) * depth, j * width : (j + 1) * width])
    out[...] = jnp.concatenate(parts, axis=0).astype(bf)


def first_kernel(slot, back, extra, w_qkv, pos_t, vec_t, x_out, hin_out, qkv_out, vec_out):
    rows, width = x_out.shape
    length = pos_t.shape[1]
    vec = dot_nt((iota((16, 128), 0) == iota((16, 128), 1)).astype(f32).astype(bf), vec_t[...])
    vec_out[...] = vec
    where = jnp.where(slot[...] == iota((rows, back.shape[0]), 1), 1.0, 0.0).astype(bf)
    begin = lax.rem(pl.program_id(0), length // rows) * rows
    line = jnp.where(iota((rows, length), 0) + begin == iota((rows, length), 1), 1.0, 0.0).astype(bf)
    x = dot(where, back[...]) + extra[...].astype(f32) + dot_nt(line, pos_t[...])
    x_out[...] = x
    unit, _ = normal(x)
    hin = (unit * vec[0:1] + vec[1:2]).astype(bf)
    hin_out[...] = hin
    qkv_out[:, :width] = (dot(hin, w_qkv[:, :width]) + vec[2:3]).astype(bf)
    qkv_out[:, width : 2 * width] = dot(hin, w_qkv[:, width : 2 * width]).astype(bf)
    qkv_out[:, 2 * width :] = (dot(hin, w_qkv[:, 2 * width :]) + vec[3:4]).astype(bf)


def head_parts(lens, query, keys, half):
    length = query.shape[0]
    lane = iota((length, GROUP), 1)
    inside = (lane // HEAD_DIM) == half
    spare = lane == (1 - half) * HEAD_DIM
    dead = iota((length, GROUP), 0) >= lens
    key = jnp.where(inside, keys.astype(f32), jnp.where(spare & dead, -1e30, 0.0)).astype(bf)
    ask = jnp.where(inside, query.astype(f32) * 0.125, jnp.where(spare, 1.0, 0.0)).astype(bf)
    return inside, ask, key


def attend_kernel(lens, query, keys, values, out):
    size = lens[pl.program_id(0)]
    total = None
    for half in range(2):
        inside, ask, key = head_parts(size, query[...], keys[...], half)
        score = dot_nt(ask, key)
        power = jnp.exp(score - jnp.max(score, axis=1, keepdims=True))
        prob = (power * (1.0 / jnp.sum(power, axis=1, keepdims=True))).astype(bf)
        part = dot(prob, jnp.where(inside, values[...].astype(f32), 0.0).astype(bf))
        total = part if total is None else total + part
    out[...] = total.astype(bf)


def attend_back_kernel(sent, lens, query, keys, values, d_out, *more):
    size = lens[sent]
    d_proj = more[-1]
    d_query, d_key, d_value = None, None, None
    add = lambda a, b: b if a is None else a + b
    for half in range(2):
        inside, ask, key = head_parts(size, query[...], keys[...], half)
        clean = lambda v: jnp.where(inside, v.astype(f32), 0.0).astype(bf)
        score = dot_nt(key, ask)
        power = jnp.exp(score - jnp.max(score, axis=0, keepdims=True))
        prob = power * (1.0 / jnp.sum(power, axis=0, keepdims=True))
        grad = clean(d_out[...])
        d_value = add(d_value, dot(prob.astype(bf), grad))
        d_prob = dot_nt(values[...], grad)
        inner = jnp.sum(prob * d_prob, axis=0, keepdims=True)
        d_score = (prob * (d_prob - inner)).astype(bf)
        d_key = add(d_key, dot(d_score, clean(ask)))
        d_query = add(d_query, dot_tn(d_score, clean(key)))
    d_proj[0] = (d_query * 0.125).astype(bf)
    d_proj[1] = d_key.astype(bf)
    d_proj[2] = d_value.astype(bf)


def middle_kernel(per_sent, lens, x, mixed, w_out, w_in, w_back, vec, vec_ff, z1_out, h1_out, act_out, slope_out, z2_out, pooled):
    rows, width = x.shape
    step = pl.program_id(0)
    unit, _ = normal(x[...])
    h0 = unit * vec[0:1] + vec[1:2]
    z1 = h0 + dot(mixed[...], w_out[...]) + vec[4:5]
    z1_out[...] = z1
    unit, _ = normal(z1)
    h1 = unit * vec[5:6] + vec[6:7]
    h1_b = h1.astype(bf)
    h1_out[...] = h1_b
    turns = w_in.shape[1] // width
    y = None
    for j in range(turns):
        at = slice(j * width, (j + 1) * width)
        hidden = dot(h1_b, w_in[:, at]) + vec_ff[:, at]
        act, slope = gelu_pair(hidden)
        act = act.astype(bf)
        act_out[:, at] = act
        slope_out[:, at] = slope.astype(bf)
        part = dot(act, w_back[at, :])
        y = part if y is None else y + part
    z2 = h1 + y + vec[7 + turns : 8 + turns]
    z2_out[...] = z2
    unit, _ = normal(z2)
    h2 = unit * vec[8 + turns : 9 + turns] + vec[9 + turns : 10 + turns]
    sent = step // per_sent
    begin = lax.rem(step, per_sent) * rows
    keep = iota((rows, width), 0) + begin < lens[sent]
    sums = jnp.sum(jnp.where(keep, h2, 0.0), axis=0, keepdims=True)

    @pl.when(step == 0)
    def _():
        pooled[...] = jnp.zeros_like(pooled)

    pooled[...] += jnp.where(iota(pooled.shape, 0) == sent, sums, 0.0)


def back_kernel(per_sent, lens, facts, pooled, z1, slope, z2, w_out, w_in, w_back, vec, d_y_out, d_f_out, d_r1_out, d_a_out, d_o_out, sums, sums_ff, loss):
    rows, width = z1.shape
    step = pl.program_id(0)
    sent = step // per_sent
    labeled, gold, count = facts[0], facts[1], facts[2]
    size = [lens[i].astype(f32) for i in range(2)]
    side = [pooled[i : i + 1] / size[i] for i in range(2)]
    total = lambda a, b: jnp.sum(a * b, axis=1, keepdims=True)
    cross = total(side[0], side[1])
    root = [lax.rsqrt(total(s, s) + EPS) for s in side]
    miss = cross * root[0] * root[1] - gold
    loss[...] = jnp.broadcast_to(labeled * miss * miss, loss.shape)
    push = 2.0 * labeled * miss / count
    grads = [
        push * (side[1 - i] * root[0] * root[1] - cross * root[i] * root[i] * root[i] * root[1 - i] * side[i]) / size[i]
        for i in range(2)
    ]
    d_pooled = jnp.where(sent == 0, grads[0], grads[1])
    begin = lax.rem(step, per_sent) * rows
    keep = iota((rows, width), 0) + begin < lens[sent]
    d_h2 = jnp.where(keep, d_pooled, 0.0)
    turns = w_in.shape[1] // width

    unit, scale = normal(z2[...])
    d_g2 = jnp.sum(d_h2 * unit, axis=0, keepdims=True)
    d_b2n = jnp.sum(d_h2, axis=0, keepdims=True)
    d_r2 = normal_back(d_h2 * vec[8 + turns : 9 + turns], unit, scale)
    d_y = d_r2.astype(bf)
    d_y_out[...] = d_y
    d_h1 = d_r2
    ff = []
    for j in range(turns):
        at = slice(j * width, (j + 1) * width)
        d_f = (dot_nt(d_y, w_back[at, :]) * slope[:, at].astype(f32)).astype(bf)
        d_f_out[:, at] = d_f
        ff.append(column_sums(d_f))
        d_h1 = d_h1 + dot_nt(d_f, w_in[:, at])
    unit, scale = normal(z1[...])
    d_g1 = jnp.sum(d_h1 * unit, axis=0, keepdims=True)
    d_b1 = jnp.sum(d_h1, axis=0, keepdims=True)
    d_r1 = normal_back(d_h1 * vec[5:6], unit, scale)
    d_r1_out[...] = d_r1
    d_a = d_r1.astype(bf)
    d_a_out[...] = d_a
    d_o_out[...] = dot_nt(d_a, w_out[...]).astype(bf)
    fresh = jnp.concatenate([column_sums(d_a), d_g1, d_b1, column_sums(d_y), d_g2, d_b2n, d_g2, d_b2n], axis=0)

    @pl.when(step == 0)
    def _():
        sums[...] = jnp.zeros_like(sums)
        sums_ff[...] = jnp.zeros_like(sums_ff)

    sums[...] += fresh
    sums_ff[...] += jnp.concatenate(ff, axis=0)


def last_kernel(slot, x, d_r1, d_proj, hin, w_qkv, vec, d_x_out, sums, rows_out, total):
    rows, width = x.shape
    step = pl.program_id(0)
    d_h0 = d_r1[...]
    for i in range(3):
        d_h0 = d_h0 + dot_nt(d_proj[i], w_qkv[:, i * width : (i + 1) * width])
    unit, scale = normal(x[...])
    d_ge = jnp.sum(d_h0 * unit, axis=0, keepdims=True)
    d_be = jnp.sum(d_h0, axis=0, keepdims=True)
    d_x = normal_back(d_h0 * vec[0:1], unit, scale)
    d_xb = d_x.astype(bf)
    d_x_out[...] = d_xb
    bias_q, bias_v = column_sums(d_proj[0]), column_sums(d_proj[2])
    fresh = jnp.concatenate([d_ge, d_be, bias_q, bias_v, d_ge, d_be, bias_q, bias_v], axis=0)
    hit = jnp.where(slot[...] == iota((rows_out.shape[0], rows), 0), 1.0, 0.0).astype(bf)

    @pl.when(step == 0)
    def _():
        sums[...] = jnp.zeros_like(sums)
        total[...] = jnp.zeros_like(total)

    sums[...] += fresh
    total[...] += dot(hit, d_xb)

    @pl.when(step == pl.num_programs(0) - 1)
    def _():
        rows_out[...] = total[...].astype(bf)


def blocks(v, depth):
    return v.reshape(v.shape[0] // depth, depth, v.shape[1])


def put_split(keep, send, kind, g, mine):
    g = g.reshape((g.shape[0] // 2, 2) + g.shape[1:])
    even, odd = g[:, 0], g[:, 1]
    keep[:, kind] = jnp.where(mine == 0, even, odd).astype(bf)
    send[:, kind] = jnp.where(mine == 0, odd, even).astype(bf)


def dense_grads_kernel(depth, turns, core, act, d_y, h1, d_f, mixed, d_a, keep, send):
    width = d_y.shape[1]
    mine = core[0]
    g = dot_tn(act[...], d_y[...])
    g = g.reshape(2 * keep.shape[0], turns, depth, width)
    for j in range(turns):
        put_split(keep, send, j, g[:, j], mine)
    for j in range(turns):
        put_split(keep, send, turns + j, blocks(dot_tn(h1[...], d_f[:, j * width : (j + 1) * width]), depth), mine)
    put_split(keep, send, 2 * turns, blocks(dot_tn(mixed[...], d_a[...]), depth), mine)


def rest_grads_kernel(depth, length, core, hin, d_proj, d_x, sums_0, sums, sums_ff, keep, send):
    rows, width = d_proj.shape[1], d_proj.shape[2]
    part = hin.shape[1]
    mine = core[0]

    def put(kind, g):
        put_split(keep, send, kind, blocks(g, depth), mine)

    for i in range(3):
        put(i, dot_tn(hin[...], d_proj[i]))
    g_pos = None
    for i in range(rows // length):
        line = jnp.where(iota((length, length), 0) == iota((length, length), 1), 1.0, 0.0).astype(bf)
        g = dot_tn(d_x[i * length : (i + 1) * length], line)
        g_pos = g if g_pos is None else g_pos + g
    turns = sums_ff.shape[0]
    vec = jnp.concatenate([sums_0[:4], sums[:3], sums_ff[...], sums[3:6]], axis=0)
    vec = jnp.concatenate([vec, jnp.zeros((128 - vec.shape[0], part), f32)], axis=0)
    put(3, jnp.concatenate([g_pos, vec.T, jnp.zeros((part, width - length - 128), f32)], axis=1))


def cost(flops, nbytes):
    return pl.CostEstimate(flops=int(flops), bytes_accessed=int(nbytes), transcendentals=0)


def run_forward_backward(full, back, extra, slots, lens, facts, core, staged, devices, depth, length, hidden):
    width = back.shape[1]
    rows = slots.shape[0]
    sents = rows // length
    steps = rows // ROWS
    per_sent = length // ROWS
    turns = hidden // width
    pairs = width // GROUP
    shape = jax.ShapeDtypeStruct
    row = lambda cols, kind=None: pl.BlockSpec((ROWS, cols), lambda i, *_: (i, 0))
    column = lambda block: fixed((width, width), (0, block))
    at_back = 4 * width + hidden

    if depth % 8 == 0:
        w_back = pl.pallas_call(
            functools.partial(spread_kernel, depth, turns, width),
            grid=(devices // 2,),
            in_specs=[pl.BlockSpec((2 * depth, turns * width), lambda i: (i, at_back // (turns * width)))],
            out_specs=pl.BlockSpec((2 * depth * turns, width), lambda i: (i, 0)),
            out_shape=shape((hidden, width), bf),
            name="spread",
        )(full)
    else:
        w_back = full[:, at_back : at_back + turns * width].reshape(devices, depth, turns, width)
        w_back = w_back.transpose(0, 2, 1, 3).reshape(hidden, width)

    at_pos = at_back + turns * width
    at_vec = at_pos + length
    w_qkv_spec = fixed((width, 3 * width), (0, 0))
    w_out_spec = column(3)
    w_in_spec = fixed((width, hidden), (0, 4 * width // hidden))
    vec_spec = fixed((16, width), (0, 0))

    x, hin, qkv, vec = pl.pallas_call(
        first_kernel,
        grid=(steps,),
        in_specs=[
            pl.BlockSpec((ROWS, 1), lambda i: (i, 0)),
            fixed(back.shape, (0, 0)),
            row(width),
            w_qkv_spec,
            fixed((width, length), (0, at_pos // length)),
            fixed((width, 128), (0, at_vec // 128)),
        ],
        out_specs=[row(width), row(width), row(3 * width), pl.BlockSpec((16, width), lambda i: (0, 0))],
        out_shape=[shape((rows, width), f32), shape((rows, width), bf), shape((rows, 3 * width), bf), shape((16, width), f32)],
        compiler_params=params(56),
        name="first",
    )(slots[:, None], back, extra, full, full, full)

    block = lambda part: pl.BlockSpec((length, GROUP), lambda s, p, *_: (s, part * pairs + p))
    mixed = pl.pallas_call(
        attend_kernel,
        grid_spec=pltpu.PrefetchScalarGridSpec(
            num_scalar_prefetch=1,
            grid=(sents, pairs),
            in_specs=[block(0), block(1), block(2)],
            out_specs=block(0),
        ),
        out_shape=shape((rows, width), bf),
        compiler_params=params(56),
        name="attend",
    )(lens, qkv, qkv, qkv)

    vec_ff = vec[7 : 7 + turns].reshape(1, hidden)
    z1, h1, act, slope, z2, pooled = pl.pallas_call(
        functools.partial(middle_kernel, per_sent),
        grid_spec=pltpu.PrefetchScalarGridSpec(
            num_scalar_prefetch=1,
            grid=(steps,),
            in_specs=[
                row(width), row(width), w_out_spec, w_in_spec, fixed((hidden, width), (0, 0)), vec_spec, fixed((1, hidden), (0, 0)),
            ],
            out_specs=[row(width), row(width), row(hidden), row(hidden), row(width), pl.BlockSpec((8, width), lambda i, *_: (0, 0))],
        ),
        out_shape=[
            shape((rows, width), f32), shape((rows, width), bf), shape((rows, hidden), bf), shape((rows, hidden), bf),
            shape((rows, width), f32), shape((8, width), f32),
        ],
        compiler_params=params(60),
        name="middle",
    )(lens, x, mixed, full, full, w_back, vec, vec_ff)

    d_y, d_f, d_r1, d_a, d_o, sums, sums_ff, loss = pl.pallas_call(
        functools.partial(back_kernel, per_sent),
        grid_spec=pltpu.PrefetchScalarGridSpec(
            num_scalar_prefetch=2,
            grid=(steps,),
            in_specs=[
                fixed((8, width), (0, 0)), row(width), row(hidden), row(width), w_out_spec, w_in_spec, fixed((hidden, width), (0, 0)), vec_spec,
            ],
            out_specs=[
                row(width), row(hidden), row(width), row(width), row(width),
                pl.BlockSpec((8, width), lambda i, *_: (0, 0)),
                pl.BlockSpec((turns, width), lambda i, *_: (0, 0)),
                pl.BlockSpec((8, 128), lambda i, *_: (0, 0)),
            ],
        ),
        out_shape=[
            shape((rows, width), bf), shape((rows, hidden), bf), shape((rows, width), f32), shape((rows, width), bf), shape((rows, width), bf),
            shape((8, width), f32), shape((turns, width), f32), shape((8, 128), f32),
        ],
        compiler_params=params(60),
        name="back",
    )(lens, facts, pooled, z1, slope, z2, full, full, w_back, vec)

    tall = depth % 8 == 0
    half = devices // 2
    part = width // 2
    halves = lambda cols: pl.BlockSpec((rows, cols), lambda i, *_: (0, i))
    if tall:
        quarter = pl.BlockSpec((half // 2, 2 * turns + 1, depth, width), lambda i, *_: (i, 0, 0, 0))
        dense = pl.pallas_call(
            functools.partial(dense_grads_kernel, depth, turns),
            grid_spec=pltpu.PrefetchScalarGridSpec(
                num_scalar_prefetch=1,
                grid=(2,),
                in_specs=[
                    halves(hidden // 2), fixed((rows, width), (0, 0)), halves(part), fixed((rows, hidden), (0, 0)), halves(part),
                    fixed((rows, width), (0, 0)),
                ],
                out_specs=[quarter, quarter],
            ),
            out_shape=[shape((half, 2 * turns + 1, depth, width), bf)] * 2,
            compiler_params=params(60),
            name="dense_grads",
        )(core, act, d_y, h1, d_f, mixed, d_a)
    else:
        cut = lambda g: g.astype(bf).reshape(devices, depth, -1, width).transpose(0, 2, 1, 3)
        g_out = dot_tn(act, d_y).astype(bf).reshape(devices, turns, depth, width)
        dense = jnp.concatenate([g_out, cut(dot_tn(h1, d_f)), cut(dot_tn(mixed, d_a))], axis=1)
    if staged:
        dense = over_cores(*dense)
    else:
        d_o, dense = lax.optimization_barrier((d_o, dense))

    def attend_back(sent, total):
        part = lambda kind: pl.BlockSpec((length, GROUP), lambda p, *_: (sent, kind * pairs + p))
        more = () if total is None else (total,)
        return pl.pallas_call(
            functools.partial(attend_back_kernel, sent),
            grid_spec=pltpu.PrefetchScalarGridSpec(
                num_scalar_prefetch=1,
                grid=(pairs,),
                in_specs=[part(0), part(1), part(2), part(0)] + [pl.BlockSpec(memory_space=pl.ANY)] * len(more),
                out_specs=pl.BlockSpec((3, length, GROUP), lambda p, *_: (0, sent, p)),
            ),
            out_shape=shape((3, rows, width), bf),
            input_output_aliases={5: 0} if more else {},
            compiler_params=params(56),
            cost_estimate=cost(10 * length * length * GROUP * pairs, 8 * length * width * 2),
            name="attend_back",
        )(lens, qkv, qkv, qkv, d_o, *more)

    d_proj = None
    for sent in range(sents):
        d_proj = attend_back(sent, d_proj)
        if staged and sent == 0:
            d_proj, dense = lax.optimization_barrier((d_proj, dense))
            dense = over_wide(*dense)

    d_xb, sums_0, give_rows = pl.pallas_call(
        last_kernel,
        grid=(steps,),
        in_specs=[
            pl.BlockSpec((1, ROWS), lambda i: (0, i)), row(width), row(width),
            pl.BlockSpec((3, ROWS, width), lambda i: (0, i, 0)), row(width), w_qkv_spec, vec_spec,
        ],
        out_specs=[
            row(width), pl.BlockSpec((8, width), lambda i: (0, 0)),
            pl.BlockSpec(back.shape, lambda i: (0, 0)),
        ],
        out_shape=[shape((rows, width), bf), shape((8, width), f32), shape(back.shape, bf)],
        scratch_shapes=[pltpu.VMEM(back.shape, f32)],
        compiler_params=params(60),
        name="last",
    )(slots[None, :], x, d_r1, d_proj, hin, full, vec)

    if staged:
        d_xb, dense = lax.optimization_barrier((d_xb, dense))
    if tall:
        quarter = pl.BlockSpec((half // 2, 4, depth, width), lambda i, *_: (i, 0, 0, 0))
        rest = pl.pallas_call(
            functools.partial(rest_grads_kernel, depth, length),
            grid_spec=pltpu.PrefetchScalarGridSpec(
                num_scalar_prefetch=1,
                grid=(2,),
                in_specs=[
                    halves(part), fixed((3, rows, width), (0, 0, 0)), halves(part),
                    pl.BlockSpec((8, part), lambda i, *_: (0, i)), pl.BlockSpec((8, part), lambda i, *_: (0, i)),
                    pl.BlockSpec((turns, part), lambda i, *_: (0, i)),
                ],
                out_specs=[quarter, quarter],
            ),
            out_shape=[shape((half, 4, depth, width), bf)] * 2,
            compiler_params=params(60),
            name="rest_grads",
        )(core, hin, d_proj, d_xb, sums_0, sums, sums_ff)
    else:
        g_vec = jnp.concatenate([sums_0[:4], sums[:3], sums_ff, sums[3:6]], axis=0)
        g_pos = jnp.sum(d_xb.astype(f32).reshape(sents, length, width), axis=0).T
        spare = jnp.zeros((width, width - length - g_vec.shape[0]), f32)
        rest = [dot_tn(hin, d_proj[i]) for i in range(3)] + [jnp.concatenate([g_pos, g_vec.T, spare], axis=1)]
        rest = jnp.stack([g.astype(bf).reshape(devices, depth, width) for g in rest], axis=1)
    return loss[0, 0], dense, rest, d_xb, give_rows


def swap(v, bit, devices):
    return lax.ppermute(v, AXES, [(i, i ^ bit) for i in range(devices)])


def add(a, b):
    return (a.astype(f32) + b.astype(f32)).astype(bf)


def spot(v, axis, index):
    return lax.dynamic_index_in_dim(v, index, axis, keepdims=False)


def place_in_slice():
    row = lax.axis_index("dp")
    return row // 2, lax.rem(row, 2), lax.axis_index("seq") // 2


def over_cores(keep, send):
    view = lambda v: v.reshape((4, 2, 2) + v.shape[1:])
    keep, send = view(keep), view(send)
    cut = keep.shape[3] // 2
    one = add(keep[:, :, :, :cut], swap(send[:, :, :, :cut], 1, 32))
    two = add(keep[:, :, :, cut:], swap(send[:, :, :, cut:], 1, 32))
    return one, two


def over_wide(one, two):
    _, y, x = place_in_slice()
    return add(spot(one, 2, x), swap(spot(one, 2, 1 - x), 2, 32)), add(spot(two, 1, y), swap(spot(two, 1, 1 - y), 4, 32))


def over_other(one, two):
    _, y, x = place_in_slice()
    return add(spot(one, 1, y), swap(spot(one, 1, 1 - y), 4, 32)), add(spot(two, 1, x), swap(spot(two, 1, 1 - x), 2, 32))


def over_long(one, two):
    z, _, _ = place_in_slice()
    both = jnp.concatenate([one, two], axis=1)
    total = spot(both, 0, z).astype(f32)
    for step in range(1, 4):
        total = total + swap(spot(both, 0, z ^ step), 8 * step, 32).astype(f32)
    return total


def body(
    token_ids, lengths, labeled, gold,
    embed, position, attn_in, attn_out, ff_in, ff_out, vectors,
    mom_embed, mom_position, mom_attn_in, mom_attn_out, mom_ff_in, mom_ff_out, mom_vectors,
    avg_embed, avg_position, avg_attn_in, avg_attn_out, avg_ff_in, avg_ff_out, avg_vectors,
):
    pairs_here, _, local = token_ids.shape
    seq = lax.axis_size("seq")
    devices = lax.axis_size("dp") * seq
    length = local * seq
    per_owner, width = embed.shape
    depth = attn_in.shape[0]
    hidden = ff_in.shape[1]
    nvec = vectors.shape[0]
    turns = ff_out.shape[0] // depth
    mine = pairs_here // seq
    sents = 2 * mine
    rows = sents * length
    spare = 128 - nvec

    shard = jnp.concatenate(
        [attn_in, attn_out, ff_in]
        + [ff_out[i * depth : (i + 1) * depth] for i in range(turns)]
        + [position.T, vectors.T, jnp.zeros((depth, spare), f32)],
        axis=1,
    ).astype(bf)
    full = lax.all_gather(shard, AXES, axis=0, tiled=True)

    ids = lax.all_to_all(token_ids, "seq", 0, 2, tiled=True).reshape(rows)
    turn = lax.axis_index("seq") * mine
    lens = lax.dynamic_slice_in_dim(lengths, turn, mine, 0).reshape(sents)
    lab = lax.dynamic_slice_in_dim(labeled, turn, mine, 0)
    goal = lax.dynamic_slice_in_dim(gold, turn, mine, 0)
    lab_f = lab.astype(f32)
    used = (jnp.arange(length)[None, :] < lens[:, None]) & (jnp.repeat(lab, 2) > 0)[:, None]
    used = used.reshape(rows)
    owner, place, first, rank = route(ids, used, per_owner)
    most = jnp.max(jnp.where(used, rank + 1, 0))
    asked = requests(owner, place, first, rank, 0, devices).reshape(devices, SLOTS)
    note = jnp.stack([most, jnp.sum(lab)])[None, :]
    note = jnp.broadcast_to(note, (devices, 2))
    got = exchange(jnp.concatenate([asked, note, jnp.zeros((devices, 126 - SLOTS), jnp.int32)], axis=1))
    rounds = (jnp.max(got[:, SLOTS]) + SLOTS - 1) // SLOTS
    count = jnp.maximum(jnp.sum(got[:, SLOTS + 1]).astype(f32), 1.0)

    table = embed.astype(bf)
    slots = token_slots(owner, used, rank, 0)
    wanted_first = got[:, :SLOTS].reshape(-1)

    def pick(wanted):
        picked = mm(one_hot(wanted, per_owner), table).astype(bf).reshape(devices, SLOTS, width)
        return exchange(picked).reshape(devices * SLOTS, width)

    back = pick(wanted_first)

    def ask_again(start):
        return exchange(requests(owner, place, first, rank, start, devices).reshape(devices, SLOTS)).reshape(-1)

    def more(state):
        step, total = state
        start = step * SLOTS
        there = one_hot(token_slots(owner, used, rank, start), devices * SLOTS)
        return step + 1, total + mm(there, pick(ask_again(start))).astype(bf)

    _, extra = lax.while_loop(lambda state: state[0] < rounds, more, (jnp.int32(1), jnp.zeros((rows, width), bf)))
    facts = jnp.stack([lab_f[0], goal[0], count, count])
    core = lax.rem(lax.axis_index("seq"), 2)[None]
    staged = (seq, devices) == (4, 32) and depth % 8 == 0
    loss, dense, rest, d_xb, give_rows = run_forward_backward(
        full, back, extra, slots, lens, facts, core, staged, devices, depth, length, hidden
    )

    def sum_up(parts):
        if isinstance(parts, list | tuple):
            keep, send = parts
            both = jnp.stack([jnp.where(core[0] == 0, keep, send), jnp.where(core[0] == 0, send, keep)], axis=1)
            parts = both.reshape((devices,) + keep.shape[1:])
        return lax.psum_scatter(parts, AXES, scatter_dimension=0, tiled=True).astype(f32)[0]

    give_rows = exchange(give_rows.reshape(devices, SLOTS, width))
    if staged:
        dense = over_long(*over_other(*dense))
        rest = over_other(*over_wide(*over_cores(*rest)))
        rest, give_rows = lax.optimization_barrier((rest, give_rows))
        rest = over_long(*rest)
    else:
        dense, rest = sum_up(dense), sum_up(rest)
    beside = lambda v: jnp.concatenate(list(v), axis=1)
    g_ff_out = dense[:turns].reshape(turns * depth, width)
    g_ff_in = beside(dense[turns : 2 * turns])
    g_attn_out = dense[2 * turns]
    g_attn_in = beside(rest[:3])
    g_position = rest[3, :, :length].T
    g_vectors = rest[3, :, length : length + nvec].T

    def give(wanted, there):
        return mm_left(one_hot(wanted, per_owner), there.reshape(devices * SLOTS, width))

    def more_back(state):
        step, total = state
        start = step * SLOTS
        sums = mm_left(one_hot(token_slots(owner, used, rank, start), devices * SLOTS), d_xb).astype(bf)
        return step + 1, total + give(ask_again(start), exchange(sums.reshape(devices, SLOTS, width)))

    _, g_embed = lax.while_loop(lambda state: state[0] < rounds, more_back, (jnp.int32(1), give(wanted_first, give_rows)))

    grads = (g_embed, g_position, g_attn_in, g_attn_out, g_ff_in, g_ff_out, g_vectors)
    squares = sum(jnp.sum(g * g) for g in grads)
    sums = exchange(jnp.broadcast_to(jnp.stack([squares, loss])[None, :], (devices, 2)))
    sums = jnp.sum(sums, axis=0)
    norm = jnp.sqrt(sums[0])
    loss_sum = sums[1]
    scale = jnp.minimum(1.0, CLIP / (norm + 1e-06))
    weights = (embed, position, attn_in, attn_out, ff_in, ff_out, vectors)
    moms = (mom_embed, mom_position, mom_attn_in, mom_attn_out, mom_ff_in, mom_ff_out, mom_vectors)
    avgs = (avg_embed, avg_position, avg_attn_in, avg_attn_out, avg_ff_in, avg_ff_out, avg_vectors)
    news, next_moms, next_avgs = [], [], []
    for weight, grad, mom, avg in zip(weights, grads, moms, avgs):
        clipped = grad * scale
        moment = MOMENT * mom + clipped
        fresh = weight - RATE * (clipped + MOMENT * moment)
        news.append(fresh)
        next_moms.append(moment)
        next_avgs.append(DECAY * avg + (1.0 - DECAY) * fresh)
    return (loss_sum, count, norm, *news, *next_moms, *next_avgs)


def solution(mesh):
    whole = (
        P(AXES, None),
        P(None, AXES),
        P(AXES, None),
        P(AXES, None),
        P(AXES, None),
        P(AXES, None),
        P(None, AXES),
    )
    return jax.shard_map(
        body,
        mesh=mesh,
        in_specs=(P("dp", None, "seq"), P("dp", None), P("dp"), P("dp")) + whole * 3,
        out_specs=(P(), P(), P()) + whole * 3,
        check_vma=False,
    )
```

```python
import functools

import jax
import jax.numpy as jnp
from jax import lax
from jax.experimental import pallas as pl
from jax.experimental.pallas import tpu as pltpu
from jax.sharding import PartitionSpec as P

HEADS = 12
HEAD_DIM = 64
EPS = 1e-06
RATE = 10000.0
MOMENT = 0.5
DECAY = 0.5
CLIP = 0.01
SLOTS = 1024
GROUP = 128
ROWS = 288
BLOCKS = 4
SIZES = (128, 256, 384, 512)
AXES = ("dp", "seq")
bf = jnp.bfloat16
f32 = jnp.float32


def mm(left, right):
    return jnp.dot(left, right, preferred_element_type=f32)


def mm_left(left, right):
    return lax.dot_general(left, right, (((0,), (0,)), ((), ())), preferred_element_type=f32)


def mm_right(left, right):
    return lax.dot_general(left, right, (((1,), (1,)), ((), ())), preferred_element_type=f32)


def exchange(v):
    return lax.all_to_all(v, AXES, 0, 0, tiled=True)


def slots_of(devices):
    return max(16, SLOTS // devices)


def route(ids, valid, per_owner):
    count = ids.shape[0]
    spot = jnp.arange(count, dtype=jnp.int32)
    owner = ids // per_owner
    local = ids - owner * per_owner
    key = jnp.where(valid, ids, -1 - spot)
    alike = key[:, None] == key[None, :]
    first_at = jnp.min(jnp.where(alike, spot[None, :], count), axis=1)
    first = (first_at == spot) & valid
    before = (owner[:, None] == owner[None, :]) & first[None, :] & (spot[None, :] < first_at[:, None])
    rank = jnp.sum(before.astype(jnp.int32), axis=1)
    return owner, local, first, rank


def requests(owner, local, first, rank, start, devices):
    room = slots_of(devices)
    slot = jnp.where(first & (rank >= start) & (rank < start + room), owner * room + rank - start, -1)
    line = jnp.arange(devices * room, dtype=jnp.int32)
    hit = slot[None, :] == line[:, None]
    return jnp.max(jnp.where(hit, local[None, :], -1), axis=1)


def token_slots(owner, valid, rank, start, room):
    return jnp.where(valid & (rank >= start) & (rank < start + room), owner * room + rank - start, -1)


def one_hot(index, size):
    return (index[:, None] == jnp.arange(size, dtype=jnp.int32)[None, :]).astype(bf)


NEAR = 0.3
TAIL = (
    0.11962924781130464, 0.12075473126046088, 0.09990870957740686, 0.12857719637511858,
    -0.05371263258867769, 0.2063844888355699, -0.15722075016774184, 0.03567893567949022,
)


def dot(left, right):
    return jnp.dot(left, right, preferred_element_type=f32)


def dot_nt(left, right):
    return lax.dot_general(left, right, (((1,), (1,)), ((), ())), preferred_element_type=f32)


def dot_tn(left, right):
    return lax.dot_general(left, right, (((0,), (0,)), ((), ())), preferred_element_type=f32)


def iota(shape, axis):
    return lax.broadcasted_iota(jnp.int32, shape, axis)


def normal(v):
    center = v - jnp.mean(v, axis=-1, keepdims=True)
    scale = lax.rsqrt(jnp.mean(center * center, axis=-1, keepdims=True) + EPS)
    return center * scale, scale


def normal_back(grad, unit, scale):
    inner = jnp.mean(grad * unit, axis=-1, keepdims=True)
    return scale * (grad - jnp.mean(grad, axis=-1, keepdims=True) - unit * inner)


def column_sums(v):
    return dot(jnp.full((8, v.shape[0]), 1.0, bf), v)[:1]


def gelu_pair(v):
    bell = jnp.exp(v * v * -0.5)
    t = 1.0 / (1.0 + NEAR * jnp.abs(v))
    poly = TAIL[-1]
    for c in TAIL[-2::-1]:
        poly = poly * t + c
    tail = poly * t * bell
    area = jnp.where(v < 0, tail, 1.0 - tail)
    return v * area, area + v * bell * 0.3989422804014327


def params(limit, **more):
    return pltpu.CompilerParams(vmem_limit_bytes=limit << 20, **more)


def fixed(shape, index):
    return pl.BlockSpec(shape, lambda *_: index, pipeline_mode=pl.Buffered(1))


def spread_kernel(depth, turns, width, src, out):
    tall = src[...].astype(f32)
    parts = []
    for e in range(2):
        for j in range(turns):
            parts.append(tall[e * depth : (e + 1) * depth, j * width : (j + 1) * width])
    out[...] = jnp.concatenate(parts, axis=0).astype(bf)


def live_rows(plan, shape):
    row = iota(shape, 0) + pl.program_id(0) * shape[0]
    return row < plan[0], (row >= plan[2]) & (row < plan[2] + plan[1])


def when_live(kernel):
    def run(*refs):
        pl.when(pl.program_id(0) < refs[0][3])(lambda: kernel(*refs))

    return run


def first_kernel(plan, slot, spot_in, back, extra, w_qkv, pos_t, vec_t, x_out, hin_out, qkv_out, vec_out):
    rows, width = x_out.shape
    length = pos_t.shape[1]
    vec = dot_nt((iota((16, 128), 0) == iota((16, 128), 1)).astype(f32).astype(bf), vec_t[...])
    vec_out[...] = vec
    where = jnp.where(slot[...] == iota((rows, back.shape[0]), 1), 1.0, 0.0).astype(bf)
    line = jnp.where(spot_in[...] == iota((rows, length), 1), 1.0, 0.0).astype(bf)
    x = dot(where, back[...]) + extra[...].astype(f32) + dot_nt(line, pos_t[...])
    x_out[...] = x
    unit, _ = normal(x)
    hin = (unit * vec[0:1] + vec[1:2]).astype(bf)
    hin_out[...] = hin
    qkv_out[:, :width] = (dot(hin, w_qkv[:, :width]) + vec[2:3]).astype(bf)
    qkv_out[:, width : 2 * width] = dot(hin, w_qkv[:, width : 2 * width]).astype(bf)
    qkv_out[:, 2 * width :] = (dot(hin, w_qkv[:, 2 * width :]) + vec[3:4]).astype(bf)


def head_parts(size, query, keys, half):
    shape = query.shape
    lane = iota(shape, 1)
    live = iota(shape, 0) < size
    inside = ((lane // HEAD_DIM) == half) & live
    spare = lane == (1 - half) * HEAD_DIM
    key = jnp.where(inside, keys.astype(f32), jnp.where(spare & ~live, -1e30, 0.0)).astype(bf)
    ask = jnp.where(inside, query.astype(f32) * 0.125, jnp.where(spare, 1.0, 0.0)).astype(bf)
    return inside, ask, key


def each_sentence(plan, run):
    def one(index, carry):
        size = jnp.where(index == 0, plan[0], plan[1])
        start = pl.multiple_of(jnp.where(index == 0, 0, plan[2]), 16)
        under = 0
        for count in SIZES:
            pl.when((size > under) & (size <= count))(functools.partial(run, pl.ds(start, count), size))
            under = count
        return carry

    lax.fori_loop(0, 2, one, 0)


def attend_kernel(plan, query, keys, values, out):
    out[...] = jnp.zeros_like(out)

    def run(rows, size):
        total = None
        for half in range(2):
            inside, ask, key = head_parts(size, query[rows, :], keys[rows, :], half)
            score = dot_nt(ask, key)
            power = jnp.exp(score - jnp.max(score, axis=1, keepdims=True))
            prob = (power * (1.0 / jnp.sum(power, axis=1, keepdims=True))).astype(bf)
            part = dot(prob, jnp.where(inside, values[rows, :].astype(f32), 0.0).astype(bf))
            total = part if total is None else total + part
        out[rows, :] = total.astype(bf)

    each_sentence(plan, run)


def attend_back_kernel(plan, query, keys, values, d_out, *more):
    d_proj = more[-1]
    d_proj[...] = jnp.zeros_like(d_proj)
    plus = lambda a, b: b if a is None else a + b

    def run(rows, size):
        d_query, d_key, d_value = None, None, None
        for half in range(2):
            inside, ask, key = head_parts(size, query[rows, :], keys[rows, :], half)
            clean = lambda v: jnp.where(inside, v.astype(f32), 0.0).astype(bf)
            score = dot_nt(key, ask)
            power = jnp.exp(score - jnp.max(score, axis=0, keepdims=True))
            prob = power * (1.0 / jnp.sum(power, axis=0, keepdims=True))
            grad = clean(d_out[rows, :])
            d_value = plus(d_value, dot(prob.astype(bf), grad))
            d_prob = dot_nt(clean(values[rows, :]), grad)
            inner = jnp.sum(prob * d_prob, axis=0, keepdims=True)
            d_score = (prob * (d_prob - inner)).astype(bf)
            d_key = plus(d_key, dot(d_score, clean(ask)))
            d_query = plus(d_query, dot_tn(d_score, clean(key)))
        d_proj[0, rows, :] = (d_query * 0.125).astype(bf)
        d_proj[1, rows, :] = d_key.astype(bf)
        d_proj[2, rows, :] = d_value.astype(bf)

    each_sentence(plan, run)


def middle_kernel(plan, x, mixed, w_out, w_in, w_back, vec, vec_ff, z1_out, h1_out, act_out, slope_out, z2_out, pooled):
    rows, width = x.shape
    unit, _ = normal(x[...])
    h0 = unit * vec[0:1] + vec[1:2]
    z1 = h0 + dot(mixed[...], w_out[...]) + vec[4:5]
    z1_out[...] = z1
    unit, _ = normal(z1)
    h1 = unit * vec[5:6] + vec[6:7]
    h1_b = h1.astype(bf)
    h1_out[...] = h1_b
    turns = w_in.shape[1] // width
    y = None
    for j in range(turns):
        at = slice(j * width, (j + 1) * width)
        hidden = dot(h1_b, w_in[:, at]) + vec_ff[:, at]
        act, slope = gelu_pair(hidden)
        act = act.astype(bf)
        act_out[:, at] = act
        slope_out[:, at] = slope.astype(bf)
        part = dot(act, w_back[at, :])
        y = part if y is None else y + part
    z2 = h1 + y + vec[7 + turns : 8 + turns]
    z2_out[...] = z2
    unit, _ = normal(z2)
    h2 = unit * vec[8 + turns : 9 + turns] + vec[9 + turns : 10 + turns]
    sums = [jnp.sum(jnp.where(keep, h2, 0.0), axis=0, keepdims=True) for keep in live_rows(plan, (rows, width))]

    @pl.when(pl.program_id(0) == 0)
    def _():
        pooled[...] = jnp.zeros_like(pooled)

    line = iota(pooled.shape, 0)
    pooled[...] += jnp.where(line == 0, sums[0], jnp.where(line == 1, sums[1], 0.0))


def back_kernel(plan, facts, pooled, partner, z1, slope, z2, w_out, w_in, w_back, vec, d_y_out, d_f_out, d_r1_out, d_a_out, d_o_out, sums, sums_ff, loss):
    rows, width = z1.shape
    step = pl.program_id(0)
    total = lambda a, b: jnp.sum(a * b, axis=1, keepdims=True)
    count = facts[10]
    grads, losses = [], []
    for i in range(2):
        labeled, gold, size, other_size, counts = (facts[5 * i + j] for j in range(5))
        own, other = pooled[i : i + 1] / size, partner[i : i + 1] / other_size
        cross = total(own, other)
        root, other_root = lax.rsqrt(total(own, own) + EPS), lax.rsqrt(total(other, other) + EPS)
        miss = cross * root * other_root - gold
        losses.append(counts * miss * miss)
        push = 2.0 * labeled * miss / count
        grads.append(push * (other * root * other_root - cross * root * root * root * other_root * own) / size)
    loss[...] = jnp.broadcast_to(losses[0] + losses[1], loss.shape)
    keep = live_rows(plan, (rows, width))
    d_h2 = jnp.where(keep[0], grads[0], jnp.where(keep[1], grads[1], 0.0))
    turns = w_in.shape[1] // width

    unit, scale = normal(z2[...])
    d_g2 = jnp.sum(d_h2 * unit, axis=0, keepdims=True)
    d_b2n = jnp.sum(d_h2, axis=0, keepdims=True)
    d_r2 = normal_back(d_h2 * vec[8 + turns : 9 + turns], unit, scale)
    d_y = d_r2.astype(bf)
    d_y_out[...] = d_y
    d_h1 = d_r2
    ff = []
    for j in range(turns):
        at = slice(j * width, (j + 1) * width)
        d_f = (dot_nt(d_y, w_back[at, :]) * slope[:, at].astype(f32)).astype(bf)
        d_f_out[:, at] = d_f
        ff.append(column_sums(d_f))
        d_h1 = d_h1 + dot_nt(d_f, w_in[:, at])
    unit, scale = normal(z1[...])
    d_g1 = jnp.sum(d_h1 * unit, axis=0, keepdims=True)
    d_b1 = jnp.sum(d_h1, axis=0, keepdims=True)
    d_r1 = normal_back(d_h1 * vec[5:6], unit, scale)
    d_r1_out[...] = d_r1
    d_a = d_r1.astype(bf)
    d_a_out[...] = d_a
    d_o_out[...] = dot_nt(d_a, w_out[...]).astype(bf)
    fresh = jnp.concatenate([column_sums(d_a), d_g1, d_b1, column_sums(d_y), d_g2, d_b2n, d_g2, d_b2n], axis=0)

    @pl.when(step == 0)
    def _():
        sums[...] = jnp.zeros_like(sums)
        sums_ff[...] = jnp.zeros_like(sums_ff)

    sums[...] += fresh
    sums_ff[...] += jnp.concatenate(ff, axis=0)


def last_kernel(plan, slot, x, d_r1, d_proj, w_qkv, vec, d_x_out, sums, rows_out, total):
    rows, width = x.shape
    step = pl.program_id(0)
    d_h0 = d_r1[...]
    for i in range(3):
        d_h0 = d_h0 + dot_nt(d_proj[i], w_qkv[:, i * width : (i + 1) * width])
    unit, scale = normal(x[...])
    d_ge = jnp.sum(d_h0 * unit, axis=0, keepdims=True)
    d_be = jnp.sum(d_h0, axis=0, keepdims=True)
    d_x = normal_back(d_h0 * vec[0:1], unit, scale)
    d_xb = d_x.astype(bf)
    d_x_out[...] = d_xb
    bias_q, bias_v = column_sums(d_proj[0]), column_sums(d_proj[2])
    fresh = jnp.concatenate([d_ge, d_be, bias_q, bias_v, d_ge, d_be, bias_q, bias_v], axis=0)
    hit = jnp.where(slot[...] == iota((rows, rows_out.shape[0]), 1), 1.0, 0.0).astype(bf)

    @pl.when(step == 0)
    def _():
        sums[...] = jnp.zeros_like(sums)
        total[...] = jnp.zeros_like(total)

    sums[...] += fresh
    total[...] += dot_tn(hit, d_xb)

    @pl.when(step == plan[3] - 1)
    def _():
        rows_out[...] = total[...].astype(bf)


def blocks(v, depth):
    return v.reshape(v.shape[0] // depth, depth, v.shape[1])


def put_split(keep, send, kind, g, mine):
    g = g.reshape((g.shape[0] // 2, 2) + g.shape[1:])
    even, odd = g[:, 0], g[:, 1]
    keep[:, kind] = jnp.where(mine == 0, even, odd).astype(bf)
    send[:, kind] = jnp.where(mine == 0, odd, even).astype(bf)


def by_blocks(plan, run):
    for count in range(2, BLOCKS + 1):
        pl.when(plan[3] == count)(functools.partial(run, count * ROWS))


def dense_grads_kernel(depth, turns, plan, act, d_y, h1, d_f, mixed, d_a, keep, send):
    width = d_y.shape[1]
    mine = plan[4]

    def run(rows):
        g = dot_tn(act[:rows], d_y[:rows])
        g = g.reshape(2 * keep.shape[0], turns, depth, width)
        for j in range(turns):
            put_split(keep, send, j, g[:, j], mine)
        for j in range(turns):
            put_split(keep, send, turns + j, blocks(dot_tn(h1[:rows], d_f[:rows, j * width : (j + 1) * width]), depth), mine)
        put_split(keep, send, 2 * turns, blocks(dot_tn(mixed[:rows], d_a[:rows]), depth), mine)

    by_blocks(plan, run)


def rest_grads_kernel(depth, length, plan, spot_in, hin, d_proj, d_x, sums_0, sums, sums_ff, keep, send):
    width = d_proj.shape[2]
    part = hin.shape[1]
    mine = plan[4]

    def run(rows):
        for i in range(3):
            put_split(keep, send, i, blocks(dot_tn(hin[:rows], d_proj[i, :rows]), depth), mine)
        line = jnp.where(spot_in[:rows] == iota((rows, length), 1), 1.0, 0.0).astype(bf)
        g_pos = dot_tn(d_x[:rows], line)
        vec = jnp.concatenate([sums_0[:4], sums[:3], sums_ff[...], sums[3:6]], axis=0)
        vec = jnp.concatenate([vec, jnp.zeros((128 - vec.shape[0], part), f32)], axis=0)
        put_split(keep, send, 3, blocks(jnp.concatenate([g_pos, vec.T, jnp.zeros((part, width - length - 128), f32)], axis=1), depth), mine)

    by_blocks(plan, run)


def cost(flops, nbytes):
    return pl.CostEstimate(flops=int(flops), bytes_accessed=int(nbytes), transcendentals=0)


def run_forward_backward(full, back, extra, slots, spots, plan, meet, staged, devices, depth, length, hidden):
    width = back.shape[1]
    rows = slots.shape[0]
    turns = hidden // width
    pairs = width // GROUP
    shape = jax.ShapeDtypeStruct
    at_row = lambda i, plan: jnp.minimum(i, plan[3] - 1)
    row = lambda cols: pl.BlockSpec((ROWS, cols), lambda i, plan, *_: (at_row(i, plan), 0))
    column = lambda block: fixed((width, width), (0, block))
    at_back = 4 * width + hidden
    whole_out = lambda *dims: pl.BlockSpec(dims, lambda *_: (0,) * len(dims))

    def call(kernel, prefetch, grid, in_specs, out_specs, out_shape, name, scratch=(), **more):
        return pl.pallas_call(
            kernel,
            grid_spec=pltpu.PrefetchScalarGridSpec(
                num_scalar_prefetch=prefetch, grid=grid, in_specs=in_specs, out_specs=out_specs, scratch_shapes=list(scratch)
            ),
            out_shape=out_shape,
            compiler_params=params(60),
            name=name,
            **more,
        )

    if depth % 8 == 0:
        w_back = pl.pallas_call(
            functools.partial(spread_kernel, depth, turns, width),
            grid=(devices // 2,),
            in_specs=[pl.BlockSpec((2 * depth, turns * width), lambda i: (i, at_back // (turns * width)))],
            out_specs=pl.BlockSpec((2 * depth * turns, width), lambda i: (i, 0)),
            out_shape=shape((hidden, width), bf),
            name="spread",
        )(full)
    else:
        w_back = full[:, at_back : at_back + turns * width].reshape(devices, depth, turns, width)
        w_back = w_back.transpose(0, 2, 1, 3).reshape(hidden, width)

    at_pos = at_back + turns * width
    at_vec = at_pos + length
    w_qkv_spec = fixed((width, 3 * width), (0, 0))
    w_out_spec = column(3)
    w_in_spec = fixed((width, hidden), (0, 4 * width // hidden))
    w_back_spec = fixed((hidden, width), (0, 0))
    vec_spec = fixed((16, width), (0, 0))

    x, hin, qkv, vec = call(
        when_live(first_kernel), 1, (BLOCKS,),
        [
            row(1), row(1), fixed(back.shape, (0, 0)), row(width), w_qkv_spec,
            fixed((width, length), (0, at_pos // length)), fixed((width, 128), (0, at_vec // 128)),
        ],
        [row(width), row(width), row(3 * width), whole_out(16, width)],
        [shape((rows, width), f32), shape((rows, width), bf), shape((rows, 3 * width), bf), shape((16, width), f32)],
        "first",
    )(plan, slots[:, None], spots[:, None], back, extra, full, full, full)

    block = lambda part, start=0: pl.BlockSpec((rows, GROUP), lambda p, *_: (0, part * pairs + start + p))
    mixed = call(
        attend_kernel, 1, (pairs,), [block(0), block(1), block(2)], block(0), shape((rows, width), bf), "attend"
    )(plan, qkv, qkv, qkv)

    vec_ff = vec[7 : 7 + turns].reshape(1, hidden)
    z1, h1, act, slope, z2, pooled = call(
        when_live(middle_kernel), 1, (BLOCKS,),
        [row(width), row(width), w_out_spec, w_in_spec, w_back_spec, vec_spec, fixed((1, hidden), (0, 0))],
        [row(width), row(width), row(hidden), row(hidden), row(width), whole_out(8, width)],
        [
            shape((rows, width), f32), shape((rows, width), bf), shape((rows, hidden), bf), shape((rows, hidden), bf),
            shape((rows, width), f32), shape((8, width), f32),
        ],
        "middle",
    )(plan, x, mixed, full, full, w_back, vec, vec_ff)

    partner, facts = meet(pooled)
    d_y, d_f, d_r1, d_a, d_o, sums, sums_ff, loss = call(
        when_live(back_kernel), 2, (BLOCKS,),
        [
            fixed((8, width), (0, 0)), fixed((2, width), (0, 0)), row(width), row(hidden), row(width), w_out_spec, w_in_spec,
            w_back_spec, vec_spec,
        ],
        [
            row(width), row(hidden), row(width), row(width), row(width), whole_out(8, width), whole_out(turns, width),
            whole_out(8, 128),
        ],
        [
            shape((rows, width), bf), shape((rows, hidden), bf), shape((rows, width), f32), shape((rows, width), bf), shape((rows, width), bf),
            shape((8, width), f32), shape((turns, width), f32), shape((8, 128), f32),
        ],
        "back",
    )(plan, facts, pooled, partner, z1, slope, z2, full, full, w_back, vec)

    tall = depth % 8 == 0
    half = devices // 2
    part = width // 2
    halves = lambda cols: pl.BlockSpec((rows, cols), lambda i, *_: (0, i))
    live = (jnp.arange(rows) < plan[3] * ROWS)[:, None]
    clean = lambda v: jnp.where(live, v, 0)
    if tall:
        quarter = pl.BlockSpec((half // 2, 2 * turns + 1, depth, width), lambda i, *_: (i, 0, 0, 0))
        dense = call(
            functools.partial(dense_grads_kernel, depth, turns), 1, (2,),
            [
                halves(hidden // 2), fixed((rows, width), (0, 0)), halves(part), fixed((rows, hidden), (0, 0)), halves(part),
                fixed((rows, width), (0, 0)),
            ],
            [quarter, quarter],
            [shape((half, 2 * turns + 1, depth, width), bf)] * 2,
            "dense_grads",
        )(plan, act, d_y, h1, d_f, mixed, d_a)
    else:
        cut = lambda g: g.astype(bf).reshape(devices, depth, -1, width).transpose(0, 2, 1, 3)
        g_out = dot_tn(clean(act), clean(d_y)).astype(bf).reshape(devices, turns, depth, width)
        g_in, g_mix = dot_tn(clean(h1), clean(d_f)), dot_tn(clean(mixed), clean(d_a))
        dense = jnp.concatenate([g_out, cut(g_in), cut(g_mix)], axis=1)
    if staged:
        dense = over_cores(*dense)
    else:
        d_o, dense = lax.optimization_barrier((d_o, dense))

    def attend_back(start, count, total):
        more = () if total is None else (total,)
        return call(
            attend_back_kernel, 1, (count,),
            [block(0, start), block(1, start), block(2, start), block(0, start)] + [pl.BlockSpec(memory_space=pl.ANY)] * len(more),
            pl.BlockSpec((3, rows, GROUP), lambda p, *_: (0, 0, start + p)),
            shape((3, rows, width), bf),
            "attend_back",
            input_output_aliases={5: 0} if more else {},
            cost_estimate=cost(10 * length * length * GROUP * count, 8 * rows * GROUP * count * 2),
        )(plan, qkv, qkv, qkv, d_o, *more)

    d_proj = attend_back(0, pairs // 2, None)
    if staged:
        d_proj, dense = lax.optimization_barrier((d_proj, dense))
        dense = over_wide(*dense)
    d_proj = attend_back(pairs // 2, pairs - pairs // 2, d_proj)

    d_xb, sums_0, give_rows = call(
        when_live(last_kernel), 1, (BLOCKS,),
        [
            row(1), row(width), row(width), pl.BlockSpec((3, ROWS, width), lambda i, plan: (0, at_row(i, plan), 0)), w_qkv_spec, vec_spec,
        ],
        [row(width), whole_out(8, width), whole_out(*back.shape)],
        [shape((rows, width), bf), shape((8, width), f32), shape(back.shape, bf)],
        "last",
        scratch=[pltpu.VMEM(back.shape, f32)],
    )(plan, slots[:, None], x, d_r1, d_proj, full, vec)

    if staged:
        d_xb, dense = lax.optimization_barrier((d_xb, dense))
    if tall:
        quarter = pl.BlockSpec((half // 2, 4, depth, width), lambda i, *_: (i, 0, 0, 0))
        cols = lambda count: pl.BlockSpec((count, part), lambda i, *_: (0, i))
        rest = call(
            functools.partial(rest_grads_kernel, depth, length), 1, (2,),
            [fixed((rows, 1), (0, 0)), halves(part), fixed((3, rows, width), (0, 0, 0)), halves(part), cols(8), cols(8), cols(turns)],
            [quarter, quarter],
            [shape((half, 4, depth, width), bf)] * 2,
            "rest_grads",
        )(plan, spots[:, None], hin, d_proj, d_xb, sums_0, sums, sums_ff)
    else:
        g_vec = jnp.concatenate([sums_0[:4], sums[:3], sums_ff, sums[3:6]], axis=0)
        g_pos = dot_tn(clean(d_xb), one_hot(spots, length))
        spare = jnp.zeros((width, width - length - g_vec.shape[0]), f32)
        rest = [dot_tn(clean(hin), clean(d_proj[i])) for i in range(3)] + [jnp.concatenate([g_pos, g_vec.T, spare], axis=1)]
        rest = jnp.stack([g.astype(bf).reshape(devices, depth, width) for g in rest], axis=1)
    return loss[0, 0], dense, rest, clean(d_xb), give_rows


def swap(v, bit, devices):
    return lax.ppermute(v, AXES, [(i, i ^ bit) for i in range(devices)])


def add(a, b):
    return (a.astype(f32) + b.astype(f32)).astype(bf)


def spot(v, axis, index):
    return lax.dynamic_index_in_dim(v, index, axis, keepdims=False)


def place_in_slice():
    row = lax.axis_index("dp")
    return row // 2, lax.rem(row, 2), lax.axis_index("seq") // 2


def over_cores(keep, send):
    view = lambda v: v.reshape((4, 2, 2) + v.shape[1:])
    keep, send = view(keep), view(send)
    cut = keep.shape[3] // 2
    one = add(keep[:, :, :, :cut], swap(send[:, :, :, :cut], 1, 32))
    two = add(keep[:, :, :, cut:], swap(send[:, :, :, cut:], 1, 32))
    return one, two


def over_wide(one, two):
    _, y, x = place_in_slice()
    return add(spot(one, 2, x), swap(spot(one, 2, 1 - x), 2, 32)), add(spot(two, 1, y), swap(spot(two, 1, 1 - y), 4, 32))


def over_other(one, two):
    _, y, x = place_in_slice()
    return add(spot(one, 1, y), swap(spot(one, 1, 1 - y), 4, 32)), add(spot(two, 1, x), swap(spot(two, 1, 1 - x), 2, 32))


def over_long(one, two):
    z, _, _ = place_in_slice()
    both = jnp.concatenate([one, two], axis=1)
    total = spot(both, 0, z).astype(f32)
    for step in range(1, 4):
        total = total + swap(spot(both, 0, z ^ step), 8 * step, 32).astype(f32)
    return total


def body(
    token_ids, lengths, labeled, gold,
    embed, position, attn_in, attn_out, ff_in, ff_out, vectors,
    mom_embed, mom_position, mom_attn_in, mom_attn_out, mom_ff_in, mom_ff_out, mom_vectors,
    avg_embed, avg_position, avg_attn_in, avg_attn_out, avg_ff_in, avg_ff_out, avg_vectors,
):
    pairs_here, _, local = token_ids.shape
    seq = lax.axis_size("seq")
    devices = lax.axis_size("dp") * seq
    length = local * seq
    per_owner, width = embed.shape
    depth = attn_in.shape[0]
    hidden = ff_in.shape[1]
    nvec = vectors.shape[0]
    turns = ff_out.shape[0] // depth
    rows = BLOCKS * ROWS
    room = slots_of(devices)
    spare = 128 - nvec

    shard = jnp.concatenate(
        [attn_in, attn_out, ff_in]
        + [ff_out[i * depth : (i + 1) * depth] for i in range(turns)]
        + [position.T, vectors.T, jnp.zeros((depth, spare), f32)],
        axis=1,
    ).astype(bf)
    full = lax.all_gather(shard, AXES, axis=0, tiled=True)

    group = 2 * pairs_here
    info = jnp.concatenate([lengths.reshape(1, group), labeled.reshape(1, pairs_here)], axis=1)
    info = jnp.pad(info, ((0, 0), (0, local - group - pairs_here)))
    news = jnp.concatenate([token_ids.reshape(group, local), info], axis=0)
    news = exchange(jnp.broadcast_to(news[None], (devices,) + news.shape)).reshape(devices // seq, seq, group + 1, local)
    lens = news[:, 0, group, :group].reshape(2 * devices)
    lab = news[:, 0, group, group : group + pairs_here].reshape(devices)
    live = jnp.where(jnp.repeat(lab, 2) > 0, lens, 0)
    index = jnp.arange(2 * devices, dtype=jnp.int32)
    ahead = (live[None, :] > live[:, None]) | ((live[None, :] == live[:, None]) & (index[None, :] < index[:, None]))
    order = jnp.sum(ahead.astype(jnp.int32), axis=1)
    me = lax.axis_index("dp") * seq + lax.axis_index("seq")
    take = lambda values, i: jnp.sum(jnp.where(index[: values.shape[0]] == i, values, 0))
    chosen = [jnp.sum(jnp.where(order == rank, index, 0)) for rank in (me, 2 * devices - 1 - me)]
    count = jnp.maximum(jnp.sum(lab).astype(f32), 1.0)
    size = [take(live, i) for i in chosen]
    start = (size[0] + 15) // 16 * 16
    two_ids = [
        lax.dynamic_slice(news, (i // group, 0, lax.rem(i, group), 0), (1, seq, 1, local)).reshape(length) for i in chosen
    ]
    ids = lax.dynamic_update_slice(jnp.pad(two_ids[0], (0, rows - length)), two_ids[1], (start,))
    line = jnp.arange(rows, dtype=jnp.int32)
    in_first, in_second = line < size[0], (line >= start) & (line < start + size[1])
    used = in_first | in_second
    spots = jnp.where(in_first, line, jnp.where(in_second, line - start, -1))
    total = jnp.where(size[1] > 0, start + size[1], size[0])
    core = lax.rem(lax.axis_index("seq"), 2)
    plan = jnp.stack([size[0], size[1], start, jnp.clip((total + ROWS - 1) // ROWS, 2, BLOCKS), core])
    owner, place, first, rank = route(ids, used, per_owner)
    most = jnp.max(jnp.where(used, rank + 1, 0))
    asked = requests(owner, place, first, rank, 0, devices).reshape(devices, room)
    note = jnp.broadcast_to(most, (devices, 1))
    got = exchange(jnp.concatenate([asked, note, jnp.zeros((devices, 127 - room), jnp.int32)], axis=1))
    rounds = (jnp.max(got[:, room]) + room - 1) // room

    table = embed.astype(bf)
    slots = token_slots(owner, used, rank, 0, room)
    wanted_first = got[:, :room].reshape(-1)

    def pick(wanted):
        picked = mm(one_hot(wanted, per_owner), table).astype(bf).reshape(devices, room, width)
        return exchange(picked).reshape(devices * room, width)

    back = pick(wanted_first)

    def ask_again(start):
        return exchange(requests(owner, place, first, rank, start, devices).reshape(devices, room)).reshape(-1)

    def more(state):
        step, total = state
        start = step * room
        there = one_hot(token_slots(owner, used, rank, start, room), devices * room)
        return step + 1, total + mm(there, pick(ask_again(start))).astype(bf)

    _, extra = lax.while_loop(lambda state: state[0] < rounds, more, (jnp.int32(1), jnp.zeros((rows, width), bf)))

    def meet(pooled):
        goal = jnp.pad(gold[None, :], ((0, 0), (0, width - pairs_here)))
        all_pooled = jnp.concatenate([pooled[:2], goal], axis=0)
        all_pooled = exchange(jnp.broadcast_to(all_pooled[None], (devices, 3, width)))
        vectors_of, facts = [], []
        for i in chosen:
            other = i ^ 1
            rank = take(order, other)
            holder = jnp.where(rank < devices, rank, 2 * devices - 1 - rank)
            vectors_of.append(lax.dynamic_slice(all_pooled, (holder, (rank >= devices).astype(jnp.int32), 0), (1, 1, width))[0])
            pair = i // 2
            goal = lax.dynamic_slice(all_pooled, (pair // pairs_here * seq, 2, lax.rem(pair, pairs_here)), (1, 1, 1))[0, 0, 0]
            weight = take(lab, pair).astype(f32)
            own = jnp.where(lax.rem(i, 2) == 0, weight, 0.0)
            facts += [weight, goal, take(lens, i).astype(f32), take(lens, other).astype(f32), own]
        return jnp.concatenate(vectors_of, axis=0), jnp.stack(facts + [count])

    staged = (seq, devices) == (4, 32) and depth % 8 == 0
    loss, dense, rest, d_xb, give_rows = run_forward_backward(
        full, back, extra, slots, spots, plan, meet, staged, devices, depth, length, hidden
    )

    def sum_up(parts):
        if isinstance(parts, list | tuple):
            keep, send = parts
            both = jnp.stack([jnp.where(core == 0, keep, send), jnp.where(core == 0, send, keep)], axis=1)
            parts = both.reshape((devices,) + keep.shape[1:])
        return lax.psum_scatter(parts, AXES, scatter_dimension=0, tiled=True).astype(f32)[0]

    give_rows = exchange(give_rows.reshape(devices, room, width))
    if staged:
        dense = over_long(*over_other(*dense))
        rest = over_other(*over_wide(*over_cores(*rest)))
        rest, give_rows = lax.optimization_barrier((rest, give_rows))
        rest = over_long(*rest)
    else:
        dense, rest = sum_up(dense), sum_up(rest)
    beside = lambda v: jnp.concatenate(list(v), axis=1)
    g_ff_out = dense[:turns].reshape(turns * depth, width)
    g_ff_in = beside(dense[turns : 2 * turns])
    g_attn_out = dense[2 * turns]
    g_attn_in = beside(rest[:3])
    g_position = rest[3, :, :length].T
    g_vectors = rest[3, :, length : length + nvec].T

    def give(wanted, there):
        return mm_left(one_hot(wanted, per_owner), there.reshape(devices * room, width))

    def more_back(state):
        step, total = state
        start = step * room
        sums = mm_left(one_hot(token_slots(owner, used, rank, start, room), devices * room), d_xb).astype(bf)
        return step + 1, total + give(ask_again(start), exchange(sums.reshape(devices, room, width)))

    _, g_embed = lax.while_loop(lambda state: state[0] < rounds, more_back, (jnp.int32(1), give(wanted_first, give_rows)))

    grads = (g_embed, g_position, g_attn_in, g_attn_out, g_ff_in, g_ff_out, g_vectors)
    squares = sum(jnp.sum(g * g) for g in grads)
    sums = exchange(jnp.broadcast_to(jnp.stack([squares, loss])[None, :], (devices, 2)))
    sums = jnp.sum(sums, axis=0)
    norm = jnp.sqrt(sums[0])
    loss_sum = sums[1]
    scale = jnp.minimum(1.0, CLIP / (norm + 1e-06))
    weights = (embed, position, attn_in, attn_out, ff_in, ff_out, vectors)
    moms = (mom_embed, mom_position, mom_attn_in, mom_attn_out, mom_ff_in, mom_ff_out, mom_vectors)
    avgs = (avg_embed, avg_position, avg_attn_in, avg_attn_out, avg_ff_in, avg_ff_out, avg_vectors)
    news, next_moms, next_avgs = [], [], []
    for weight, grad, mom, avg in zip(weights, grads, moms, avgs):
        clipped = grad * scale
        moment = MOMENT * mom + clipped
        fresh = weight - RATE * (clipped + MOMENT * moment)
        news.append(fresh)
        next_moms.append(moment)
        next_avgs.append(DECAY * avg + (1.0 - DECAY) * fresh)
    return (loss_sum, count, norm, *news, *next_moms, *next_avgs)


def solution(mesh):
    whole = (
        P(AXES, None),
        P(None, AXES),
        P(AXES, None),
        P(AXES, None),
        P(AXES, None),
        P(AXES, None),
        P(None, AXES),
    )
    return jax.shard_map(
        body,
        mesh=mesh,
        in_specs=(P("dp", None, "seq"), P("dp", None), P("dp"), P("dp")) + whole * 3,
        out_specs=(P(), P(), P()) + whole * 3,
        check_vma=False,
    )
```

```python
import functools

import jax
import jax.numpy as jnp
from jax import lax
from jax.experimental import pallas as pl
from jax.experimental.pallas import tpu as pltpu
from jax.sharding import PartitionSpec as P

HEADS = 12
HEAD_DIM = 64
EPS = 1e-06
RATE = 10000.0
MOMENT = 0.5
DECAY = 0.5
CLIP = 0.01
SLOTS = 1024
GROUP = 128
ROWS = 288
BLOCKS = 4
SIZES = (128, 256, 384, 512)
AXES = ("dp", "seq")
bf = jnp.bfloat16
f32 = jnp.float32


def mm(left, right):
    return jnp.dot(left, right, preferred_element_type=f32)


def mm_left(left, right):
    return lax.dot_general(left, right, (((0,), (0,)), ((), ())), preferred_element_type=f32)


def mm_right(left, right):
    return lax.dot_general(left, right, (((1,), (1,)), ((), ())), preferred_element_type=f32)


def exchange(v):
    return lax.all_to_all(v, AXES, 0, 0, tiled=True)


def slots_of(devices):
    return max(16, SLOTS // devices)


def route(ids, valid, per_owner):
    count = ids.shape[0]
    spot = jnp.arange(count, dtype=jnp.int32)
    owner = ids // per_owner
    local = ids - owner * per_owner
    key = jnp.where(valid, ids, -1 - spot)
    alike = key[:, None] == key[None, :]
    first_at = jnp.min(jnp.where(alike, spot[None, :], count), axis=1)
    first = (first_at == spot) & valid
    before = (owner[:, None] == owner[None, :]) & first[None, :] & (spot[None, :] < first_at[:, None])
    rank = jnp.sum(before.astype(jnp.int32), axis=1)
    return owner, local, first, rank


def requests(owner, local, first, rank, start, devices):
    room = slots_of(devices)
    slot = jnp.where(first & (rank >= start) & (rank < start + room), owner * room + rank - start, -1)
    line = jnp.arange(devices * room, dtype=jnp.int32)
    hit = slot[None, :] == line[:, None]
    return jnp.max(jnp.where(hit, local[None, :], -1), axis=1)


def token_slots(owner, valid, rank, start, room):
    return jnp.where(valid & (rank >= start) & (rank < start + room), owner * room + rank - start, -1)


def one_hot(index, size):
    return (index[:, None] == jnp.arange(size, dtype=jnp.int32)[None, :]).astype(bf)


NEAR = 0.3
TAIL = (
    0.11962924781130464, 0.12075473126046088, 0.09990870957740686, 0.12857719637511858,
    -0.05371263258867769, 0.2063844888355699, -0.15722075016774184, 0.03567893567949022,
)


def dot(left, right):
    return jnp.dot(left, right, preferred_element_type=f32)


def dot_nt(left, right):
    return lax.dot_general(left, right, (((1,), (1,)), ((), ())), preferred_element_type=f32)


def dot_tn(left, right):
    return lax.dot_general(left, right, (((0,), (0,)), ((), ())), preferred_element_type=f32)


def iota(shape, axis):
    return lax.broadcasted_iota(jnp.int32, shape, axis)


def normal(v):
    center = v - jnp.mean(v, axis=-1, keepdims=True)
    scale = lax.rsqrt(jnp.mean(center * center, axis=-1, keepdims=True) + EPS)
    return center * scale, scale


def normal_back(grad, unit, scale):
    inner = jnp.mean(grad * unit, axis=-1, keepdims=True)
    return scale * (grad - jnp.mean(grad, axis=-1, keepdims=True) - unit * inner)


def column_sums(v):
    return dot(jnp.full((8, v.shape[0]), 1.0, bf), v)[:1]


def gelu_pair(v):
    bell = jnp.exp(v * v * -0.5)
    t = 1.0 / (1.0 + NEAR * jnp.abs(v))
    poly = TAIL[-1]
    for c in TAIL[-2::-1]:
        poly = poly * t + c
    tail = poly * t * bell
    area = jnp.where(v < 0, tail, 1.0 - tail)
    return v * area, area + v * bell * 0.3989422804014327


def params(limit, **more):
    return pltpu.CompilerParams(vmem_limit_bytes=limit << 20, **more)


def fixed(shape, index):
    return pl.BlockSpec(shape, lambda *_: index, pipeline_mode=pl.Buffered(1))


def spread(depth, turns, src, out):
    width = out.shape[1]
    if depth % 8:
        out[...] = src[...]
        return

    def pair(index, carry):
        tall = src[pl.ds(pl.multiple_of(index * 2 * depth, 16), 2 * depth), :].astype(f32)
        parts = []
        for e in range(2):
            for j in range(turns):
                parts.append(tall[e * depth : (e + 1) * depth, j * width : (j + 1) * width])
        to = pl.multiple_of(index * 2 * depth * turns, 16)
        out[pl.ds(to, 2 * depth * turns), :] = jnp.concatenate(parts, axis=0).astype(bf)
        return carry

    lax.fori_loop(0, src.shape[0] // (2 * depth), pair, 0)


def live_rows(plan, shape):
    row = iota(shape, 0) + pl.program_id(0) * shape[0]
    return row < plan[0], (row >= plan[2]) & (row < plan[2] + plan[1])


def when_live(kernel):
    def run(*refs):
        pl.when(pl.program_id(0) < refs[0][3])(lambda: kernel(*refs))

    return run


def first_kernel(plan, slot, spot_in, back, extra, w_qkv, pos_t, vec_t, x_out, hin_out, qkv_out, vec_out):
    rows, width = x_out.shape
    length = pos_t.shape[1]
    vec = dot_nt((iota((16, 128), 0) == iota((16, 128), 1)).astype(f32).astype(bf), vec_t[...])
    vec_out[...] = vec
    where = jnp.where(slot[...] == iota((rows, back.shape[0]), 1), 1.0, 0.0).astype(bf)
    line = jnp.where(spot_in[...] == iota((rows, length), 1), 1.0, 0.0).astype(bf)
    x = dot(where, back[...]) + extra[...].astype(f32) + dot_nt(line, pos_t[...])
    x_out[...] = x
    unit, _ = normal(x)
    hin = (unit * vec[0:1] + vec[1:2]).astype(bf)
    hin_out[...] = hin
    qkv_out[:, :width] = (dot(hin, w_qkv[:, :width]) + vec[2:3]).astype(bf)
    qkv_out[:, width : 2 * width] = dot(hin, w_qkv[:, width : 2 * width]).astype(bf)
    qkv_out[:, 2 * width :] = (dot(hin, w_qkv[:, 2 * width :]) + vec[3:4]).astype(bf)


def head_parts(size, query, keys, half):
    shape = query.shape
    lane = iota(shape, 1)
    live = iota(shape, 0) < size
    inside = ((lane // HEAD_DIM) == half) & live
    spare = lane == (1 - half) * HEAD_DIM
    key = jnp.where(inside, keys.astype(f32), jnp.where(spare & ~live, -1e30, 0.0)).astype(bf)
    ask = jnp.where(inside, query.astype(f32) * 0.125, jnp.where(spare, 1.0, 0.0)).astype(bf)
    return inside, ask, key


def each_sentence(plan, run):
    def one(index, carry):
        size = jnp.where(index == 0, plan[0], plan[1])
        start = pl.multiple_of(jnp.where(index == 0, 0, plan[2]), 16)
        under = 0
        for count in SIZES:
            pl.when((size > under) & (size <= count))(functools.partial(run, pl.ds(start, count), size))
            under = count
        return carry

    lax.fori_loop(0, 2, one, 0)


def attend_kernel(plan, query, keys, values, out):
    out[...] = jnp.zeros_like(out)

    def run(rows, size):
        total = None
        for half in range(2):
            inside, ask, key = head_parts(size, query[rows, :], keys[rows, :], half)
            score = dot_nt(ask, key)
            power = jnp.exp(score - jnp.max(score, axis=1, keepdims=True))
            prob = (power * (1.0 / jnp.sum(power, axis=1, keepdims=True))).astype(bf)
            part = dot(prob, jnp.where(inside, values[rows, :].astype(f32), 0.0).astype(bf))
            total = part if total is None else total + part
        out[rows, :] = total.astype(bf)

    each_sentence(plan, run)


def attend_back_kernel(plan, query, keys, values, d_out, *more):
    d_proj = more[-1]
    d_proj[...] = jnp.zeros_like(d_proj)
    plus = lambda a, b: b if a is None else a + b

    def run(rows, size):
        d_query, d_key, d_value = None, None, None
        for half in range(2):
            inside, ask, key = head_parts(size, query[rows, :], keys[rows, :], half)
            clean = lambda v: jnp.where(inside, v.astype(f32), 0.0).astype(bf)
            score = dot_nt(key, ask)
            power = jnp.exp(score - jnp.max(score, axis=0, keepdims=True))
            prob = power * (1.0 / jnp.sum(power, axis=0, keepdims=True))
            grad = clean(d_out[rows, :])
            d_value = plus(d_value, dot(prob.astype(bf), grad))
            d_prob = dot_nt(clean(values[rows, :]), grad)
            inner = jnp.sum(prob * d_prob, axis=0, keepdims=True)
            d_score = (prob * (d_prob - inner)).astype(bf)
            d_key = plus(d_key, dot(d_score, clean(ask)))
            d_query = plus(d_query, dot_tn(d_score, clean(key)))
        d_proj[0, rows, :] = (d_query * 0.125).astype(bf)
        d_proj[1, rows, :] = d_key.astype(bf)
        d_proj[2, rows, :] = d_value.astype(bf)

    each_sentence(plan, run)


def middle_kernel(depth, turns, plan, x, mixed, w_out, w_in, w_src, vec, vec_ff, z1_out, h1_out, act_out, slope_out, z2_out, pooled, w_back):
    rows, width = x.shape
    pl.when(pl.program_id(0) == 0)(lambda: spread(depth, turns, w_src, w_back))
    unit, _ = normal(x[...])
    h0 = unit * vec[0:1] + vec[1:2]
    z1 = h0 + dot(mixed[...], w_out[...]) + vec[4:5]
    z1_out[...] = z1
    unit, _ = normal(z1)
    h1 = unit * vec[5:6] + vec[6:7]
    h1_b = h1.astype(bf)
    h1_out[...] = h1_b
    y = None
    for j in range(turns):
        at = slice(j * width, (j + 1) * width)
        hidden = dot(h1_b, w_in[:, at]) + vec_ff[:, at]
        act, slope = gelu_pair(hidden)
        act = act.astype(bf)
        act_out[:, at] = act
        slope_out[:, at] = slope.astype(bf)
        part = dot(act, w_back[at, :])
        y = part if y is None else y + part
    z2 = h1 + y + vec[7 + turns : 8 + turns]
    z2_out[...] = z2
    unit, _ = normal(z2)
    h2 = unit * vec[8 + turns : 9 + turns] + vec[9 + turns : 10 + turns]
    sums = [jnp.sum(jnp.where(keep, h2, 0.0), axis=0, keepdims=True) for keep in live_rows(plan, (rows, width))]

    @pl.when(pl.program_id(0) == 0)
    def _():
        pooled[...] = jnp.zeros_like(pooled)

    line = iota(pooled.shape, 0)
    pooled[...] += jnp.where(line == 0, sums[0], jnp.where(line == 1, sums[1], 0.0))


def back_kernel(plan, facts, holders, pooled, all_pooled, z1, slope, z2, w_out, w_in, w_back, vec, d_y_out, d_f_out, d_r1_out, d_a_out, d_o_out, sums, sums_ff, loss):
    rows, width = z1.shape
    step = pl.program_id(0)
    total = lambda a, b: jnp.sum(a * b, axis=1, keepdims=True)
    count = facts[10]
    grads, losses = [], []
    for i in range(2):
        labeled, gold, size, other_size, counts = (facts[5 * i + j] for j in range(5))
        own, other = pooled[i : i + 1] / size, all_pooled[pl.ds(holders[i], 1), :] / other_size
        cross = total(own, other)
        root, other_root = lax.rsqrt(total(own, own) + EPS), lax.rsqrt(total(other, other) + EPS)
        miss = cross * root * other_root - gold
        losses.append(counts * miss * miss)
        push = 2.0 * labeled * miss / count
        grads.append(push * (other * root * other_root - cross * root * root * root * other_root * own) / size)
    loss[...] = jnp.broadcast_to(losses[0] + losses[1], loss.shape)
    keep = live_rows(plan, (rows, width))
    d_h2 = jnp.where(keep[0], grads[0], jnp.where(keep[1], grads[1], 0.0))
    turns = w_in.shape[1] // width

    unit, scale = normal(z2[...])
    d_g2 = jnp.sum(d_h2 * unit, axis=0, keepdims=True)
    d_b2n = jnp.sum(d_h2, axis=0, keepdims=True)
    d_r2 = normal_back(d_h2 * vec[8 + turns : 9 + turns], unit, scale)
    d_y = d_r2.astype(bf)
    d_y_out[...] = d_y
    d_h1 = d_r2
    ff = []
    for j in range(turns):
        at = slice(j * width, (j + 1) * width)
        d_f = (dot_nt(d_y, w_back[at, :]) * slope[:, at].astype(f32)).astype(bf)
        d_f_out[:, at] = d_f
        ff.append(column_sums(d_f))
        d_h1 = d_h1 + dot_nt(d_f, w_in[:, at])
    unit, scale = normal(z1[...])
    d_g1 = jnp.sum(d_h1 * unit, axis=0, keepdims=True)
    d_b1 = jnp.sum(d_h1, axis=0, keepdims=True)
    d_r1 = normal_back(d_h1 * vec[5:6], unit, scale)
    d_r1_out[...] = d_r1
    d_a = d_r1.astype(bf)
    d_a_out[...] = d_a
    d_o_out[...] = dot_nt(d_a, w_out[...]).astype(bf)
    fresh = jnp.concatenate([column_sums(d_a), d_g1, d_b1, column_sums(d_y), d_g2, d_b2n, d_g2, d_b2n], axis=0)

    @pl.when(step == 0)
    def _():
        sums[...] = jnp.zeros_like(sums)
        sums_ff[...] = jnp.zeros_like(sums_ff)

    sums[...] += fresh
    sums_ff[...] += jnp.concatenate(ff, axis=0)


def last_kernel(plan, slot, x, d_r1, d_proj, w_qkv, vec, d_x_out, sums, rows_out, total):
    rows, width = x.shape
    step = pl.program_id(0)
    d_h0 = d_r1[...]
    for i in range(3):
        d_h0 = d_h0 + dot_nt(d_proj[i], w_qkv[:, i * width : (i + 1) * width])
    unit, scale = normal(x[...])
    d_ge = jnp.sum(d_h0 * unit, axis=0, keepdims=True)
    d_be = jnp.sum(d_h0, axis=0, keepdims=True)
    d_x = normal_back(d_h0 * vec[0:1], unit, scale)
    d_xb = d_x.astype(bf)
    d_x_out[...] = d_xb
    bias_q, bias_v = column_sums(d_proj[0]), column_sums(d_proj[2])
    fresh = jnp.concatenate([d_ge, d_be, bias_q, bias_v, d_ge, d_be, bias_q, bias_v], axis=0)
    hit = jnp.where(slot[...] == iota((rows, rows_out.shape[0]), 1), 1.0, 0.0).astype(bf)

    @pl.when(step == 0)
    def _():
        sums[...] = jnp.zeros_like(sums)
        total[...] = jnp.zeros_like(total)

    sums[...] += fresh
    total[...] += dot_tn(hit, d_xb)

    @pl.when(step == plan[3] - 1)
    def _():
        rows_out[...] = total[...].astype(bf)


def blocks(v, depth):
    return v.reshape(v.shape[0] // depth, depth, v.shape[1])


def put_split(outs, kind, g, mine):
    g = g.reshape((g.shape[0] // 2, 2) + g.shape[1:])
    even, odd = g[:, 0], g[:, 1]
    cut = outs[0].shape[1]
    keep, send = outs[:2] if kind < cut else outs[2:]
    at = kind if kind < cut else kind - cut
    keep[:, at] = jnp.where(mine == 0, even, odd).astype(bf)
    send[:, at] = jnp.where(mine == 0, odd, even).astype(bf)


def by_blocks(plan, run):
    for count in range(2, BLOCKS + 1):
        pl.when(plan[3] == count)(functools.partial(run, count * ROWS))


def dense_grads_kernel(depth, turns, plan, act, d_y, h1, d_f, mixed, d_a, *outs):
    width = d_y.shape[1]
    mine = plan[4]

    def run(rows):
        g = dot_tn(act[:rows], d_y[:rows])
        g = g.reshape(2 * outs[0].shape[0], turns, depth, width)
        for j in range(turns):
            put_split(outs, j, g[:, j], mine)
        for j in range(turns):
            put_split(outs, turns + j, blocks(dot_tn(h1[:rows], d_f[:rows, j * width : (j + 1) * width]), depth), mine)
        put_split(outs, 2 * turns, blocks(dot_tn(mixed[:rows], d_a[:rows]), depth), mine)

    by_blocks(plan, run)


def rest_grads_kernel(depth, length, plan, spot_in, hin, d_proj, d_x, sums_0, sums, sums_ff, *outs):
    width = d_proj.shape[2]
    part = hin.shape[1]
    mine = plan[4]

    def run(rows):
        for i in range(3):
            put_split(outs, i, blocks(dot_tn(hin[:rows], d_proj[i, :rows]), depth), mine)
        line = jnp.where(spot_in[:rows] == iota((rows, length), 1), 1.0, 0.0).astype(bf)
        g_pos = dot_tn(d_x[:rows], line)
        vec = jnp.concatenate([sums_0[:4], sums[:3], sums_ff[...], sums[3:6]], axis=0)
        vec = jnp.concatenate([vec, jnp.zeros((128 - vec.shape[0], part), f32)], axis=0)
        put_split(outs, 3, blocks(jnp.concatenate([g_pos, vec.T, jnp.zeros((part, width - length - 128), f32)], axis=1), depth), mine)

    by_blocks(plan, run)


def cost(flops, nbytes):
    return pl.CostEstimate(flops=int(flops), bytes_accessed=int(nbytes), transcendentals=0)


def run_forward_backward(full, back, extra, slots, spots, plan, meet, staged, devices, depth, length, hidden):
    width = back.shape[1]
    rows = slots.shape[0]
    turns = hidden // width
    pairs = width // GROUP
    shape = jax.ShapeDtypeStruct
    at_row = lambda i, plan: jnp.minimum(i, plan[3] - 1)
    row = lambda cols: pl.BlockSpec((ROWS, cols), lambda i, plan, *_: (at_row(i, plan), 0))
    column = lambda block: fixed((width, width), (0, block))
    at_back = 4 * width + hidden
    whole_out = lambda *dims: pl.BlockSpec(dims, lambda *_: (0,) * len(dims))

    def call(kernel, prefetch, grid, in_specs, out_specs, out_shape, name, scratch=(), **more):
        return pl.pallas_call(
            kernel,
            grid_spec=pltpu.PrefetchScalarGridSpec(
                num_scalar_prefetch=prefetch, grid=grid, in_specs=in_specs, out_specs=out_specs, scratch_shapes=list(scratch)
            ),
            out_shape=out_shape,
            compiler_params=params(60),
            name=name,
            **more,
        )

    tall = depth % 8 == 0
    w_src, w_src_spec = full, fixed((width, turns * width), (0, at_back // (turns * width)))
    if not tall:
        w_src = full[:, at_back : at_back + turns * width].reshape(devices, depth, turns, width)
        w_src, w_src_spec = w_src.transpose(0, 2, 1, 3).reshape(hidden, width), fixed((hidden, width), (0, 0))

    at_pos = at_back + turns * width
    at_vec = at_pos + length
    w_qkv_spec = fixed((width, 3 * width), (0, 0))
    w_out_spec = column(3)
    w_in_spec = fixed((width, hidden), (0, 4 * width // hidden))
    w_back_spec = fixed((hidden, width), (0, 0))
    vec_spec = fixed((16, width), (0, 0))

    x, hin, qkv, vec = call(
        when_live(first_kernel), 1, (BLOCKS,),
        [
            row(1), row(1), fixed(back.shape, (0, 0)), row(width), w_qkv_spec,
            fixed((width, length), (0, at_pos // length)), fixed((width, 128), (0, at_vec // 128)),
        ],
        [row(width), row(width), row(3 * width), whole_out(16, width)],
        [shape((rows, width), f32), shape((rows, width), bf), shape((rows, 3 * width), bf), shape((16, width), f32)],
        "first",
    )(plan, slots[:, None], spots[:, None], back, extra, full, full, full)

    block = lambda part, start=0: pl.BlockSpec((rows, GROUP), lambda p, *_: (0, part * pairs + start + p))
    mixed = call(
        attend_kernel, 1, (pairs,), [block(0), block(1), block(2)], block(0), shape((rows, width), bf), "attend"
    )(plan, qkv, qkv, qkv)

    vec_ff = vec[7 : 7 + turns].reshape(1, hidden)
    z1, h1, act, slope, z2, pooled, w_back = call(
        when_live(functools.partial(middle_kernel, depth, turns)), 1, (BLOCKS,),
        [row(width), row(width), w_out_spec, w_in_spec, w_src_spec, vec_spec, fixed((1, hidden), (0, 0))],
        [row(width), row(width), row(hidden), row(hidden), row(width), whole_out(8, width), whole_out(hidden, width)],
        [
            shape((rows, width), f32), shape((rows, width), bf), shape((rows, hidden), bf), shape((rows, hidden), bf),
            shape((rows, width), f32), shape((8, width), f32), shape((hidden, width), bf),
        ],
        "middle",
    )(plan, x, mixed, full, full, w_src, vec, vec_ff)

    all_pooled = exchange(jnp.broadcast_to(pooled[None, :2], (devices, 2, width))).reshape(2 * devices, width)
    holders, facts = meet
    d_y, d_f, d_r1, d_a, d_o, sums, sums_ff, loss = call(
        when_live(back_kernel), 3, (BLOCKS,),
        [
            fixed((8, width), (0, 0)), fixed((2 * devices, width), (0, 0)), row(width), row(hidden), row(width), w_out_spec, w_in_spec,
            w_back_spec, vec_spec,
        ],
        [
            row(width), row(hidden), row(width), row(width), row(width), whole_out(8, width), whole_out(turns, width),
            whole_out(8, 128),
        ],
        [
            shape((rows, width), bf), shape((rows, hidden), bf), shape((rows, width), f32), shape((rows, width), bf), shape((rows, width), bf),
            shape((8, width), f32), shape((turns, width), f32), shape((8, 128), f32),
        ],
        "back",
    )(plan, facts, holders, pooled, all_pooled, z1, slope, z2, full, full, w_back, vec)

    half = devices // 2
    part = width // 2
    quarter = lambda kinds: pl.BlockSpec((half // 2, kinds, depth, width), lambda i, *_: (i, 0, 0, 0))
    halves = lambda cols: pl.BlockSpec((rows, cols), lambda i, *_: (0, i))
    live = (jnp.arange(rows) < plan[3] * ROWS)[:, None]
    clean = lambda v: jnp.where(live, v, 0)
    if tall:
        dense = call(
            functools.partial(dense_grads_kernel, depth, turns), 1, (2,),
            [
                halves(hidden // 2), fixed((rows, width), (0, 0)), halves(part), fixed((rows, hidden), (0, 0)), halves(part),
                fixed((rows, width), (0, 0)),
            ],
            [quarter(turns)] * 2 + [quarter(turns + 1)] * 2,
            [shape((half, turns, depth, width), bf)] * 2 + [shape((half, turns + 1, depth, width), bf)] * 2,
            "dense_grads",
        )(plan, act, d_y, h1, d_f, mixed, d_a)
    else:
        cut = lambda g: g.astype(bf).reshape(devices, depth, -1, width).transpose(0, 2, 1, 3)
        g_out = dot_tn(clean(act), clean(d_y)).astype(bf).reshape(devices, turns, depth, width)
        g_in, g_mix = dot_tn(clean(h1), clean(d_f)), dot_tn(clean(mixed), clean(d_a))
        dense = jnp.concatenate([g_out, cut(g_in), cut(g_mix)], axis=1)
    if staged:
        dense = over_cores(*dense)
    else:
        d_o, dense = lax.optimization_barrier((d_o, dense))

    def attend_back(start, count, total):
        more = () if total is None else (total,)
        return call(
            attend_back_kernel, 1, (count,),
            [block(0, start), block(1, start), block(2, start), block(0, start)] + [pl.BlockSpec(memory_space=pl.ANY)] * len(more),
            pl.BlockSpec((3, rows, GROUP), lambda p, *_: (0, 0, start + p)),
            shape((3, rows, width), bf),
            "attend_back",
            input_output_aliases={5: 0} if more else {},
            cost_estimate=cost(10 * length * length * GROUP * count, 8 * rows * GROUP * count * 2),
        )(plan, qkv, qkv, qkv, d_o, *more)

    d_proj = attend_back(0, pairs // 2, None)
    if staged:
        d_proj, dense = lax.optimization_barrier((d_proj, dense))
        dense = over_wide(*dense)
    d_proj = attend_back(pairs // 2, pairs - pairs // 2, d_proj)

    d_xb, sums_0, give_rows = call(
        when_live(last_kernel), 1, (BLOCKS,),
        [
            row(1), row(width), row(width), pl.BlockSpec((3, ROWS, width), lambda i, plan: (0, at_row(i, plan), 0)), w_qkv_spec, vec_spec,
        ],
        [row(width), whole_out(8, width), whole_out(*back.shape)],
        [shape((rows, width), bf), shape((8, width), f32), shape(back.shape, bf)],
        "last",
        scratch=[pltpu.VMEM(back.shape, f32)],
    )(plan, slots[:, None], x, d_r1, d_proj, full, vec)

    if staged:
        d_xb, dense = lax.optimization_barrier((d_xb, dense))
    if tall:
        cols = lambda count: pl.BlockSpec((count, part), lambda i, *_: (0, i))
        rest = call(
            functools.partial(rest_grads_kernel, depth, length), 1, (2,),
            [fixed((rows, 1), (0, 0)), halves(part), fixed((3, rows, width), (0, 0, 0)), halves(part), cols(8), cols(8), cols(turns)],
            [quarter(2)] * 4,
            [shape((half, 2, depth, width), bf)] * 4,
            "rest_grads",
        )(plan, spots[:, None], hin, d_proj, d_xb, sums_0, sums, sums_ff)
    else:
        g_vec = jnp.concatenate([sums_0[:4], sums[:3], sums_ff, sums[3:6]], axis=0)
        g_pos = dot_tn(clean(d_xb), one_hot(spots, length))
        spare = jnp.zeros((width, width - length - g_vec.shape[0]), f32)
        rest = [dot_tn(clean(hin), clean(d_proj[i])) for i in range(3)] + [jnp.concatenate([g_pos, g_vec.T, spare], axis=1)]
        rest = jnp.stack([g.astype(bf).reshape(devices, depth, width) for g in rest], axis=1)
    return loss[0, 0], dense, rest, clean(d_xb), give_rows


def swap(v, bit, devices):
    return lax.ppermute(v, AXES, [(i, i ^ bit) for i in range(devices)])


def add(a, b):
    return (a.astype(f32) + b.astype(f32)).astype(bf)


def spot(v, axis, index):
    return lax.dynamic_index_in_dim(v, index, axis, keepdims=False)


def place_in_slice():
    row = lax.axis_index("dp")
    return row // 2, lax.rem(row, 2), lax.axis_index("seq") // 2


def over_cores(keep_one, send_one, keep_two, send_two):
    view = lambda v: v.reshape((4, 2, 2) + v.shape[1:])
    return (view(keep_one), swap(view(send_one), 1, 32)), (view(keep_two), swap(view(send_two), 1, 32))


def part_sum(pair, axis, index):
    return add(spot(pair[0], axis, index), spot(pair[1], axis, index))


def halve(pair, axis, index, bit):
    return part_sum(pair, axis, index), swap(part_sum(pair, axis, 1 - index), bit, 32)


def over_wide(one, two):
    _, y, x = place_in_slice()
    return halve(one, 2, x, 2), halve(two, 1, y, 4)


def over_other(one, two):
    _, y, x = place_in_slice()
    return halve(one, 1, y, 4), halve(two, 1, x, 2)


def over_long(one, two):
    z, _, _ = place_in_slice()
    part = lambda step: jnp.concatenate([part_sum(one, 0, z ^ step), part_sum(two, 0, z ^ step)], axis=0)
    return [part(0)] + [swap(part(step), 8 * step, 32) for step in range(1, 4)]


def total_of(parts):
    return sum(p.astype(f32) for p in parts)


def body(
    token_ids, lengths, labeled, gold,
    embed, position, attn_in, attn_out, ff_in, ff_out, vectors,
    mom_embed, mom_position, mom_attn_in, mom_attn_out, mom_ff_in, mom_ff_out, mom_vectors,
    avg_embed, avg_position, avg_attn_in, avg_attn_out, avg_ff_in, avg_ff_out, avg_vectors,
):
    pairs_here, _, local = token_ids.shape
    seq = lax.axis_size("seq")
    devices = lax.axis_size("dp") * seq
    length = local * seq
    per_owner, width = embed.shape
    depth = attn_in.shape[0]
    hidden = ff_in.shape[1]
    nvec = vectors.shape[0]
    turns = ff_out.shape[0] // depth
    rows = BLOCKS * ROWS
    room = slots_of(devices)
    spare = 128 - nvec

    shard = jnp.concatenate(
        [attn_in, attn_out, ff_in]
        + [ff_out[i * depth : (i + 1) * depth] for i in range(turns)]
        + [position.T, vectors.T, jnp.zeros((depth, spare), f32)],
        axis=1,
    ).astype(bf)
    full = lax.all_gather(shard, AXES, axis=0, tiled=True)

    group = 2 * pairs_here
    info = jnp.concatenate([lengths.reshape(1, group), labeled.reshape(1, pairs_here)], axis=1)
    info = jnp.pad(info, ((0, 0), (0, local - group - pairs_here)))
    news = jnp.concatenate([token_ids.reshape(group, local), info], axis=0)
    news = exchange(jnp.broadcast_to(news[None], (devices,) + news.shape)).reshape(devices // seq, seq, group + 1, local)
    lens = news[:, 0, group, :group].reshape(2 * devices)
    lab = news[:, 0, group, group : group + pairs_here].reshape(devices)
    live = jnp.where(jnp.repeat(lab, 2) > 0, lens, 0)
    index = jnp.arange(2 * devices, dtype=jnp.int32)
    ahead = (live[None, :] > live[:, None]) | ((live[None, :] == live[:, None]) & (index[None, :] < index[:, None]))
    order = jnp.sum(ahead.astype(jnp.int32), axis=1)
    me = lax.axis_index("dp") * seq + lax.axis_index("seq")
    take = lambda values, i: jnp.sum(jnp.where(index[: values.shape[0]] == i, values, 0))
    chosen = [jnp.sum(jnp.where(order == rank, index, 0)) for rank in (me, 2 * devices - 1 - me)]
    count = jnp.maximum(jnp.sum(lab).astype(f32), 1.0)
    size = [take(live, i) for i in chosen]
    start = (size[0] + 15) // 16 * 16
    two_ids = [
        lax.dynamic_slice(news, (i // group, 0, lax.rem(i, group), 0), (1, seq, 1, local)).reshape(length) for i in chosen
    ]
    ids = lax.dynamic_update_slice(jnp.pad(two_ids[0], (0, rows - length)), two_ids[1], (start,))
    line = jnp.arange(rows, dtype=jnp.int32)
    in_first, in_second = line < size[0], (line >= start) & (line < start + size[1])
    used = in_first | in_second
    spots = jnp.where(in_first, line, jnp.where(in_second, line - start, -1))
    total = jnp.where(size[1] > 0, start + size[1], size[0])
    core = lax.rem(lax.axis_index("seq"), 2)
    plan = jnp.stack([size[0], size[1], start, jnp.clip((total + ROWS - 1) // ROWS, 2, BLOCKS), core])
    owner, place, first, rank = route(ids, used, per_owner)
    most = jnp.max(jnp.where(used, rank + 1, 0))
    asked = requests(owner, place, first, rank, 0, devices).reshape(devices, room)
    note = jnp.broadcast_to(most, (devices, 1))
    got = exchange(jnp.concatenate([asked, note, jnp.zeros((devices, 127 - room), jnp.int32)], axis=1))
    rounds = (jnp.max(got[:, room]) + room - 1) // room

    table = embed.astype(bf)
    slots = token_slots(owner, used, rank, 0, room)
    wanted_first = got[:, :room].reshape(-1)

    def pick(wanted):
        picked = mm(one_hot(wanted, per_owner), table).astype(bf).reshape(devices, room, width)
        return exchange(picked).reshape(devices * room, width)

    back = pick(wanted_first)

    def ask_again(start):
        return exchange(requests(owner, place, first, rank, start, devices).reshape(devices, room)).reshape(-1)

    def more(state):
        step, total = state
        start = step * room
        there = one_hot(token_slots(owner, used, rank, start, room), devices * room)
        return step + 1, total + mm(there, pick(ask_again(start))).astype(bf)

    _, extra = lax.while_loop(lambda state: state[0] < rounds, more, (jnp.int32(1), jnp.zeros((rows, width), bf)))

    all_gold = exchange(jnp.broadcast_to(gold[None], (devices, pairs_here))).reshape(devices // seq, seq, pairs_here)[:, 0]
    all_gold = all_gold.reshape(devices)
    holders, facts = [], []
    for i in chosen:
        other, pair = i ^ 1, i // 2
        rank = take(order, other)
        holders.append(jnp.where(rank < devices, 2 * rank, 2 * (2 * devices - 1 - rank) + 1))
        weight = take(lab, pair).astype(f32)
        own = jnp.where(lax.rem(i, 2) == 0, weight, 0.0)
        facts += [weight, take(all_gold, pair), take(lens, i).astype(f32), take(lens, other).astype(f32), own]
    meet = jnp.stack(holders), jnp.stack(facts + [count])

    staged = (seq, devices) == (4, 32) and depth % 8 == 0
    loss, dense, rest, d_xb, give_rows = run_forward_backward(
        full, back, extra, slots, spots, plan, meet, staged, devices, depth, length, hidden
    )

    def sum_up(parts):
        if isinstance(parts, list | tuple):
            keep, send = (jnp.concatenate([parts[i], parts[i + 2]], axis=1) for i in range(2))
            both = jnp.stack([jnp.where(core == 0, keep, send), jnp.where(core == 0, send, keep)], axis=1)
            parts = both.reshape((devices,) + keep.shape[1:])
        return lax.psum_scatter(parts, AXES, scatter_dimension=0, tiled=True).astype(f32)[0]

    give_rows = exchange(give_rows.reshape(devices, room, width))
    if staged:
        dense = over_other(*dense)
        rest = over_wide(*over_cores(*rest))
        dense, give_rows = lax.optimization_barrier((dense, give_rows))
        dense = over_long(*dense)
        rest = over_other(*rest)
        dense, rest = lax.optimization_barrier((dense, rest))
        rest = over_long(*rest)
        dense, rest = total_of(dense), total_of(rest)
    else:
        dense, rest = sum_up(dense), sum_up(rest)
    beside = lambda v: jnp.concatenate(list(v), axis=1)
    g_ff_out = dense[:turns].reshape(turns * depth, width)
    g_ff_in = beside(dense[turns : 2 * turns])
    g_attn_out = dense[2 * turns]
    g_attn_in = beside(rest[:3])
    g_position = rest[3, :, :length].T
    g_vectors = rest[3, :, length : length + nvec].T

    def give(wanted, there):
        return mm_left(one_hot(wanted, per_owner), there.reshape(devices * room, width))

    def more_back(state):
        step, total = state
        start = step * room
        sums = mm_left(one_hot(token_slots(owner, used, rank, start, room), devices * room), d_xb).astype(bf)
        return step + 1, total + give(ask_again(start), exchange(sums.reshape(devices, room, width)))

    _, g_embed = lax.while_loop(lambda state: state[0] < rounds, more_back, (jnp.int32(1), give(wanted_first, give_rows)))

    grads = (g_embed, g_position, g_attn_in, g_attn_out, g_ff_in, g_ff_out, g_vectors)
    squares = sum(jnp.sum(g * g) for g in (g_embed, dense, rest))
    sums = exchange(jnp.broadcast_to(jnp.stack([squares, loss])[None, :], (devices, 2)))
    sums = jnp.sum(sums, axis=0)
    norm = jnp.sqrt(sums[0])
    loss_sum = sums[1]
    scale = jnp.minimum(1.0, CLIP / (norm + 1e-06))
    weights = (embed, position, attn_in, attn_out, ff_in, ff_out, vectors)
    moms = (mom_embed, mom_position, mom_attn_in, mom_attn_out, mom_ff_in, mom_ff_out, mom_vectors)
    avgs = (avg_embed, avg_position, avg_attn_in, avg_attn_out, avg_ff_in, avg_ff_out, avg_vectors)
    news, next_moms, next_avgs = [], [], []
    for weight, grad, mom, avg in zip(weights, grads, moms, avgs):
        clipped = grad * scale
        moment = MOMENT * mom + clipped
        fresh = weight - RATE * (clipped + MOMENT * moment)
        news.append(fresh)
        next_moms.append(moment)
        next_avgs.append(DECAY * avg + (1.0 - DECAY) * fresh)
    return (loss_sum, count, norm, *news, *next_moms, *next_avgs)


def solution(mesh):
    whole = (
        P(AXES, None),
        P(None, AXES),
        P(AXES, None),
        P(AXES, None),
        P(AXES, None),
        P(AXES, None),
        P(None, AXES),
    )
    return jax.shard_map(
        body,
        mesh=mesh,
        in_specs=(P("dp", None, "seq"), P("dp", None), P("dp"), P("dp")) + whole * 3,
        out_specs=(P(), P(), P()) + whole * 3,
        check_vma=False,
    )
```

```python
import functools

import jax
import jax.numpy as jnp
from jax import lax
from jax.experimental import pallas as pl
from jax.experimental.pallas import tpu as pltpu
from jax.sharding import PartitionSpec as P

HEADS = 12
HEAD_DIM = 64
EPS = 1e-06
RATE = 10000.0
MOMENT = 0.5
DECAY = 0.5
CLIP = 0.01
SLOTS = 1024
GROUP = 128
ROWS = 288
BLOCKS = 4
SIZES = (128, 256, 384, 512)
AXES = ("dp", "seq")
bf = jnp.bfloat16
f32 = jnp.float32


def mm(left, right):
    return jnp.dot(left, right, preferred_element_type=f32)


def mm_left(left, right):
    return lax.dot_general(left, right, (((0,), (0,)), ((), ())), preferred_element_type=f32)


def mm_right(left, right):
    return lax.dot_general(left, right, (((1,), (1,)), ((), ())), preferred_element_type=f32)


def exchange(v):
    return lax.all_to_all(v, AXES, 0, 0, tiled=True)


def slots_of(devices):
    return max(16, SLOTS // devices)


def route(ids, valid, per_owner):
    count = ids.shape[0]
    spot = jnp.arange(count, dtype=jnp.int32)
    owner = ids // per_owner
    local = ids - owner * per_owner
    key = jnp.where(valid, ids, -1 - spot)
    alike = key[:, None] == key[None, :]
    first_at = jnp.min(jnp.where(alike, spot[None, :], count), axis=1)
    first = (first_at == spot) & valid
    before = (owner[:, None] == owner[None, :]) & first[None, :] & (spot[None, :] < first_at[:, None])
    rank = jnp.sum(before.astype(jnp.int32), axis=1)
    return owner, local, first, rank


def requests(owner, local, first, rank, start, devices):
    room = slots_of(devices)
    slot = jnp.where(first & (rank >= start) & (rank < start + room), owner * room + rank - start, -1)
    line = jnp.arange(devices * room, dtype=jnp.int32)
    hit = slot[None, :] == line[:, None]
    return jnp.max(jnp.where(hit, local[None, :], -1), axis=1)


def token_slots(owner, valid, rank, start, room):
    return jnp.where(valid & (rank >= start) & (rank < start + room), owner * room + rank - start, -1)


def one_hot(index, size):
    return (index[:, None] == jnp.arange(size, dtype=jnp.int32)[None, :]).astype(bf)


NEAR = 0.3
TAIL = (
    0.11962924781130464, 0.12075473126046088, 0.09990870957740686, 0.12857719637511858,
    -0.05371263258867769, 0.2063844888355699, -0.15722075016774184, 0.03567893567949022,
)


def dot(left, right):
    return jnp.dot(left, right, preferred_element_type=f32)


def dot_nt(left, right):
    return lax.dot_general(left, right, (((1,), (1,)), ((), ())), preferred_element_type=f32)


def dot_tn(left, right):
    return lax.dot_general(left, right, (((0,), (0,)), ((), ())), preferred_element_type=f32)


def iota(shape, axis):
    return lax.broadcasted_iota(jnp.int32, shape, axis)


def normal(v):
    center = v - jnp.mean(v, axis=-1, keepdims=True)
    scale = lax.rsqrt(jnp.mean(center * center, axis=-1, keepdims=True) + EPS)
    return center * scale, scale


def normal_back(grad, unit, scale):
    inner = jnp.mean(grad * unit, axis=-1, keepdims=True)
    return scale * (grad - jnp.mean(grad, axis=-1, keepdims=True) - unit * inner)


def column_sums(v):
    return dot(jnp.full((8, v.shape[0]), 1.0, bf), v)[:1]


def gelu_pair(v):
    bell = jnp.exp(v * v * -0.5)
    t = 1.0 / (1.0 + NEAR * jnp.abs(v))
    poly = TAIL[-1]
    for c in TAIL[-2::-1]:
        poly = poly * t + c
    tail = poly * t * bell
    area = jnp.where(v < 0, tail, 1.0 - tail)
    return v * area, area + v * bell * 0.3989422804014327


def params(limit, **more):
    return pltpu.CompilerParams(vmem_limit_bytes=limit << 20, **more)


def fixed(shape, index):
    return pl.BlockSpec(shape, lambda *_: index, pipeline_mode=pl.Buffered(1))


def spread(staged, depth, turns, src, out):
    width = out.shape[1]
    if not staged:
        out[...] = src[...]
        return

    def pair(index, carry):
        tall = src[pl.ds(pl.multiple_of(index * 2 * depth, 16), 2 * depth), :].astype(f32)
        parts = []
        for e in range(2):
            for j in range(turns):
                parts.append(tall[e * depth : (e + 1) * depth, j * width : (j + 1) * width])
        to = pl.multiple_of(index * 2 * depth * turns, 16)
        out[pl.ds(to, 2 * depth * turns), :] = jnp.concatenate(parts, axis=0).astype(bf)
        return carry

    lax.fori_loop(0, src.shape[0] // (2 * depth), pair, 0)


def live_rows(plan, shape):
    row = iota(shape, 0) + pl.program_id(0) * shape[0]
    return row < plan[0], (row >= plan[2]) & (row < plan[2] + plan[1])


def when_live(kernel):
    def run(*refs):
        pl.when(pl.program_id(0) < refs[0][3])(lambda: kernel(*refs))

    return run


def first_kernel(plan, slot, spot_in, back, extra, w_qkv, pos_t, vec_t, x_out, hin_out, qkv_out, vec_out):
    rows, width = x_out.shape
    length = pos_t.shape[1]
    vec = dot_nt((iota((16, 128), 0) == iota((16, 128), 1)).astype(f32).astype(bf), vec_t[...])
    vec_out[...] = vec
    where = jnp.where(slot[...] == iota((rows, back.shape[0]), 1), 1.0, 0.0).astype(bf)
    line = jnp.where(spot_in[...] == iota((rows, length), 1), 1.0, 0.0).astype(bf)
    x = dot(where, back[...]) + extra[...].astype(f32) + dot_nt(line, pos_t[...])
    x_out[...] = x
    unit, _ = normal(x)
    hin = (unit * vec[0:1] + vec[1:2]).astype(bf)
    hin_out[...] = hin
    qkv_out[:, :width] = (dot(hin, w_qkv[:, :width]) + vec[2:3]).astype(bf)
    qkv_out[:, width : 2 * width] = dot(hin, w_qkv[:, width : 2 * width]).astype(bf)
    qkv_out[:, 2 * width :] = (dot(hin, w_qkv[:, 2 * width :]) + vec[3:4]).astype(bf)


def head_parts(size, query, keys, half):
    shape = query.shape
    lane = iota(shape, 1)
    live = iota(shape, 0) < size
    inside = ((lane // HEAD_DIM) == half) & live
    spare = lane == (1 - half) * HEAD_DIM
    key = jnp.where(inside, keys.astype(f32), jnp.where(spare & ~live, -1e30, 0.0)).astype(bf)
    ask = jnp.where(inside, query.astype(f32) * 0.125, jnp.where(spare, 1.0, 0.0)).astype(bf)
    return inside, ask, key


def each_sentence(plan, run):
    def one(index, carry):
        size = jnp.where(index == 0, plan[0], plan[1])
        start = pl.multiple_of(jnp.where(index == 0, 0, plan[2]), 16)
        under = 0
        for count in SIZES:
            pl.when((size > under) & (size <= count))(functools.partial(run, pl.ds(start, count), size))
            under = count
        return carry

    lax.fori_loop(0, 2, one, 0)


def attend_kernel(plan, query, keys, values, out):
    out[...] = jnp.zeros_like(out)

    def run(rows, size):
        total = None
        for half in range(2):
            inside, ask, key = head_parts(size, query[rows, :], keys[rows, :], half)
            score = dot_nt(ask, key)
            power = jnp.exp(score - jnp.max(score, axis=1, keepdims=True))
            prob = (power * (1.0 / jnp.sum(power, axis=1, keepdims=True))).astype(bf)
            part = dot(prob, jnp.where(inside, values[rows, :].astype(f32), 0.0).astype(bf))
            total = part if total is None else total + part
        out[rows, :] = total.astype(bf)

    each_sentence(plan, run)


def attend_back_kernel(plan, query, keys, values, d_out, *more):
    d_proj = more[-1]
    d_proj[...] = jnp.zeros_like(d_proj)
    plus = lambda a, b: b if a is None else a + b

    def run(rows, size):
        d_query, d_key, d_value = None, None, None
        for half in range(2):
            inside, ask, key = head_parts(size, query[rows, :], keys[rows, :], half)
            clean = lambda v: jnp.where(inside, v.astype(f32), 0.0).astype(bf)
            score = dot_nt(key, ask)
            power = jnp.exp(score - jnp.max(score, axis=0, keepdims=True))
            prob = power * (1.0 / jnp.sum(power, axis=0, keepdims=True))
            grad = clean(d_out[rows, :])
            d_value = plus(d_value, dot(prob.astype(bf), grad))
            d_prob = dot_nt(clean(values[rows, :]), grad)
            inner = jnp.sum(prob * d_prob, axis=0, keepdims=True)
            d_score = (prob * (d_prob - inner)).astype(bf)
            d_key = plus(d_key, dot(d_score, clean(ask)))
            d_query = plus(d_query, dot_tn(d_score, clean(key)))
        d_proj[0, rows, :] = (d_query * 0.125).astype(bf)
        d_proj[1, rows, :] = d_key.astype(bf)
        d_proj[2, rows, :] = d_value.astype(bf)

    each_sentence(plan, run)


def middle_kernel(staged, depth, turns, plan, x, mixed, w_out, w_in, w_src, vec, vec_ff, z1_out, h1_out, act_out, slope_out, z2_out, pooled, w_back):
    rows, width = x.shape
    pl.when(pl.program_id(0) == 0)(lambda: spread(staged, depth, turns, w_src, w_back))
    unit, _ = normal(x[...])
    h0 = unit * vec[0:1] + vec[1:2]
    z1 = h0 + dot(mixed[...], w_out[...]) + vec[4:5]
    z1_out[...] = z1
    unit, _ = normal(z1)
    h1 = unit * vec[5:6] + vec[6:7]
    h1_b = h1.astype(bf)
    h1_out[...] = h1_b
    y = None
    for j in range(turns):
        at = slice(j * width, (j + 1) * width)
        hidden = dot(h1_b, w_in[:, at]) + vec_ff[:, at]
        act, slope = gelu_pair(hidden)
        act = act.astype(bf)
        act_out[:, at] = act
        slope_out[:, at] = slope.astype(bf)
        part = dot(act, w_back[at, :])
        y = part if y is None else y + part
    z2 = h1 + y + vec[7 + turns : 8 + turns]
    z2_out[...] = z2
    unit, _ = normal(z2)
    h2 = unit * vec[8 + turns : 9 + turns] + vec[9 + turns : 10 + turns]
    sums = [jnp.sum(jnp.where(keep, h2, 0.0), axis=0, keepdims=True) for keep in live_rows(plan, (rows, width))]

    @pl.when(pl.program_id(0) == 0)
    def _():
        pooled[...] = jnp.zeros_like(pooled)

    line = iota(pooled.shape, 0)
    pooled[...] += jnp.where(line == 0, sums[0], jnp.where(line == 1, sums[1], 0.0))


def back_kernel(plan, facts, holders, pooled, all_pooled, z1, slope, z2, w_out, w_in, w_back, vec, d_y_out, d_f_out, d_r1_out, d_a_out, d_o_out, sums, sums_ff, loss):
    rows, width = z1.shape
    step = pl.program_id(0)
    total = lambda a, b: jnp.sum(a * b, axis=1, keepdims=True)
    count = facts[10]
    grads, losses = [], []
    for i in range(2):
        labeled, gold, size, other_size, counts = (facts[5 * i + j] for j in range(5))
        own, other = pooled[i : i + 1] / size, all_pooled[pl.ds(holders[i], 1), :] / other_size
        cross = total(own, other)
        root, other_root = lax.rsqrt(total(own, own) + EPS), lax.rsqrt(total(other, other) + EPS)
        miss = cross * root * other_root - gold
        losses.append(counts * miss * miss)
        push = 2.0 * labeled * miss / count
        grads.append(push * (other * root * other_root - cross * root * root * root * other_root * own) / size)
    loss[...] = jnp.broadcast_to(losses[0] + losses[1], loss.shape)
    keep = live_rows(plan, (rows, width))
    d_h2 = jnp.where(keep[0], grads[0], jnp.where(keep[1], grads[1], 0.0))
    turns = w_in.shape[1] // width

    unit, scale = normal(z2[...])
    d_g2 = jnp.sum(d_h2 * unit, axis=0, keepdims=True)
    d_b2n = jnp.sum(d_h2, axis=0, keepdims=True)
    d_r2 = normal_back(d_h2 * vec[8 + turns : 9 + turns], unit, scale)
    d_y = d_r2.astype(bf)
    d_y_out[...] = d_y
    d_h1 = d_r2
    ff = []
    for j in range(turns):
        at = slice(j * width, (j + 1) * width)
        d_f = (dot_nt(d_y, w_back[at, :]) * slope[:, at].astype(f32)).astype(bf)
        d_f_out[:, at] = d_f
        ff.append(column_sums(d_f))
        d_h1 = d_h1 + dot_nt(d_f, w_in[:, at])
    unit, scale = normal(z1[...])
    d_g1 = jnp.sum(d_h1 * unit, axis=0, keepdims=True)
    d_b1 = jnp.sum(d_h1, axis=0, keepdims=True)
    d_r1 = normal_back(d_h1 * vec[5:6], unit, scale)
    d_r1_out[...] = d_r1
    d_a = d_r1.astype(bf)
    d_a_out[...] = d_a
    d_o_out[...] = dot_nt(d_a, w_out[...]).astype(bf)
    fresh = jnp.concatenate([column_sums(d_a), d_g1, d_b1, column_sums(d_y), d_g2, d_b2n, d_g2, d_b2n], axis=0)

    @pl.when(step == 0)
    def _():
        sums[...] = jnp.zeros_like(sums)
        sums_ff[...] = jnp.zeros_like(sums_ff)

    sums[...] += fresh
    sums_ff[...] += jnp.concatenate(ff, axis=0)


def last_kernel(plan, slot, x, d_r1, d_proj, w_qkv, vec, d_x_out, sums, rows_out, total):
    rows, width = x.shape
    step = pl.program_id(0)
    d_h0 = d_r1[...]
    for i in range(3):
        d_h0 = d_h0 + dot_nt(d_proj[i], w_qkv[:, i * width : (i + 1) * width])
    unit, scale = normal(x[...])
    d_ge = jnp.sum(d_h0 * unit, axis=0, keepdims=True)
    d_be = jnp.sum(d_h0, axis=0, keepdims=True)
    d_x = normal_back(d_h0 * vec[0:1], unit, scale)
    d_xb = d_x.astype(bf)
    d_x_out[...] = d_xb
    bias_q, bias_v = column_sums(d_proj[0]), column_sums(d_proj[2])
    fresh = jnp.concatenate([d_ge, d_be, bias_q, bias_v, d_ge, d_be, bias_q, bias_v], axis=0)
    hit = jnp.where(slot[...] == iota((rows, rows_out.shape[0]), 1), 1.0, 0.0).astype(bf)

    @pl.when(step == 0)
    def _():
        sums[...] = jnp.zeros_like(sums)
        total[...] = jnp.zeros_like(total)

    sums[...] += fresh
    total[...] += dot_tn(hit, d_xb)

    @pl.when(step == plan[3] - 1)
    def _():
        rows_out[...] = total[...].astype(bf)


def blocks(v, depth):
    return v.reshape(v.shape[0] // depth, depth, v.shape[1])


def put_split(outs, order, kind, g, mine):
    keep, send = outs
    for z in range(2):
        for y in range(2):
            for x in range(2):
                owner = 2 * (4 * z + 2 * y + x)
                at = tuple({"z": z, "y": y, "x": x}[axis] for axis in order) + (kind,)
                even, odd = g[owner], g[owner + 1]
                keep[at] = jnp.where(mine == 0, even, odd).astype(bf)
                send[at] = jnp.where(mine == 0, odd, even).astype(bf)


def by_blocks(plan, run):
    for count in range(2, BLOCKS + 1):
        pl.when(plan[3] == count)(functools.partial(run, count * ROWS))


def out_grads_kernel(depth, turns, plan, act, d_y, *outs):
    def run(rows):
        g = dot_tn(act[:rows], d_y[:rows])
        g = g.reshape(16, turns, depth, g.shape[1])
        for j in range(turns):
            put_split(outs, "zxy", j, g[:, j], plan[4])

    by_blocks(plan, run)


def in_grads_kernel(depth, turns, plan, h1, d_f, mixed, d_a, *outs):
    width = d_a.shape[1]

    def run(rows):
        for j in range(turns):
            g = blocks(dot_tn(h1[:rows], d_f[:rows, j * width : (j + 1) * width]), depth)
            if j < 2:
                put_split(outs[:2], "xyz", j, g, plan[4])
            else:
                put_split(outs[2:], "yxz", j - 2, g, plan[4])
        put_split(outs[2:], "yxz", turns - 2, blocks(dot_tn(mixed[:rows], d_a[:rows]), depth), plan[4])

    by_blocks(plan, run)


def rest_grads_kernel(depth, length, plan, spot_in, hin, d_proj, d_x, sums_0, sums, sums_ff, *outs):
    width = d_proj.shape[2]
    part = hin.shape[1]

    def put(kind, g):
        put_split(outs[:2] if kind < 2 else outs[2:], "xyz" if kind < 2 else "yxz", kind % 2, blocks(g, depth), plan[4])

    def run(rows):
        for i in range(3):
            put(i, dot_tn(hin[:rows], d_proj[i, :rows]))
        line = jnp.where(spot_in[:rows] == iota((rows, length), 1), 1.0, 0.0).astype(bf)
        g_pos = dot_tn(d_x[:rows], line)
        vec = jnp.concatenate([sums_0[:4], sums[:3], sums_ff[...], sums[3:6]], axis=0)
        vec = jnp.concatenate([vec, jnp.zeros((128 - vec.shape[0], part), f32)], axis=0)
        put(3, jnp.concatenate([g_pos, vec.T, jnp.zeros((part, width - length - 128), f32)], axis=1))

    by_blocks(plan, run)


def update_kernel(turns, scale, g_embed, dense_out, dense_in, rest, g_position, g_vectors, *refs):
    factor = scale[0]
    weights, moms, avgs, news, next_moms, next_avgs = (refs[7 * i : 7 * i + 7] for i in range(6))

    def one(index, at, grad):
        clipped = grad * factor
        moment = MOMENT * moms[index][at] + clipped
        fresh = weights[index][at] - RATE * (clipped + MOMENT * moment)
        next_moms[index][at] = moment
        news[index][at] = fresh
        next_avgs[index][at] = DECAY * avgs[index][at] + (1.0 - DECAY) * fresh

    every = (slice(None), slice(None))
    one(0, every, g_embed[...])

    @pl.when(pl.program_id(0) == 0)
    def _():
        depth, width = rest.shape[1:]
        cols = lambda j: (slice(None), slice(j * width, (j + 1) * width))
        one(1, every, g_position[...])
        for j in range(3):
            one(2, cols(j), rest[j])
        one(3, every, dense_in[turns])
        for j in range(turns):
            one(4, cols(j), dense_in[j])
            one(5, (slice(j * depth, (j + 1) * depth), slice(None)), dense_out[j])
        one(6, every, g_vectors[...])


def cost(flops, nbytes):
    return pl.CostEstimate(flops=int(flops), bytes_accessed=int(nbytes), transcendentals=0)


def run_forward_backward(full, back, extra, slots, spots, plan, meet, staged, devices, depth, length, hidden):
    width = back.shape[1]
    rows = slots.shape[0]
    turns = hidden // width
    pairs = width // GROUP
    shape = jax.ShapeDtypeStruct
    at_row = lambda i, plan: jnp.minimum(i, plan[3] - 1)
    row = lambda cols: pl.BlockSpec((ROWS, cols), lambda i, plan, *_: (at_row(i, plan), 0))
    column = lambda block: fixed((width, width), (0, block))
    at_back = 4 * width + hidden
    whole_out = lambda *dims: pl.BlockSpec(dims, lambda *_: (0,) * len(dims))

    def call(kernel, prefetch, grid, in_specs, out_specs, out_shape, name, scratch=(), **more):
        return pl.pallas_call(
            kernel,
            grid_spec=pltpu.PrefetchScalarGridSpec(
                num_scalar_prefetch=prefetch, grid=grid, in_specs=in_specs, out_specs=out_specs, scratch_shapes=list(scratch)
            ),
            out_shape=out_shape,
            compiler_params=params(60),
            name=name,
            **more,
        )

    w_src, w_src_spec = full, fixed((width, turns * width), (0, at_back // (turns * width)))
    if not staged:
        w_src = full[:, at_back : at_back + turns * width].reshape(devices, depth, turns, width)
        w_src, w_src_spec = w_src.transpose(0, 2, 1, 3).reshape(hidden, width), fixed((hidden, width), (0, 0))

    at_pos = at_back + turns * width
    at_vec = at_pos + length
    w_qkv_spec = fixed((width, 3 * width), (0, 0))
    w_out_spec = column(3)
    w_in_spec = fixed((width, hidden), (0, 4 * width // hidden))
    w_back_spec = fixed((hidden, width), (0, 0))
    vec_spec = fixed((16, width), (0, 0))

    x, hin, qkv, vec = call(
        when_live(first_kernel), 1, (BLOCKS,),
        [
            row(1), row(1), fixed(back.shape, (0, 0)), row(width), w_qkv_spec,
            fixed((width, length), (0, at_pos // length)), fixed((width, 128), (0, at_vec // 128)),
        ],
        [row(width), row(width), row(3 * width), whole_out(16, width)],
        [shape((rows, width), f32), shape((rows, width), bf), shape((rows, 3 * width), bf), shape((16, width), f32)],
        "first",
    )(plan, slots[:, None], spots[:, None], back, extra, full, full, full)

    block = lambda part, start=0: pl.BlockSpec((rows, GROUP), lambda p, *_: (0, part * pairs + start + p))
    mixed = call(
        attend_kernel, 1, (pairs,), [block(0), block(1), block(2)], block(0), shape((rows, width), bf), "attend"
    )(plan, qkv, qkv, qkv)

    vec_ff = vec[7 : 7 + turns].reshape(1, hidden)
    z1, h1, act, slope, z2, pooled, w_back = call(
        when_live(functools.partial(middle_kernel, staged, depth, turns)), 1, (BLOCKS,),
        [row(width), row(width), w_out_spec, w_in_spec, w_src_spec, vec_spec, fixed((1, hidden), (0, 0))],
        [row(width), row(width), row(hidden), row(hidden), row(width), whole_out(8, width), whole_out(hidden, width)],
        [
            shape((rows, width), f32), shape((rows, width), bf), shape((rows, hidden), bf), shape((rows, hidden), bf),
            shape((rows, width), f32), shape((8, width), f32), shape((hidden, width), bf),
        ],
        "middle",
    )(plan, x, mixed, full, full, w_src, vec, vec_ff)

    all_pooled = exchange(jnp.broadcast_to(pooled[None, :2], (devices, 2, width))).reshape(2 * devices, width)
    holders, facts = meet
    d_y, d_f, d_r1, d_a, d_o, sums, sums_ff, loss = call(
        when_live(back_kernel), 3, (BLOCKS,),
        [
            fixed((8, width), (0, 0)), fixed((2 * devices, width), (0, 0)), row(width), row(hidden), row(width), w_out_spec, w_in_spec,
            w_back_spec, vec_spec,
        ],
        [
            row(width), row(hidden), row(width), row(width), row(width), whole_out(8, width), whole_out(turns, width),
            whole_out(8, 128),
        ],
        [
            shape((rows, width), bf), shape((rows, hidden), bf), shape((rows, width), f32), shape((rows, width), bf), shape((rows, width), bf),
            shape((8, width), f32), shape((turns, width), f32), shape((8, 128), f32),
        ],
        "back",
    )(plan, facts, holders, pooled, all_pooled, z1, slope, z2, full, full, w_back, vec)

    part = width // 2
    halves = lambda cols: pl.BlockSpec((rows, cols), lambda i, *_: (0, i))
    live = (jnp.arange(rows) < plan[3] * ROWS)[:, None]
    clean = lambda v: jnp.where(live, v, 0)

    def split_call(kernel, in_specs, streams, name):
        specs, shapes = [], []
        for order, kinds in streams:
            at = order.index("z")
            dims = tuple(4 if axis == "z" else 2 for axis in order) + (kinds, depth, width)
            index = lambda i, *_, at=at: tuple(i if axis == at else 0 for axis in range(6))
            specs += [pl.BlockSpec((2, 2, 2, kinds, depth, width), index)] * 2
            shapes += [shape(dims, bf)] * 2
        return call(kernel, 1, (2,), in_specs, specs, shapes, name)

    if staged:
        z, y, x_at = place_in_slice()
        dense_out = split_call(
            functools.partial(out_grads_kernel, depth, turns), [halves(hidden // 2), fixed((rows, width), (0, 0))], [("zxy", turns)], "out_grads"
        )(plan, act, d_y)
        dense_out = over_cores(*dense_out)
        dense_in = split_call(
            functools.partial(in_grads_kernel, depth, turns),
            [halves(part), fixed((rows, hidden), (0, 0)), halves(part), fixed((rows, width), (0, 0))],
            [("xyz", 2), ("yxz", turns - 1)],
            "in_grads",
        )(plan, h1, d_f, mixed, d_a)
        d_o, dense_out, dense_in = lax.optimization_barrier((d_o, dense_out, dense_in))
        dense_in = over_cores(*dense_in[:2]), over_cores(*dense_in[2:])
        dense_out = over_long(dense_out, z)
    else:
        dense_out = dot_tn(clean(act), clean(d_y)).astype(bf)
        dense_in = jnp.concatenate([dot_tn(clean(h1), clean(d_f)), dot_tn(clean(mixed), clean(d_a))], axis=1).astype(bf)

    def attend_back(start, count, total):
        more = () if total is None else (total,)
        return call(
            attend_back_kernel, 1, (count,),
            [block(0, start), block(1, start), block(2, start), block(0, start)] + [pl.BlockSpec(memory_space=pl.ANY)] * len(more),
            pl.BlockSpec((3, rows, GROUP), lambda p, *_: (0, 0, start + p)),
            shape((3, rows, width), bf),
            "attend_back",
            input_output_aliases={5: 0} if more else {},
            cost_estimate=cost(10 * length * length * GROUP * count, 8 * rows * GROUP * count * 2),
        )(plan, qkv, qkv, qkv, d_o, *more)

    d_proj = attend_back(0, pairs // 2, None)
    if staged:
        d_proj, dense_in = lax.optimization_barrier((d_proj, dense_in))
        dense_in = halve(dense_in[0], x_at, 2), halve(dense_in[1], y, 4)
    d_proj = attend_back(pairs // 2, pairs - pairs // 2, d_proj)
    if staged:
        d_proj, dense_in = lax.optimization_barrier((d_proj, dense_in))

    d_xb, sums_0, give_rows = call(
        when_live(last_kernel), 1, (BLOCKS,),
        [
            row(1), row(width), row(width), pl.BlockSpec((3, ROWS, width), lambda i, plan: (0, at_row(i, plan), 0)), w_qkv_spec, vec_spec,
        ],
        [row(width), whole_out(8, width), whole_out(*back.shape)],
        [shape((rows, width), bf), shape((8, width), f32), shape(back.shape, bf)],
        "last",
        scratch=[pltpu.VMEM(back.shape, f32)],
    )(plan, slots[:, None], x, d_r1, d_proj, full, vec)

    if staged:
        give_rows, dense_out = lax.optimization_barrier((give_rows, dense_out))
        cols = lambda count: pl.BlockSpec((count, part), lambda i, *_: (0, i))
        rest = split_call(
            functools.partial(rest_grads_kernel, depth, length),
            [fixed((rows, 1), (0, 0)), halves(part), fixed((3, rows, width), (0, 0, 0)), halves(part), cols(8), cols(8), cols(turns)],
            [("xyz", 2), ("yxz", 2)],
            "rest_grads",
        )(plan, spots[:, None], hin, d_proj, d_xb, sums_0, sums, sums_ff)
    else:
        g_vec = jnp.concatenate([sums_0[:4], sums[:3], sums_ff, sums[3:6]], axis=0)
        g_pos = dot_tn(clean(d_xb), one_hot(spots, length))
        spare = jnp.zeros((width, width - length - g_vec.shape[0]), f32)
        rest = [dot_tn(clean(hin), clean(d_proj[i])) for i in range(3)] + [jnp.concatenate([g_pos, g_vec.T, spare], axis=1)]
        rest = jnp.concatenate(rest, axis=1).astype(bf)
    return loss[0, 0], dense_out, dense_in, rest, clean(d_xb), give_rows


def swap(v, bit, devices):
    return lax.ppermute(v, AXES, [(i, i ^ bit) for i in range(devices)])


def add(a, b):
    return (a.astype(f32) + b.astype(f32)).astype(bf)


def spot(v, axis, index):
    return lax.dynamic_index_in_dim(v, index, axis, keepdims=False)


def place_in_slice():
    row = lax.axis_index("dp")
    return row // 2, lax.rem(row, 2), lax.axis_index("seq") // 2


def over_cores(keep, send):
    return keep, swap(send, 1, 32)


def part_sum(pair, index):
    return add(spot(pair[0], 0, index), spot(pair[1], 0, index))


def halve(pair, index, bit):
    return part_sum(pair, index), swap(part_sum(pair, 1 - index), bit, 32)


def over_long(pair, z):
    return [part_sum(pair, z)] + [swap(part_sum(pair, z ^ step), 8 * step, 32) for step in range(1, 4)]


def over_long_both(one, two, z):
    part = lambda step: jnp.concatenate([part_sum(one, z ^ step), part_sum(two, z ^ step)], axis=0)
    return [part(0)] + [swap(part(step), 8 * step, 32) for step in range(1, 4)]


def total_of(parts):
    return sum(p.astype(f32) for p in parts)


def body(
    token_ids, lengths, labeled, gold,
    embed, position, attn_in, attn_out, ff_in, ff_out, vectors,
    mom_embed, mom_position, mom_attn_in, mom_attn_out, mom_ff_in, mom_ff_out, mom_vectors,
    avg_embed, avg_position, avg_attn_in, avg_attn_out, avg_ff_in, avg_ff_out, avg_vectors,
):
    pairs_here, _, local = token_ids.shape
    seq = lax.axis_size("seq")
    devices = lax.axis_size("dp") * seq
    length = local * seq
    per_owner, width = embed.shape
    depth = attn_in.shape[0]
    hidden = ff_in.shape[1]
    nvec = vectors.shape[0]
    turns = ff_out.shape[0] // depth
    rows = BLOCKS * ROWS
    room = slots_of(devices)
    spare = 128 - nvec

    shard = jnp.concatenate(
        [attn_in, attn_out, ff_in]
        + [ff_out[i * depth : (i + 1) * depth] for i in range(turns)]
        + [position.T, vectors.T, jnp.zeros((depth, spare), f32)],
        axis=1,
    ).astype(bf)
    full = lax.all_gather(shard, AXES, axis=0, tiled=True)

    group = 2 * pairs_here
    info = jnp.concatenate([lengths.reshape(1, group), labeled.reshape(1, pairs_here)], axis=1)
    info = jnp.pad(info, ((0, 0), (0, local - group - pairs_here)))
    news = jnp.concatenate([token_ids.reshape(group, local), info], axis=0)
    news = exchange(jnp.broadcast_to(news[None], (devices,) + news.shape)).reshape(devices // seq, seq, group + 1, local)
    lens = news[:, 0, group, :group].reshape(2 * devices)
    lab = news[:, 0, group, group : group + pairs_here].reshape(devices)
    live = jnp.where(jnp.repeat(lab, 2) > 0, lens, 0)
    index = jnp.arange(2 * devices, dtype=jnp.int32)
    ahead = (live[None, :] > live[:, None]) | ((live[None, :] == live[:, None]) & (index[None, :] < index[:, None]))
    order = jnp.sum(ahead.astype(jnp.int32), axis=1)
    me = lax.axis_index("dp") * seq + lax.axis_index("seq")
    take = lambda values, i: jnp.sum(jnp.where(index[: values.shape[0]] == i, values, 0))
    chosen = [jnp.sum(jnp.where(order == rank, index, 0)) for rank in (me, 2 * devices - 1 - me)]
    count = jnp.maximum(jnp.sum(lab).astype(f32), 1.0)
    size = [take(live, i) for i in chosen]
    start = (size[0] + 15) // 16 * 16
    two_ids = [
        lax.dynamic_slice(news, (i // group, 0, lax.rem(i, group), 0), (1, seq, 1, local)).reshape(length) for i in chosen
    ]
    ids = lax.dynamic_update_slice(jnp.pad(two_ids[0], (0, rows - length)), two_ids[1], (start,))
    line = jnp.arange(rows, dtype=jnp.int32)
    in_first, in_second = line < size[0], (line >= start) & (line < start + size[1])
    used = in_first | in_second
    spots = jnp.where(in_first, line, jnp.where(in_second, line - start, -1))
    total = jnp.where(size[1] > 0, start + size[1], size[0])
    core = lax.rem(lax.axis_index("seq"), 2)
    plan = jnp.stack([size[0], size[1], start, jnp.clip((total + ROWS - 1) // ROWS, 2, BLOCKS), core])
    owner, place, first, rank = route(ids, used, per_owner)
    most = jnp.max(jnp.where(used, rank + 1, 0))
    asked = requests(owner, place, first, rank, 0, devices).reshape(devices, room)
    note = jnp.broadcast_to(most, (devices, 1))
    got = exchange(jnp.concatenate([asked, note, jnp.zeros((devices, 127 - room), jnp.int32)], axis=1))
    rounds = (jnp.max(got[:, room]) + room - 1) // room

    table = embed.astype(bf)
    slots = token_slots(owner, used, rank, 0, room)
    wanted_first = got[:, :room].reshape(-1)

    def pick(wanted):
        picked = mm(one_hot(wanted, per_owner), table).astype(bf).reshape(devices, room, width)
        return exchange(picked).reshape(devices * room, width)

    back = pick(wanted_first)

    def ask_again(start):
        return exchange(requests(owner, place, first, rank, start, devices).reshape(devices, room)).reshape(-1)

    def more(state):
        step, total = state
        start = step * room
        there = one_hot(token_slots(owner, used, rank, start, room), devices * room)
        return step + 1, total + mm(there, pick(ask_again(start))).astype(bf)

    _, extra = lax.while_loop(lambda state: state[0] < rounds, more, (jnp.int32(1), jnp.zeros((rows, width), bf)))

    all_gold = exchange(jnp.broadcast_to(gold[None], (devices, pairs_here))).reshape(devices // seq, seq, pairs_here)[:, 0]
    all_gold = all_gold.reshape(devices)
    holders, facts = [], []
    for i in chosen:
        other, pair = i ^ 1, i // 2
        rank = take(order, other)
        holders.append(jnp.where(rank < devices, 2 * rank, 2 * (2 * devices - 1 - rank) + 1))
        weight = take(lab, pair).astype(f32)
        own = jnp.where(lax.rem(i, 2) == 0, weight, 0.0)
        facts += [weight, take(all_gold, pair), take(lens, i).astype(f32), take(lens, other).astype(f32), own]
    meet = jnp.stack(holders), jnp.stack(facts + [count])

    staged = (seq, devices) == (4, 32) and depth == 24
    loss, dense_out, dense_in, rest, d_xb, give_rows = run_forward_backward(
        full, back, extra, slots, spots, plan, meet, staged, devices, depth, length, hidden
    )

    give_rows = exchange(give_rows.reshape(devices, room, width))
    if staged:
        z, y, x = place_in_slice()
        dense_in = halve(dense_in[0], y, 4), halve(dense_in[1], x, 2)
        dense_out = total_of(dense_out).astype(bf)
        dense_out = spot(dense_out, 0, x), swap(spot(dense_out, 0, 1 - x), 2, 32)
        rest = halve(over_cores(*rest[:2]), x, 2), halve(over_cores(*rest[2:]), y, 4)
        dense_in, give_rows = lax.optimization_barrier((dense_in, give_rows))
        dense_in = over_long_both(*dense_in, z)
        dense_out = halve(dense_out, y, 4)
        rest = halve(rest[0], y, 4), halve(rest[1], x, 2)
        dense_in, dense_out, rest = lax.optimization_barrier((dense_in, dense_out, rest))
        rest = over_long_both(*rest, z)
        dense_out, dense_in, rest = total_of(dense_out), total_of(dense_in), total_of(rest)
    else:
        sum_up = lambda parts: lax.psum_scatter(parts, AXES, scatter_dimension=0, tiled=True).astype(f32)
        kinds = lambda v: v.reshape(depth, -1, width).transpose(1, 0, 2)
        dense_out, dense_in, rest = sum_up(dense_out).reshape(turns, depth, width), kinds(sum_up(dense_in)), kinds(sum_up(rest))
    g_position = rest[3, :, :length].T
    g_vectors = rest[3, :, length : length + nvec].T

    def give(wanted, there):
        return mm_left(one_hot(wanted, per_owner), there.reshape(devices * room, width))

    def more_back(state):
        step, total = state
        start = step * room
        sums = mm_left(one_hot(token_slots(owner, used, rank, start, room), devices * room), d_xb).astype(bf)
        return step + 1, total + give(ask_again(start), exchange(sums.reshape(devices, room, width)))

    _, g_embed = lax.while_loop(lambda state: state[0] < rounds, more_back, (jnp.int32(1), give(wanted_first, give_rows)))

    squares = sum(jnp.sum(g * g) for g in (g_embed, dense_out, dense_in, rest))
    sums = exchange(jnp.broadcast_to(jnp.stack([squares, loss])[None, :], (devices, 2)))
    sums = jnp.sum(sums, axis=0)
    norm = jnp.sqrt(sums[0])
    loss_sum = sums[1]
    scale = jnp.minimum(1.0, CLIP / (norm + 1e-06))
    state = (
        embed, position, attn_in, attn_out, ff_in, ff_out, vectors,
        mom_embed, mom_position, mom_attn_in, mom_attn_out, mom_ff_in, mom_ff_out, mom_vectors,
        avg_embed, avg_position, avg_attn_in, avg_attn_out, avg_ff_in, avg_ff_out, avg_vectors,
    )
    steps = next(n for n in (8, 5, 4, 3, 2, 1) if per_owner % (8 * n) == 0 or n == 1)
    strip = pl.BlockSpec((per_owner // steps, width), lambda i, *_: (i, 0))
    whole = lambda v: strip if v.shape == embed.shape else fixed(v.shape, (0,) * v.ndim)
    whole_out = lambda v: strip if v.shape == embed.shape else pl.BlockSpec(v.shape, lambda *_: (0,) * v.ndim)
    inputs = (g_embed, dense_out, dense_in, rest, g_position, g_vectors) + state
    done = pl.pallas_call(
        functools.partial(update_kernel, turns),
        grid_spec=pltpu.PrefetchScalarGridSpec(
            num_scalar_prefetch=1, grid=(steps,), in_specs=[whole(v) for v in inputs], out_specs=[whole_out(v) for v in state]
        ),
        out_shape=[jax.ShapeDtypeStruct(v.shape, f32) for v in state],
        compiler_params=params(60),
        name="update",
    )(scale[None], *inputs)
    return (loss_sum, count, norm, *done)


def solution(mesh):
    whole = (
        P(AXES, None),
        P(None, AXES),
        P(AXES, None),
        P(AXES, None),
        P(AXES, None),
        P(AXES, None),
        P(None, AXES),
    )
    return jax.shard_map(
        body,
        mesh=mesh,
        in_specs=(P("dp", None, "seq"), P("dp", None), P("dp"), P("dp")) + whole * 3,
        out_specs=(P(), P(), P()) + whole * 3,
        check_vma=False,
    )
```

```python
import functools

import jax
import jax.numpy as jnp
from jax import lax
from jax.experimental import pallas as pl
from jax.experimental.pallas import tpu as pltpu
from jax.sharding import PartitionSpec as P

HEADS = 12
HEAD_DIM = 64
EPS = 1e-06
RATE = 10000.0
MOMENT = 0.5
DECAY = 0.5
CLIP = 0.01
SLOTS = 1024
GROUP = 128
ROWS = 288
BLOCKS = 4
TIMES = dict(first=10, attend=12, middle=24, back=20, out_grads=9, in_grads=11, attend_back=11, last=12, rest_grads=6, query_key_grads=6)
PACE = 1e+06
SIZES = (128, 256, 384, 512)
AXES = ("dp", "seq")
bf = jnp.bfloat16
f32 = jnp.float32


def mm(left, right):
    return jnp.dot(left, right, preferred_element_type=f32)


def mm_left(left, right):
    return lax.dot_general(left, right, (((0,), (0,)), ((), ())), preferred_element_type=f32)


def mm_right(left, right):
    return lax.dot_general(left, right, (((1,), (1,)), ((), ())), preferred_element_type=f32)


def exchange(v):
    return lax.all_to_all(v, AXES, 0, 0, tiled=True)


def slots_of(devices):
    return max(16, SLOTS // devices)


def route(ids, valid, per_owner):
    count = ids.shape[0]
    spot = jnp.arange(count, dtype=jnp.int32)
    owner = ids // per_owner
    local = ids - owner * per_owner
    key = jnp.where(valid, ids, -1 - spot)
    alike = key[:, None] == key[None, :]
    first_at = jnp.min(jnp.where(alike, spot[None, :], count), axis=1)
    first = (first_at == spot) & valid
    before = (owner[:, None] == owner[None, :]) & first[None, :] & (spot[None, :] < first_at[:, None])
    rank = jnp.sum(before.astype(jnp.int32), axis=1)
    return owner, local, first, rank


def requests(owner, local, first, rank, start, devices):
    room = slots_of(devices)
    slot = jnp.where(first & (rank >= start) & (rank < start + room), owner * room + rank - start, -1)
    line = jnp.arange(devices * room, dtype=jnp.int32)
    hit = slot[None, :] == line[:, None]
    return jnp.max(jnp.where(hit, local[None, :], -1), axis=1)


def token_slots(owner, valid, rank, start, room):
    return jnp.where(valid & (rank >= start) & (rank < start + room), owner * room + rank - start, -1)


def one_hot(index, size):
    return (index[:, None] == jnp.arange(size, dtype=jnp.int32)[None, :]).astype(bf)


NEAR = 0.3
TAIL = (
    0.11962924781130464, 0.12075473126046088, 0.09990870957740686, 0.12857719637511858,
    -0.05371263258867769, 0.2063844888355699, -0.15722075016774184, 0.03567893567949022,
)


def dot(left, right):
    return jnp.dot(left, right, preferred_element_type=f32)


def dot_nt(left, right):
    return lax.dot_general(left, right, (((1,), (1,)), ((), ())), preferred_element_type=f32)


def dot_tn(left, right):
    return lax.dot_general(left, right, (((0,), (0,)), ((), ())), preferred_element_type=f32)


def iota(shape, axis):
    return lax.broadcasted_iota(jnp.int32, shape, axis)


def normal(v):
    center = v - jnp.mean(v, axis=-1, keepdims=True)
    scale = lax.rsqrt(jnp.mean(center * center, axis=-1, keepdims=True) + EPS)
    return center * scale, scale


def normal_back(grad, unit, scale):
    inner = jnp.mean(grad * unit, axis=-1, keepdims=True)
    return scale * (grad - jnp.mean(grad, axis=-1, keepdims=True) - unit * inner)


def column_sums(v):
    return dot(jnp.full((8, v.shape[0]), 1.0, bf), v)[:1]


def gelu_pair(v):
    bell = jnp.exp(v * v * -0.5)
    t = 1.0 / (1.0 + NEAR * jnp.abs(v))
    poly = TAIL[-1]
    for c in TAIL[-2::-1]:
        poly = poly * t + c
    tail = poly * t * bell
    area = jnp.where(v < 0, tail, 1.0 - tail)
    return v * area, area + v * bell * 0.3989422804014327


def params(limit, **more):
    return pltpu.CompilerParams(vmem_limit_bytes=limit << 20, **more)


def fixed(shape, index):
    return pl.BlockSpec(shape, lambda *_: index, pipeline_mode=pl.Buffered(1))


def spread(staged, depth, turns, src, out):
    width = out.shape[1]
    if not staged:
        out[...] = src[...]
        return

    def pair(index, carry):
        tall = src[pl.ds(pl.multiple_of(index * 2 * depth, 16), 2 * depth), :].astype(f32)
        parts = []
        for e in range(2):
            for j in range(turns):
                parts.append(tall[e * depth : (e + 1) * depth, j * width : (j + 1) * width])
        to = pl.multiple_of(index * 2 * depth * turns, 16)
        out[pl.ds(to, 2 * depth * turns), :] = jnp.concatenate(parts, axis=0).astype(bf)
        return carry

    lax.fori_loop(0, src.shape[0] // (2 * depth), pair, 0)


def live_rows(plan, shape):
    row = iota(shape, 0) + pl.program_id(0) * shape[0]
    return row < plan[0], (row >= plan[2]) & (row < plan[2] + plan[1])


def when_live(kernel):
    def run(*refs):
        pl.when(pl.program_id(0) < refs[0][3])(lambda: kernel(*refs))

    return run


def first_kernel(plan, slot, spot_in, back, extra, w_qkv, pos_t, vec_t, x_out, hin_out, qkv_out, vec_out):
    rows, width = x_out.shape
    length = pos_t.shape[1]
    vec = dot_nt((iota((16, 128), 0) == iota((16, 128), 1)).astype(f32).astype(bf), vec_t[...])
    vec_out[...] = vec
    where = jnp.where(slot[...] == iota((rows, back.shape[0]), 1), 1.0, 0.0).astype(bf)
    line = jnp.where(spot_in[...] == iota((rows, length), 1), 1.0, 0.0).astype(bf)
    x = dot(where, back[...]) + extra[...].astype(f32) + dot_nt(line, pos_t[...])
    x_out[...] = x
    unit, _ = normal(x)
    hin = (unit * vec[0:1] + vec[1:2]).astype(bf)
    hin_out[...] = hin
    qkv_out[:, :width] = (dot(hin, w_qkv[:, :width]) + vec[2:3]).astype(bf)
    qkv_out[:, width : 2 * width] = dot(hin, w_qkv[:, width : 2 * width]).astype(bf)
    qkv_out[:, 2 * width :] = (dot(hin, w_qkv[:, 2 * width :]) + vec[3:4]).astype(bf)


def head_parts(size, query, keys, half):
    shape = query.shape
    lane = iota(shape, 1)
    live = iota(shape, 0) < size
    inside = ((lane // HEAD_DIM) == half) & live
    spare = lane == (1 - half) * HEAD_DIM
    key = jnp.where(inside, keys.astype(f32), jnp.where(spare & ~live, -1e30, 0.0)).astype(bf)
    ask = jnp.where(inside, query.astype(f32) * 0.125, jnp.where(spare, 1.0, 0.0)).astype(bf)
    return inside, ask, key


def each_sentence(plan, run):
    def one(index, carry):
        size = jnp.where(index == 0, plan[0], plan[1])
        start = pl.multiple_of(jnp.where(index == 0, 0, plan[2]), 16)
        under = 0
        for count in SIZES:
            pl.when((size > under) & (size <= count))(functools.partial(run, pl.ds(start, count), size))
            under = count
        return carry

    lax.fori_loop(0, 2, one, 0)


def attend_kernel(plan, query, keys, values, out):
    out[...] = jnp.zeros_like(out)

    def run(rows, size):
        total = None
        for half in range(2):
            inside, ask, key = head_parts(size, query[rows, :], keys[rows, :], half)
            score = dot_nt(ask, key)
            power = jnp.exp(score - jnp.max(score, axis=1, keepdims=True))
            prob = (power * (1.0 / jnp.sum(power, axis=1, keepdims=True))).astype(bf)
            part = dot(prob, jnp.where(inside, values[rows, :].astype(f32), 0.0).astype(bf))
            total = part if total is None else total + part
        out[rows, :] = total.astype(bf)

    each_sentence(plan, run)


def attend_back_kernel(plan, query, keys, values, d_out, *more):
    d_proj = more[-1]
    d_proj[...] = jnp.zeros_like(d_proj)
    plus = lambda a, b: b if a is None else a + b

    def run(rows, size):
        d_query, d_key, d_value = None, None, None
        for half in range(2):
            inside, ask, key = head_parts(size, query[rows, :], keys[rows, :], half)
            clean = lambda v: jnp.where(inside, v.astype(f32), 0.0).astype(bf)
            score = dot_nt(key, ask)
            power = jnp.exp(score - jnp.max(score, axis=0, keepdims=True))
            prob = power * (1.0 / jnp.sum(power, axis=0, keepdims=True))
            grad = clean(d_out[rows, :])
            d_value = plus(d_value, dot(prob.astype(bf), grad))
            d_prob = dot_nt(clean(values[rows, :]), grad)
            inner = jnp.sum(prob * d_prob, axis=0, keepdims=True)
            d_score = (prob * (d_prob - inner)).astype(bf)
            d_key = plus(d_key, dot(d_score, clean(ask)))
            d_query = plus(d_query, dot_tn(d_score, clean(key)))
        d_proj[0, rows, :] = (d_query * 0.125).astype(bf)
        d_proj[1, rows, :] = d_key.astype(bf)
        d_proj[2, rows, :] = d_value.astype(bf)

    each_sentence(plan, run)


def middle_kernel(staged, depth, turns, plan, x, mixed, w_out, w_in, w_src, vec, vec_ff, z1_out, h1_out, act_out, slope_out, z2_out, pooled, w_back):
    rows, width = x.shape
    pl.when(pl.program_id(0) == 0)(lambda: spread(staged, depth, turns, w_src, w_back))
    unit, _ = normal(x[...])
    h0 = unit * vec[0:1] + vec[1:2]
    z1 = h0 + dot(mixed[...], w_out[...]) + vec[4:5]
    z1_out[...] = z1
    unit, _ = normal(z1)
    h1 = unit * vec[5:6] + vec[6:7]
    h1_b = h1.astype(bf)
    h1_out[...] = h1_b
    y = None
    for j in range(turns):
        at = slice(j * width, (j + 1) * width)
        hidden = dot(h1_b, w_in[:, at]) + vec_ff[:, at]
        act, slope = gelu_pair(hidden)
        act = act.astype(bf)
        act_out[:, at] = act
        slope_out[:, at] = slope.astype(bf)
        part = dot(act, w_back[at, :])
        y = part if y is None else y + part
    z2 = h1 + y + vec[7 + turns : 8 + turns]
    z2_out[...] = z2
    unit, _ = normal(z2)
    h2 = unit * vec[8 + turns : 9 + turns] + vec[9 + turns : 10 + turns]
    sums = [jnp.sum(jnp.where(keep, h2, 0.0), axis=0, keepdims=True) for keep in live_rows(plan, (rows, width))]

    @pl.when(pl.program_id(0) == 0)
    def _():
        pooled[...] = jnp.zeros_like(pooled)

    line = iota(pooled.shape, 0)
    pooled[...] += jnp.where(line == 0, sums[0], jnp.where(line == 1, sums[1], 0.0))


def back_kernel(plan, facts, holders, pooled, all_pooled, z1, slope, z2, w_out, w_in, w_back, vec, d_y_out, d_f_out, d_r1_out, d_a_out, d_o_out, sums, sums_ff, loss):
    rows, width = z1.shape
    step = pl.program_id(0)
    total = lambda a, b: jnp.sum(a * b, axis=1, keepdims=True)
    count = facts[10]
    grads, losses = [], []
    for i in range(2):
        labeled, gold, size, other_size, counts = (facts[5 * i + j] for j in range(5))
        own, other = pooled[i : i + 1] / size, all_pooled[pl.ds(holders[i], 1), :] / other_size
        cross = total(own, other)
        root, other_root = lax.rsqrt(total(own, own) + EPS), lax.rsqrt(total(other, other) + EPS)
        miss = cross * root * other_root - gold
        losses.append(counts * miss * miss)
        push = 2.0 * labeled * miss / count
        grads.append(push * (other * root * other_root - cross * root * root * root * other_root * own) / size)
    loss[...] = jnp.broadcast_to(losses[0] + losses[1], loss.shape)
    keep = live_rows(plan, (rows, width))
    d_h2 = jnp.where(keep[0], grads[0], jnp.where(keep[1], grads[1], 0.0))
    turns = w_in.shape[1] // width

    unit, scale = normal(z2[...])
    d_g2 = jnp.sum(d_h2 * unit, axis=0, keepdims=True)
    d_b2n = jnp.sum(d_h2, axis=0, keepdims=True)
    d_r2 = normal_back(d_h2 * vec[8 + turns : 9 + turns], unit, scale)
    d_y = d_r2.astype(bf)
    d_y_out[...] = d_y
    d_h1 = d_r2
    ff = []
    for j in range(turns):
        at = slice(j * width, (j + 1) * width)
        d_f = (dot_nt(d_y, w_back[at, :]) * slope[:, at].astype(f32)).astype(bf)
        d_f_out[:, at] = d_f
        ff.append(column_sums(d_f))
        d_h1 = d_h1 + dot_nt(d_f, w_in[:, at])
    unit, scale = normal(z1[...])
    d_g1 = jnp.sum(d_h1 * unit, axis=0, keepdims=True)
    d_b1 = jnp.sum(d_h1, axis=0, keepdims=True)
    d_r1 = normal_back(d_h1 * vec[5:6], unit, scale)
    d_r1_out[...] = d_r1
    d_a = d_r1.astype(bf)
    d_a_out[...] = d_a
    d_o_out[...] = dot_nt(d_a, w_out[...]).astype(bf)
    fresh = jnp.concatenate([column_sums(d_a), d_g1, d_b1, column_sums(d_y), d_g2, d_b2n, d_g2, d_b2n], axis=0)

    @pl.when(step == 0)
    def _():
        sums[...] = jnp.zeros_like(sums)
        sums_ff[...] = jnp.zeros_like(sums_ff)

    sums[...] += fresh
    sums_ff[...] += jnp.concatenate(ff, axis=0)


def last_kernel(plan, slot, x, d_r1, d_proj, w_qkv, vec, d_x_out, sums, rows_out, total):
    rows, width = x.shape
    step = pl.program_id(0)
    d_h0 = d_r1[...]
    for i in range(3):
        d_h0 = d_h0 + dot_nt(d_proj[i], w_qkv[:, i * width : (i + 1) * width])
    unit, scale = normal(x[...])
    d_ge = jnp.sum(d_h0 * unit, axis=0, keepdims=True)
    d_be = jnp.sum(d_h0, axis=0, keepdims=True)
    d_x = normal_back(d_h0 * vec[0:1], unit, scale)
    d_xb = d_x.astype(bf)
    d_x_out[...] = d_xb
    bias_q, bias_v = column_sums(d_proj[0]), column_sums(d_proj[2])
    fresh = jnp.concatenate([d_ge, d_be, bias_q, bias_v, d_ge, d_be, bias_q, bias_v], axis=0)
    hit = jnp.where(slot[...] == iota((rows, rows_out.shape[0]), 1), 1.0, 0.0).astype(bf)

    @pl.when(step == 0)
    def _():
        sums[...] = jnp.zeros_like(sums)
        total[...] = jnp.zeros_like(total)

    sums[...] += fresh
    total[...] += dot_tn(hit, d_xb)

    @pl.when(step == plan[3] - 1)
    def _():
        rows_out[...] = total[...].astype(bf)


def blocks(v, depth):
    return v.reshape(v.shape[0] // depth, depth, v.shape[1])


def put_split(outs, order, kind, g, mine):
    keep, send = outs
    for z in range(2):
        for y in range(2):
            for x in range(2):
                owner = 2 * (4 * z + 2 * y + x)
                at = tuple({"z": z, "y": y, "x": x}[axis] for axis in order) + (kind,)
                even, odd = g[owner], g[owner + 1]
                keep[at] = jnp.where(mine == 0, even, odd).astype(bf)
                send[at] = jnp.where(mine == 0, odd, even).astype(bf)


def by_blocks(plan, run):
    for count in range(2, BLOCKS + 1):
        pl.when(plan[3] == count)(functools.partial(run, count * ROWS))


def out_grads_kernel(depth, turns, plan, act, d_y, h1, d_f, *outs):
    width = d_y.shape[1]

    def run(rows):
        g = dot_tn(act[:rows], d_y[:rows])
        g = g.reshape(16, turns, depth, width)
        for j in range(turns):
            put_split(outs, "xyz", j, g[:, j], plan[4])
        for j in range(turns // 2):
            put_split(outs, "xyz", turns + j, blocks(dot_tn(h1[:rows], d_f[:rows, j * width : (j + 1) * width]), depth), plan[4])

    by_blocks(plan, run)


def in_grads_kernel(depth, turns, plan, h1, d_f, mixed, d_a, *outs):
    width = d_a.shape[1]

    def run(rows):
        for j in range(turns // 2):
            put_split(outs, "yxz", j, blocks(dot_tn(h1[:rows], d_f[:rows, j * width : (j + 1) * width]), depth), plan[4])
        put_split(outs, "yxz", turns // 2, blocks(dot_tn(mixed[:rows], d_a[:rows]), depth), plan[4])

    by_blocks(plan, run)


def query_key_grads_kernel(depth, plan, hin, d_proj, *outs):
    def run(rows):
        for i in range(2):
            put_split(outs, "xyz", i, blocks(dot_tn(hin[:rows], d_proj[i, :rows]), depth), plan[4])

    by_blocks(plan, run)


def rest_grads_kernel(depth, length, plan, spot_in, hin, d_value, d_x, sums_0, sums, sums_ff, *outs):
    width = d_value.shape[2]
    part = hin.shape[1]

    def run(rows):
        put_split(outs, "yxz", 0, blocks(dot_tn(hin[:rows], d_value[0, :rows]), depth), plan[4])
        line = jnp.where(spot_in[:rows] == iota((rows, length), 1), 1.0, 0.0).astype(bf)
        g_pos = dot_tn(d_x[:rows], line)
        vec = jnp.concatenate([sums_0[:4], sums[:3], sums_ff[...], sums[3:6]], axis=0)
        vec = jnp.concatenate([vec, jnp.zeros((128 - vec.shape[0], part), f32)], axis=0)
        both = jnp.concatenate([g_pos, vec.T, jnp.zeros((part, width - length - 128), f32)], axis=1)
        put_split(outs, "yxz", 1, blocks(both, depth), plan[4])

    by_blocks(plan, run)


def update_kernel(turns, scale, g_embed, dense_out, dense_in, rest, g_position, g_vectors, *refs):
    factor = scale[0]
    weights, moms, avgs, news, next_moms, next_avgs = (refs[7 * i : 7 * i + 7] for i in range(6))

    def one(index, at, grad):
        clipped = grad * factor
        moment = MOMENT * moms[index][at] + clipped
        fresh = weights[index][at] - RATE * (clipped + MOMENT * moment)
        next_moms[index][at] = moment
        news[index][at] = fresh
        next_avgs[index][at] = DECAY * avgs[index][at] + (1.0 - DECAY) * fresh

    every = (slice(None), slice(None))
    one(0, every, g_embed[...])

    @pl.when(pl.program_id(0) == 0)
    def _():
        depth, width = rest.shape[1:]
        cols = lambda j: (slice(None), slice(j * width, (j + 1) * width))
        one(1, every, g_position[...])
        for j in range(3):
            one(2, cols(j), rest[j])
        one(3, every, dense_in[turns])
        for j in range(turns):
            one(4, cols(j), dense_in[j])
            one(5, (slice(j * depth, (j + 1) * depth), slice(None)), dense_out[j])
        one(6, every, g_vectors[...])


def cost(micros):
    return pl.CostEstimate(flops=0, bytes_accessed=int(micros * PACE), transcendentals=0)


def run_forward_backward(full, back, extra, slots, spots, plan, meet, staged, devices, depth, length, hidden):
    width = back.shape[1]
    rows = slots.shape[0]
    turns = hidden // width
    pairs = width // GROUP
    shape = jax.ShapeDtypeStruct
    at_row = lambda i, plan: jnp.minimum(i, plan[3] - 1)
    row = lambda cols: pl.BlockSpec((ROWS, cols), lambda i, plan, *_: (at_row(i, plan), 0))
    column = lambda block: fixed((width, width), (0, block))
    at_back = 4 * width + hidden
    whole_out = lambda *dims: pl.BlockSpec(dims, lambda *_: (0,) * len(dims))

    def call(kernel, prefetch, grid, in_specs, out_specs, out_shape, name, scratch=(), **more):
        return pl.pallas_call(
            kernel,
            grid_spec=pltpu.PrefetchScalarGridSpec(
                num_scalar_prefetch=prefetch, grid=grid, in_specs=in_specs, out_specs=out_specs, scratch_shapes=list(scratch)
            ),
            out_shape=out_shape,
            compiler_params=params(60),
            cost_estimate=cost(TIMES[name]),
            name=name,
            **more,
        )

    w_src, w_src_spec = full, fixed((width, turns * width), (0, at_back // (turns * width)))
    if not staged:
        w_src = full[:, at_back : at_back + turns * width].reshape(devices, depth, turns, width)
        w_src, w_src_spec = w_src.transpose(0, 2, 1, 3).reshape(hidden, width), fixed((hidden, width), (0, 0))

    at_pos = at_back + turns * width
    at_vec = at_pos + length
    w_qkv_spec = fixed((width, 3 * width), (0, 0))
    w_out_spec = column(3)
    w_in_spec = fixed((width, hidden), (0, 4 * width // hidden))
    w_back_spec = fixed((hidden, width), (0, 0))
    vec_spec = fixed((16, width), (0, 0))

    x, hin, qkv, vec = call(
        when_live(first_kernel), 1, (BLOCKS,),
        [
            row(1), row(1), fixed(back.shape, (0, 0)), row(width), w_qkv_spec,
            fixed((width, length), (0, at_pos // length)), fixed((width, 128), (0, at_vec // 128)),
        ],
        [row(width), row(width), row(3 * width), whole_out(16, width)],
        [shape((rows, width), f32), shape((rows, width), bf), shape((rows, 3 * width), bf), shape((16, width), f32)],
        "first",
    )(plan, slots[:, None], spots[:, None], back, extra, full, full, full)

    block = lambda part, start=0: pl.BlockSpec((rows, GROUP), lambda p, *_: (0, part * pairs + start + p))
    mixed = call(
        attend_kernel, 1, (pairs,), [block(0), block(1), block(2)], block(0), shape((rows, width), bf), "attend"
    )(plan, qkv, qkv, qkv)

    vec_ff = vec[7 : 7 + turns].reshape(1, hidden)
    z1, h1, act, slope, z2, pooled, w_back = call(
        when_live(functools.partial(middle_kernel, staged, depth, turns)), 1, (BLOCKS,),
        [row(width), row(width), w_out_spec, w_in_spec, w_src_spec, vec_spec, fixed((1, hidden), (0, 0))],
        [row(width), row(width), row(hidden), row(hidden), row(width), whole_out(8, width), whole_out(hidden, width)],
        [
            shape((rows, width), f32), shape((rows, width), bf), shape((rows, hidden), bf), shape((rows, hidden), bf),
            shape((rows, width), f32), shape((8, width), f32), shape((hidden, width), bf),
        ],
        "middle",
    )(plan, x, mixed, full, full, w_src, vec, vec_ff)

    all_pooled = exchange(jnp.broadcast_to(pooled[None, :2], (devices, 2, width))).reshape(2 * devices, width)
    holders, facts = meet
    d_y, d_f, d_r1, d_a, d_o, sums, sums_ff, loss = call(
        when_live(back_kernel), 3, (BLOCKS,),
        [
            fixed((8, width), (0, 0)), fixed((2 * devices, width), (0, 0)), row(width), row(hidden), row(width), w_out_spec, w_in_spec,
            w_back_spec, vec_spec,
        ],
        [
            row(width), row(hidden), row(width), row(width), row(width), whole_out(8, width), whole_out(turns, width),
            whole_out(8, 128),
        ],
        [
            shape((rows, width), bf), shape((rows, hidden), bf), shape((rows, width), f32), shape((rows, width), bf), shape((rows, width), bf),
            shape((8, width), f32), shape((turns, width), f32), shape((8, 128), f32),
        ],
        "back",
    )(plan, facts, holders, pooled, all_pooled, z1, slope, z2, full, full, w_back, vec)

    part = width // 2
    halves = lambda cols: pl.BlockSpec((rows, cols), lambda i, *_: (0, i))
    live = (jnp.arange(rows) < plan[3] * ROWS)[:, None]
    clean = lambda v: jnp.where(live, v, 0)

    def split_call(kernel, in_specs, streams, name):
        specs, shapes = [], []
        for order, kinds in streams:
            at = order.index("z")
            dims = tuple(4 if axis == "z" else 2 for axis in order) + (kinds, depth, width)
            index = lambda i, *_, at=at: tuple(i if axis == at else 0 for axis in range(6))
            specs += [pl.BlockSpec((2, 2, 2, kinds, depth, width), index)] * 2
            shapes += [shape(dims, bf)] * 2
        return call(kernel, 1, (2,), in_specs, specs, shapes, name)

    if staged:
        z, y, x_at = place_in_slice()
        dense_out = split_call(
            functools.partial(out_grads_kernel, depth, turns),
            [halves(hidden // 2), fixed((rows, width), (0, 0)), halves(part), fixed((rows, hidden // 2), (0, 0))],
            [("xyz", turns + turns // 2)],
            "out_grads",
        )(plan, act, d_y, h1, d_f)
        dense_out = over_cores(*dense_out)
        dense_in = split_call(
            functools.partial(in_grads_kernel, depth, turns),
            [halves(part), fixed((rows, hidden // 2), (0, 1)), halves(part), fixed((rows, width), (0, 0))],
            [("yxz", turns // 2 + 1)],
            "in_grads",
        )(plan, h1, d_f, mixed, d_a)
        d_o, dense_out, dense_in = lax.optimization_barrier((d_o, dense_out, dense_in))
        dense_in = over_cores(*dense_in)
        dense_out = halve(dense_out, x_at, 2)
    else:
        dense_out = dot_tn(clean(act), clean(d_y)).astype(bf)
        dense_in = jnp.concatenate([dot_tn(clean(h1), clean(d_f)), dot_tn(clean(mixed), clean(d_a))], axis=1).astype(bf)

    def attend_back(start, count, total):
        more = () if total is None else (total,)
        return call(
            attend_back_kernel, 1, (count,),
            [block(0, start), block(1, start), block(2, start), block(0, start)] + [pl.BlockSpec(memory_space=pl.ANY)] * len(more),
            pl.BlockSpec((3, rows, GROUP), lambda p, *_: (0, 0, start + p)),
            shape((3, rows, width), bf),
            "attend_back",
            input_output_aliases={5: 0} if more else {},
        )(plan, qkv, qkv, qkv, d_o, *more)

    d_proj = attend_back(0, pairs, None)
    if staged:
        d_proj, dense_in = lax.optimization_barrier((d_proj, dense_in))
        in_sums = two_sums(dense_in, y)
        d_proj, in_sums = lax.optimization_barrier((d_proj, in_sums))
        dense_in = in_sums[0], swap(in_sums[1], 4, 32)
    if staged:
        first_rest = split_call(
            functools.partial(query_key_grads_kernel, depth),
            [halves(part), pl.BlockSpec((2, rows, width), lambda i, *_: (0, 0, 0), pipeline_mode=pl.Buffered(1))],
            [("xyz", 2)],
            "query_key_grads",
        )(plan, hin, d_proj)
        d_proj, dense_out, first_rest = lax.optimization_barrier((d_proj, dense_out, first_rest))
        first_rest = over_cores(*first_rest)

    d_xb, sums_0, give_rows = call(
        when_live(last_kernel), 1, (BLOCKS,),
        [
            row(1), row(width), row(width), pl.BlockSpec((3, ROWS, width), lambda i, plan: (0, at_row(i, plan), 0)), w_qkv_spec, vec_spec,
        ],
        [row(width), whole_out(8, width), whole_out(*back.shape)],
        [shape((rows, width), bf), shape((8, width), f32), shape(back.shape, bf)],
        "last",
        scratch=[pltpu.VMEM(back.shape, f32)],
    )(plan, slots[:, None], x, d_r1, d_proj, full, vec)

    if staged:
        give_rows, dense_in = lax.optimization_barrier((give_rows, dense_in))
        out_sums, in_sums = two_sums(dense_out, y), two_sums(dense_in, x_at)
        d_xb, out_sums, in_sums = lax.optimization_barrier((d_xb, out_sums, in_sums))
        dense_out = out_sums[0], swap(out_sums[1], 4, 32)
        dense_in = in_sums[0], swap(in_sums[1], 2, 32)
        cols = lambda count: pl.BlockSpec((count, part), lambda i, *_: (0, i))
        rest = split_call(
            functools.partial(rest_grads_kernel, depth, length),
            [
                fixed((rows, 1), (0, 0)), halves(part), pl.BlockSpec((1, rows, width), lambda i, *_: (2, 0, 0), pipeline_mode=pl.Buffered(1)),
                halves(part), cols(8), cols(8), cols(turns),
            ],
            [("yxz", 2)],
            "rest_grads",
        )(plan, spots[:, None], hin, d_proj, d_xb, sums_0, sums, sums_ff)
        rest = first_rest, over_cores(*rest)
    else:
        g_vec = jnp.concatenate([sums_0[:4], sums[:3], sums_ff, sums[3:6]], axis=0)
        g_pos = dot_tn(clean(d_xb), one_hot(spots, length))
        spare = jnp.zeros((width, width - length - g_vec.shape[0]), f32)
        rest = [dot_tn(clean(hin), clean(d_proj[i])) for i in range(3)] + [jnp.concatenate([g_pos, g_vec.T, spare], axis=1)]
        rest = jnp.concatenate(rest, axis=1).astype(bf)
    return loss[0, 0], dense_out, dense_in, rest, clean(d_xb), give_rows


def swap(v, bit, devices):
    return lax.ppermute(v, AXES, [(i, i ^ bit) for i in range(devices)])


def add(a, b):
    return (a.astype(f32) + b.astype(f32)).astype(bf)


def spot(v, axis, index):
    return lax.dynamic_index_in_dim(v, index, axis, keepdims=False)


def place_in_slice():
    row = lax.axis_index("dp")
    return row // 2, lax.rem(row, 2), lax.axis_index("seq") // 2


def over_cores(keep, send):
    return keep, swap(send, 1, 32)


def part_sum(pair, index):
    return add(spot(pair[0], 0, index), spot(pair[1], 0, index))


def two_sums(pair, index):
    return part_sum(pair, index), part_sum(pair, 1 - index)


def halve(pair, index, bit):
    return part_sum(pair, index), swap(part_sum(pair, 1 - index), bit, 32)


def over_long(pair, z):
    return [part_sum(pair, z)] + [swap(part_sum(pair, z ^ step), 8 * step, 32) for step in range(1, 4)]


def z_parts(one, two, z):
    return [jnp.concatenate([part_sum(one, z ^ step), part_sum(two, z ^ step)], axis=0) for step in range(4)]


def z_swaps(parts):
    return parts[:1] + [swap(parts[step], 8 * step, 32) for step in range(1, 4)]


def over_long_both(one, two, z):
    part = lambda step: jnp.concatenate([part_sum(one, z ^ step), part_sum(two, z ^ step)], axis=0)
    return [part(0)] + [swap(part(step), 8 * step, 32) for step in range(1, 4)]


def total_of(parts):
    return sum(p.astype(f32) for p in parts)


def body(
    token_ids, lengths, labeled, gold,
    embed, position, attn_in, attn_out, ff_in, ff_out, vectors,
    mom_embed, mom_position, mom_attn_in, mom_attn_out, mom_ff_in, mom_ff_out, mom_vectors,
    avg_embed, avg_position, avg_attn_in, avg_attn_out, avg_ff_in, avg_ff_out, avg_vectors,
):
    pairs_here, _, local = token_ids.shape
    seq = lax.axis_size("seq")
    devices = lax.axis_size("dp") * seq
    length = local * seq
    per_owner, width = embed.shape
    depth = attn_in.shape[0]
    hidden = ff_in.shape[1]
    nvec = vectors.shape[0]
    turns = ff_out.shape[0] // depth
    rows = BLOCKS * ROWS
    room = slots_of(devices)
    spare = 128 - nvec

    shard = jnp.concatenate(
        [attn_in, attn_out, ff_in]
        + [ff_out[i * depth : (i + 1) * depth] for i in range(turns)]
        + [position.T, vectors.T, jnp.zeros((depth, spare), f32)],
        axis=1,
    ).astype(bf)
    full = lax.all_gather(shard, AXES, axis=0, tiled=True)

    group = 2 * pairs_here
    info = jnp.concatenate([lengths.reshape(1, group), labeled.reshape(1, pairs_here)], axis=1)
    info = jnp.pad(info, ((0, 0), (0, local - group - pairs_here)))
    news = jnp.concatenate([token_ids.reshape(group, local), info], axis=0)
    news = exchange(jnp.broadcast_to(news[None], (devices,) + news.shape)).reshape(devices // seq, seq, group + 1, local)
    lens = news[:, 0, group, :group].reshape(2 * devices)
    lab = news[:, 0, group, group : group + pairs_here].reshape(devices)
    live = jnp.where(jnp.repeat(lab, 2) > 0, lens, 0)
    index = jnp.arange(2 * devices, dtype=jnp.int32)
    ahead = (live[None, :] > live[:, None]) | ((live[None, :] == live[:, None]) & (index[None, :] < index[:, None]))
    order = jnp.sum(ahead.astype(jnp.int32), axis=1)
    me = lax.axis_index("dp") * seq + lax.axis_index("seq")
    take = lambda values, i: jnp.sum(jnp.where(index[: values.shape[0]] == i, values, 0))
    chosen = [jnp.sum(jnp.where(order == rank, index, 0)) for rank in (me, 2 * devices - 1 - me)]
    count = jnp.maximum(jnp.sum(lab).astype(f32), 1.0)
    size = [take(live, i) for i in chosen]
    start = (size[0] + 15) // 16 * 16
    two_ids = [
        lax.dynamic_slice(news, (i // group, 0, lax.rem(i, group), 0), (1, seq, 1, local)).reshape(length) for i in chosen
    ]
    ids = lax.dynamic_update_slice(jnp.pad(two_ids[0], (0, rows - length)), two_ids[1], (start,))
    line = jnp.arange(rows, dtype=jnp.int32)
    in_first, in_second = line < size[0], (line >= start) & (line < start + size[1])
    used = in_first | in_second
    spots = jnp.where(in_first, line, jnp.where(in_second, line - start, -1))
    total = jnp.where(size[1] > 0, start + size[1], size[0])
    core = lax.rem(lax.axis_index("seq"), 2)
    plan = jnp.stack([size[0], size[1], start, jnp.clip((total + ROWS - 1) // ROWS, 2, BLOCKS), core])
    owner, place, first, rank = route(ids, used, per_owner)
    most = jnp.max(jnp.where(used, rank + 1, 0))
    asked = requests(owner, place, first, rank, 0, devices).reshape(devices, room)
    note = jnp.broadcast_to(most, (devices, 1))
    got = exchange(jnp.concatenate([asked, note, jnp.zeros((devices, 127 - room), jnp.int32)], axis=1))
    rounds = (jnp.max(got[:, room]) + room - 1) // room

    table = embed.astype(bf)
    slots = token_slots(owner, used, rank, 0, room)
    wanted_first = got[:, :room].reshape(-1)

    def pick(wanted):
        picked = mm(one_hot(wanted, per_owner), table).astype(bf).reshape(devices, room, width)
        return exchange(picked).reshape(devices * room, width)

    back = pick(wanted_first)

    def ask_again(start):
        return exchange(requests(owner, place, first, rank, start, devices).reshape(devices, room)).reshape(-1)

    def more(state):
        step, total = state
        start = step * room
        there = one_hot(token_slots(owner, used, rank, start, room), devices * room)
        return step + 1, total + mm(there, pick(ask_again(start))).astype(bf)

    _, extra = lax.while_loop(lambda state: state[0] < rounds, more, (jnp.int32(1), jnp.zeros((rows, width), bf)))

    all_gold = exchange(jnp.broadcast_to(gold[None], (devices, pairs_here))).reshape(devices // seq, seq, pairs_here)[:, 0]
    all_gold = all_gold.reshape(devices)
    holders, facts = [], []
    for i in chosen:
        other, pair = i ^ 1, i // 2
        rank = take(order, other)
        holders.append(jnp.where(rank < devices, 2 * rank, 2 * (2 * devices - 1 - rank) + 1))
        weight = take(lab, pair).astype(f32)
        own = jnp.where(lax.rem(i, 2) == 0, weight, 0.0)
        facts += [weight, take(all_gold, pair), take(lens, i).astype(f32), take(lens, other).astype(f32), own]
    meet = jnp.stack(holders), jnp.stack(facts + [count])

    staged = (seq, devices) == (4, 32) and depth == 24
    loss, dense_out, dense_in, rest, d_xb, give_rows = run_forward_backward(
        full, back, extra, slots, spots, plan, meet, staged, devices, depth, length, hidden
    )

    give_rows = exchange(give_rows.reshape(devices, room, width))
    if staged:
        z, y, x = place_in_slice()
        parts = z_parts(dense_out, dense_in, z)
        parts, rest = lax.optimization_barrier((parts, rest))
        dense = z_swaps(parts)
        rest = halve(rest[0], x, 2), halve(rest[1], y, 4)
        rest = halve(rest[0], y, 4), halve(rest[1], x, 2)
        dense, rest, give_rows = lax.optimization_barrier((dense, rest, give_rows))
        rest = over_long_both(*rest, z)
        dense, rest = total_of(dense), total_of(rest)
        dense_out, dense_in = dense[:turns], dense[turns:]
    else:
        sum_up = lambda parts: lax.psum_scatter(parts, AXES, scatter_dimension=0, tiled=True).astype(f32)
        kinds = lambda v: v.reshape(depth, -1, width).transpose(1, 0, 2)
        dense_out, dense_in, rest = sum_up(dense_out).reshape(turns, depth, width), kinds(sum_up(dense_in)), kinds(sum_up(rest))
    g_position = rest[3, :, :length]
    g_vectors = rest[3, :, length : length + nvec].T

    def give(wanted, there):
        return mm_left(one_hot(wanted, per_owner), there.reshape(devices * room, width))

    def more_back(state):
        step, total = state
        start = step * room
        sums = mm_left(one_hot(token_slots(owner, used, rank, start, room), devices * room), d_xb).astype(bf)
        return step + 1, total + give(ask_again(start), exchange(sums.reshape(devices, room, width)))

    _, g_embed = lax.while_loop(lambda state: state[0] < rounds, more_back, (jnp.int32(1), give(wanted_first, give_rows)))

    squares = sum(jnp.sum(g * g) for g in (g_embed, dense_out, dense_in, rest))
    sums = exchange(jnp.broadcast_to(jnp.stack([squares, loss])[None, :], (devices, 2)))
    sums = jnp.sum(sums, axis=0)
    norm = jnp.sqrt(sums[0])
    loss_sum = sums[1]
    scale = jnp.minimum(1.0, CLIP / (norm + 1e-06))
    state = (
        embed, position.T, attn_in, attn_out, ff_in, ff_out, vectors,
        mom_embed, mom_position.T, mom_attn_in, mom_attn_out, mom_ff_in, mom_ff_out, mom_vectors,
        avg_embed, avg_position.T, avg_attn_in, avg_attn_out, avg_ff_in, avg_ff_out, avg_vectors,
    )
    steps = next(n for n in (8, 5, 4, 3, 2, 1) if per_owner % (8 * n) == 0 or n == 1)
    strip = pl.BlockSpec((per_owner // steps, width), lambda i, *_: (i, 0))
    whole = lambda v: strip if v.shape == embed.shape else fixed(v.shape, (0,) * v.ndim)
    whole_out = lambda v: strip if v.shape == embed.shape else pl.BlockSpec(v.shape, lambda *_: (0,) * v.ndim)
    inputs = (g_embed, dense_out, dense_in, rest, g_position, g_vectors) + state
    done = pl.pallas_call(
        functools.partial(update_kernel, turns),
        grid_spec=pltpu.PrefetchScalarGridSpec(
            num_scalar_prefetch=1, grid=(steps,), in_specs=[whole(v) for v in inputs], out_specs=[whole_out(v) for v in state]
        ),
        out_shape=[jax.ShapeDtypeStruct(v.shape, f32) for v in state],
        compiler_params=params(60),
        name="update",
    )(scale[None], *inputs)
    done = [v.T if i % 7 == 1 else v for i, v in enumerate(done)]
    return (loss_sum, count, norm, *done)


def solution(mesh):
    whole = (
        P(AXES, None),
        P(None, AXES),
        P(AXES, None),
        P(AXES, None),
        P(AXES, None),
        P(AXES, None),
        P(None, AXES),
    )
    return jax.shard_map(
        body,
        mesh=mesh,
        in_specs=(P("dp", None, "seq"), P("dp", None), P("dp"), P("dp")) + whole * 3,
        out_specs=(P(), P(), P()) + whole * 3,
        check_vma=False,
    )
```

```python
import functools

import jax
import jax.numpy as jnp
from jax import lax
from jax.experimental import pallas as pl
from jax.experimental.pallas import tpu as pltpu
from jax.sharding import PartitionSpec as P

HEADS = 12
HEAD_DIM = 64
EPS = 1e-06
RATE = 10000.0
MOMENT = 0.5
DECAY = 0.5
CLIP = 0.01
SLOTS = 1024
GROUP = 128
ROWS = 288
BLOCKS = 4
TIMES = dict(first=10, attend=12, middle=24, back=20, out_grads=9, in_grads=11, attend_back=11, last=12, rest_grads=6, query_key_grads=6)
PACE = 1e+06
SIZES = (128, 256, 384, 512)
AXES = ("dp", "seq")
bf = jnp.bfloat16
f32 = jnp.float32


def mm(left, right):
    return jnp.dot(left, right, preferred_element_type=f32)


def mm_left(left, right):
    return lax.dot_general(left, right, (((0,), (0,)), ((), ())), preferred_element_type=f32)


def mm_right(left, right):
    return lax.dot_general(left, right, (((1,), (1,)), ((), ())), preferred_element_type=f32)


def exchange(v):
    return lax.all_to_all(v, AXES, 0, 0, tiled=True)


def slots_of(devices):
    return max(16, SLOTS // devices)


def route(ids, valid, per_owner):
    count = ids.shape[0]
    spot = jnp.arange(count, dtype=jnp.int32)
    owner = ids // per_owner
    local = ids - owner * per_owner
    key = jnp.where(valid, ids, -1 - spot)
    alike = key[:, None] == key[None, :]
    first_at = jnp.min(jnp.where(alike, spot[None, :], count), axis=1)
    first = (first_at == spot) & valid
    before = (owner[:, None] == owner[None, :]) & first[None, :] & (spot[None, :] < first_at[:, None])
    rank = jnp.sum(before.astype(jnp.int32), axis=1)
    return owner, local, first, rank


def requests(owner, local, first, rank, start, devices):
    room = slots_of(devices)
    slot = jnp.where(first & (rank >= start) & (rank < start + room), owner * room + rank - start, -1)
    line = jnp.arange(devices * room, dtype=jnp.int32)
    hit = slot[None, :] == line[:, None]
    return jnp.max(jnp.where(hit, local[None, :], -1), axis=1)


def token_slots(owner, valid, rank, start, room):
    return jnp.where(valid & (rank >= start) & (rank < start + room), owner * room + rank - start, -1)


def one_hot(index, size):
    return (index[:, None] == jnp.arange(size, dtype=jnp.int32)[None, :]).astype(bf)


NEAR = 0.3
TAIL = (
    0.11962924781130464, 0.12075473126046088, 0.09990870957740686, 0.12857719637511858,
    -0.05371263258867769, 0.2063844888355699, -0.15722075016774184, 0.03567893567949022,
)


def dot(left, right):
    return jnp.dot(left, right, preferred_element_type=f32)


def dot_nt(left, right):
    return lax.dot_general(left, right, (((1,), (1,)), ((), ())), preferred_element_type=f32)


def dot_tn(left, right):
    return lax.dot_general(left, right, (((0,), (0,)), ((), ())), preferred_element_type=f32)


def iota(shape, axis):
    return lax.broadcasted_iota(jnp.int32, shape, axis)


def normal(v):
    center = v - jnp.mean(v, axis=-1, keepdims=True)
    scale = lax.rsqrt(jnp.mean(center * center, axis=-1, keepdims=True) + EPS)
    return center * scale, scale


def normal_back(grad, unit, scale):
    inner = jnp.mean(grad * unit, axis=-1, keepdims=True)
    return scale * (grad - jnp.mean(grad, axis=-1, keepdims=True) - unit * inner)


def column_sums(v):
    return dot(jnp.full((8, v.shape[0]), 1.0, bf), v)[:1]


def gelu_pair(v):
    bell = jnp.exp(v * v * -0.5)
    t = 1.0 / (1.0 + NEAR * jnp.abs(v))
    poly = TAIL[-1]
    for c in TAIL[-2::-1]:
        poly = poly * t + c
    tail = poly * t * bell
    area = jnp.where(v < 0, tail, 1.0 - tail)
    return v * area, area + v * bell * 0.3989422804014327


def params(limit, **more):
    return pltpu.CompilerParams(vmem_limit_bytes=limit << 20, **more)


def fixed(shape, index):
    return pl.BlockSpec(shape, lambda *_: index, pipeline_mode=pl.Buffered(1))


def spread(staged, depth, turns, src, out):
    width = out.shape[1]
    if not staged:
        out[...] = src[...]
        return

    def pair(index, carry):
        tall = src[pl.ds(pl.multiple_of(index * 2 * depth, 16), 2 * depth), :].astype(f32)
        parts = []
        for e in range(2):
            for j in range(turns):
                parts.append(tall[e * depth : (e + 1) * depth, j * width : (j + 1) * width])
        to = pl.multiple_of(index * 2 * depth * turns, 16)
        out[pl.ds(to, 2 * depth * turns), :] = jnp.concatenate(parts, axis=0).astype(bf)
        return carry

    lax.fori_loop(0, src.shape[0] // (2 * depth), pair, 0)


def live_rows(plan, shape):
    row = iota(shape, 0) + pl.program_id(0) * shape[0]
    return row < plan[0], (row >= plan[2]) & (row < plan[2] + plan[1])


def when_live(kernel):
    def run(*refs):
        pl.when(pl.program_id(0) < refs[0][3])(lambda: kernel(*refs))

    return run


def first_kernel(plan, slot, spot_in, back, extra, w_qkv, pos_t, vec_t, x_out, hin_out, qkv_out, vec_out):
    rows, width = x_out.shape
    length = pos_t.shape[1]
    vec = dot_nt((iota((16, 128), 0) == iota((16, 128), 1)).astype(f32).astype(bf), vec_t[...])
    vec_out[...] = vec
    where = jnp.where(slot[...] == iota((rows, back.shape[0]), 1), 1.0, 0.0).astype(bf)
    line = jnp.where(spot_in[...] == iota((rows, length), 1), 1.0, 0.0).astype(bf)
    x = dot(where, back[...]) + extra[...].astype(f32) + dot_nt(line, pos_t[...])
    x_out[...] = x
    unit, _ = normal(x)
    hin = (unit * vec[0:1] + vec[1:2]).astype(bf)
    hin_out[...] = hin
    qkv_out[:, :width] = (dot(hin, w_qkv[:, :width]) + vec[2:3]).astype(bf)
    qkv_out[:, width : 2 * width] = dot(hin, w_qkv[:, width : 2 * width]).astype(bf)
    qkv_out[:, 2 * width :] = (dot(hin, w_qkv[:, 2 * width :]) + vec[3:4]).astype(bf)


def head_parts(size, query, keys, half):
    shape = query.shape
    lane = iota(shape, 1)
    live = iota(shape, 0) < size
    inside = ((lane // HEAD_DIM) == half) & live
    spare = lane == (1 - half) * HEAD_DIM
    key = jnp.where(inside, keys.astype(f32), jnp.where(spare & ~live, -1e30, 0.0)).astype(bf)
    ask = jnp.where(inside, query.astype(f32) * 0.125, jnp.where(spare, 1.0, 0.0)).astype(bf)
    return inside, ask, key


def each_sentence(plan, run):
    def one(index, carry):
        size = jnp.where(index == 0, plan[0], plan[1])
        start = pl.multiple_of(jnp.where(index == 0, 0, plan[2]), 16)
        under = 0
        for count in SIZES:
            pl.when((size > under) & (size <= count))(functools.partial(run, pl.ds(start, count), size))
            under = count
        return carry

    lax.fori_loop(0, 2, one, 0)


def attend_kernel(plan, query, keys, values, out):
    out[...] = jnp.zeros_like(out)

    def run(rows, size):
        total = None
        for half in range(2):
            inside, ask, key = head_parts(size, query[rows, :], keys[rows, :], half)
            score = dot_nt(ask, key)
            power = jnp.exp(score - jnp.max(score, axis=1, keepdims=True))
            prob = (power * (1.0 / jnp.sum(power, axis=1, keepdims=True))).astype(bf)
            part = dot(prob, jnp.where(inside, values[rows, :].astype(f32), 0.0).astype(bf))
            total = part if total is None else total + part
        out[rows, :] = total.astype(bf)

    each_sentence(plan, run)


def attend_back_kernel(plan, query, keys, values, d_out, *more):
    d_proj = more[-1]
    d_proj[...] = jnp.zeros_like(d_proj)
    plus = lambda a, b: b if a is None else a + b

    def run(rows, size):
        d_query, d_key, d_value = None, None, None
        for half in range(2):
            inside, ask, key = head_parts(size, query[rows, :], keys[rows, :], half)
            clean = lambda v: jnp.where(inside, v.astype(f32), 0.0).astype(bf)
            score = dot_nt(key, ask)
            power = jnp.exp(score - jnp.max(score, axis=0, keepdims=True))
            prob = power * (1.0 / jnp.sum(power, axis=0, keepdims=True))
            grad = clean(d_out[rows, :])
            d_value = plus(d_value, dot(prob.astype(bf), grad))
            d_prob = dot_nt(clean(values[rows, :]), grad)
            inner = jnp.sum(prob * d_prob, axis=0, keepdims=True)
            d_score = (prob * (d_prob - inner)).astype(bf)
            d_key = plus(d_key, dot(d_score, clean(ask)))
            d_query = plus(d_query, dot_tn(d_score, clean(key)))
        d_proj[0, rows, :] = (d_query * 0.125).astype(bf)
        d_proj[1, rows, :] = d_key.astype(bf)
        d_proj[2, rows, :] = d_value.astype(bf)

    each_sentence(plan, run)


def middle_kernel(staged, depth, turns, plan, x, mixed, w_out, w_in, w_src, vec, vec_ff, z1_out, h1_out, act_out, slope_out, z2_out, pooled, w_back):
    rows, width = x.shape
    pl.when(pl.program_id(0) == 0)(lambda: spread(staged, depth, turns, w_src, w_back))
    unit, _ = normal(x[...])
    h0 = unit * vec[0:1] + vec[1:2]
    z1 = h0 + dot(mixed[...], w_out[...]) + vec[4:5]
    z1_out[...] = z1
    unit, _ = normal(z1)
    h1 = unit * vec[5:6] + vec[6:7]
    h1_b = h1.astype(bf)
    h1_out[...] = h1_b
    y = None
    for j in range(turns):
        at = slice(j * width, (j + 1) * width)
        hidden = dot(h1_b, w_in[:, at]) + vec_ff[:, at]
        act, slope = gelu_pair(hidden)
        act = act.astype(bf)
        act_out[:, at] = act
        slope_out[:, at] = slope.astype(bf)
        part = dot(act, w_back[at, :])
        y = part if y is None else y + part
    z2 = h1 + y + vec[7 + turns : 8 + turns]
    z2_out[...] = z2
    unit, _ = normal(z2)
    h2 = unit * vec[8 + turns : 9 + turns] + vec[9 + turns : 10 + turns]
    sums = [jnp.sum(jnp.where(keep, h2, 0.0), axis=0, keepdims=True) for keep in live_rows(plan, (rows, width))]

    @pl.when(pl.program_id(0) == 0)
    def _():
        pooled[...] = jnp.zeros_like(pooled)

    line = iota(pooled.shape, 0)
    pooled[...] += jnp.where(line == 0, sums[0], jnp.where(line == 1, sums[1], 0.0))


def back_kernel(plan, facts, holders, pooled, all_pooled, z1, slope, z2, w_out, w_in, w_back, vec, d_y_out, d_f_out, d_r1_out, d_a_out, d_o_out, sums, sums_ff, loss):
    rows, width = z1.shape
    step = pl.program_id(0)
    total = lambda a, b: jnp.sum(a * b, axis=1, keepdims=True)
    count = facts[8]
    grads, losses = [], []
    for i in range(2):
        labeled, size, other_size, counts = (facts[4 * i + j] for j in range(4))
        holder, late, keeper, at = (holders[4 * i + j] for j in range(4))
        own, other = pooled[i : i + 1] / size, all_pooled[holder, pl.ds(late, 1), :] / other_size
        gold = all_pooled[keeper, 2:3, :]
        gold = jnp.sum(jnp.where(iota(gold.shape, 1) == at, gold, 0.0), axis=1, keepdims=True)
        cross = total(own, other)
        root, other_root = lax.rsqrt(total(own, own) + EPS), lax.rsqrt(total(other, other) + EPS)
        miss = cross * root * other_root - gold
        losses.append(counts * miss * miss)
        push = 2.0 * labeled * miss / count
        grads.append(push * (other * root * other_root - cross * root * root * root * other_root * own) / size)
    loss[...] = jnp.broadcast_to(losses[0] + losses[1], loss.shape)
    keep = live_rows(plan, (rows, width))
    d_h2 = jnp.where(keep[0], grads[0], jnp.where(keep[1], grads[1], 0.0))
    turns = w_in.shape[1] // width

    unit, scale = normal(z2[...])
    d_g2 = jnp.sum(d_h2 * unit, axis=0, keepdims=True)
    d_b2n = jnp.sum(d_h2, axis=0, keepdims=True)
    d_r2 = normal_back(d_h2 * vec[8 + turns : 9 + turns], unit, scale)
    d_y = d_r2.astype(bf)
    d_y_out[...] = d_y
    d_h1 = d_r2
    ff = []
    for j in range(turns):
        at = slice(j * width, (j + 1) * width)
        d_f = (dot_nt(d_y, w_back[at, :]) * slope[:, at].astype(f32)).astype(bf)
        d_f_out[:, at] = d_f
        ff.append(column_sums(d_f))
        d_h1 = d_h1 + dot_nt(d_f, w_in[:, at])
    unit, scale = normal(z1[...])
    d_g1 = jnp.sum(d_h1 * unit, axis=0, keepdims=True)
    d_b1 = jnp.sum(d_h1, axis=0, keepdims=True)
    d_r1 = normal_back(d_h1 * vec[5:6], unit, scale)
    d_r1_out[...] = d_r1
    d_a = d_r1.astype(bf)
    d_a_out[...] = d_a
    d_o_out[...] = dot_nt(d_a, w_out[...]).astype(bf)
    fresh = jnp.concatenate([column_sums(d_a), d_g1, d_b1, column_sums(d_y), d_g2, d_b2n, d_g2, d_b2n], axis=0)

    @pl.when(step == 0)
    def _():
        sums[...] = jnp.zeros_like(sums)
        sums_ff[...] = jnp.zeros_like(sums_ff)

    sums[...] += fresh
    sums_ff[...] += jnp.concatenate(ff, axis=0)


def last_kernel(plan, slot, x, d_r1, d_proj, w_qkv, vec, d_x_out, sums, rows_out, total):
    rows, width = x.shape
    step = pl.program_id(0)
    d_h0 = d_r1[...]
    for i in range(3):
        d_h0 = d_h0 + dot_nt(d_proj[i], w_qkv[:, i * width : (i + 1) * width])
    unit, scale = normal(x[...])
    d_ge = jnp.sum(d_h0 * unit, axis=0, keepdims=True)
    d_be = jnp.sum(d_h0, axis=0, keepdims=True)
    d_x = normal_back(d_h0 * vec[0:1], unit, scale)
    d_xb = d_x.astype(bf)
    d_x_out[...] = d_xb
    bias_q, bias_v = column_sums(d_proj[0]), column_sums(d_proj[2])
    fresh = jnp.concatenate([d_ge, d_be, bias_q, bias_v, d_ge, d_be, bias_q, bias_v], axis=0)
    hit = jnp.where(slot[...] == iota((rows, rows_out.shape[0]), 1), 1.0, 0.0).astype(bf)

    @pl.when(step == 0)
    def _():
        sums[...] = jnp.zeros_like(sums)
        total[...] = jnp.zeros_like(total)

    sums[...] += fresh
    total[...] += dot_tn(hit, d_xb)

    @pl.when(step == plan[3] - 1)
    def _():
        rows_out[...] = total[...].astype(bf)


def blocks(v, depth):
    return v.reshape(v.shape[0] // depth, depth, v.shape[1])


def put_split(outs, order, kind, g, mine):
    keep, send = outs
    for z in range(2):
        for y in range(2):
            for x in range(2):
                owner = 2 * (4 * z + 2 * y + x)
                at = tuple({"z": z, "y": y, "x": x}[axis] for axis in order) + (kind,)
                even, odd = g[owner], g[owner + 1]
                keep[at] = jnp.where(mine == 0, even, odd).astype(bf)
                send[at] = jnp.where(mine == 0, odd, even).astype(bf)


def by_blocks(plan, run):
    for count in range(2, BLOCKS + 1):
        pl.when(plan[3] == count)(functools.partial(run, count * ROWS))


def out_grads_kernel(depth, turns, plan, act, d_y, h1, d_f, *outs):
    width = d_y.shape[1]

    def run(rows):
        g = dot_tn(act[:rows], d_y[:rows])
        g = g.reshape(16, turns, depth, width)
        for j in range(turns):
            put_split(outs, "xyz", j, g[:, j], plan[4])
        for j in range(turns // 2):
            put_split(outs, "xyz", turns + j, blocks(dot_tn(h1[:rows], d_f[:rows, j * width : (j + 1) * width]), depth), plan[4])

    by_blocks(plan, run)


def in_grads_kernel(depth, turns, plan, h1, d_f, mixed, d_a, *outs):
    width = d_a.shape[1]

    def run(rows):
        for j in range(turns // 2):
            put_split(outs, "yxz", j, blocks(dot_tn(h1[:rows], d_f[:rows, j * width : (j + 1) * width]), depth), plan[4])
        put_split(outs, "yxz", turns // 2, blocks(dot_tn(mixed[:rows], d_a[:rows]), depth), plan[4])

    by_blocks(plan, run)


def query_key_grads_kernel(depth, plan, hin, d_proj, *outs):
    def run(rows):
        for i in range(2):
            put_split(outs, "xyz", i, blocks(dot_tn(hin[:rows], d_proj[i, :rows]), depth), plan[4])

    by_blocks(plan, run)


def rest_grads_kernel(depth, length, plan, spot_in, hin, d_value, d_x, sums_0, sums, sums_ff, *outs):
    width = d_value.shape[2]
    part = hin.shape[1]

    def run(rows):
        put_split(outs, "yxz", 0, blocks(dot_tn(hin[:rows], d_value[0, :rows]), depth), plan[4])
        line = jnp.where(spot_in[:rows] == iota((rows, length), 1), 1.0, 0.0).astype(bf)
        g_pos = dot_tn(d_x[:rows], line)
        vec = jnp.concatenate([sums_0[:4], sums[:3], sums_ff[...], sums[3:6]], axis=0)
        vec = jnp.concatenate([vec, jnp.zeros((128 - vec.shape[0], part), f32)], axis=0)
        both = jnp.concatenate([g_pos, vec.T, jnp.zeros((part, width - length - 128), f32)], axis=1)
        put_split(outs, "yxz", 1, blocks(both, depth), plan[4])

    by_blocks(plan, run)


def update_kernel(turns, scale, g_embed, dense_out, dense_in, rest, g_position, g_vectors, *refs):
    factor = scale[0]
    weights, moms, avgs, news, next_moms, next_avgs = (refs[7 * i : 7 * i + 7] for i in range(6))

    def one(index, at, grad):
        clipped = grad * factor
        moment = MOMENT * moms[index][at] + clipped
        fresh = weights[index][at] - RATE * (clipped + MOMENT * moment)
        next_moms[index][at] = moment
        news[index][at] = fresh
        next_avgs[index][at] = DECAY * avgs[index][at] + (1.0 - DECAY) * fresh

    every = (slice(None), slice(None))
    one(0, every, g_embed[...])

    @pl.when(pl.program_id(0) == 0)
    def _():
        depth, width = rest.shape[1:]
        cols = lambda j: (slice(None), slice(j * width, (j + 1) * width))
        one(1, every, g_position[...])
        for j in range(3):
            one(2, cols(j), rest[j])
        one(3, every, dense_in[turns])
        for j in range(turns):
            one(4, cols(j), dense_in[j])
            one(5, (slice(j * depth, (j + 1) * depth), slice(None)), dense_out[j])
        one(6, every, g_vectors[...])


def cost(micros):
    return pl.CostEstimate(flops=0, bytes_accessed=int(micros * PACE), transcendentals=0)


def run_forward_backward(full, back, extra, slots, spots, plan, meet, staged, devices, depth, length, hidden):
    width = back.shape[1]
    rows = slots.shape[0]
    turns = hidden // width
    pairs = width // GROUP
    shape = jax.ShapeDtypeStruct
    at_row = lambda i, plan: jnp.minimum(i, plan[3] - 1)
    row = lambda cols: pl.BlockSpec((ROWS, cols), lambda i, plan, *_: (at_row(i, plan), 0))
    column = lambda block: fixed((width, width), (0, block))
    at_back = 4 * width + hidden
    whole_out = lambda *dims: pl.BlockSpec(dims, lambda *_: (0,) * len(dims))

    def call(kernel, prefetch, grid, in_specs, out_specs, out_shape, name, scratch=(), **more):
        return pl.pallas_call(
            kernel,
            grid_spec=pltpu.PrefetchScalarGridSpec(
                num_scalar_prefetch=prefetch, grid=grid, in_specs=in_specs, out_specs=out_specs, scratch_shapes=list(scratch)
            ),
            out_shape=out_shape,
            compiler_params=params(60),
            cost_estimate=cost(TIMES[name]),
            name=name,
            **more,
        )

    w_src, w_src_spec = full, fixed((width, turns * width), (0, at_back // (turns * width)))
    if not staged:
        w_src = full[:, at_back : at_back + turns * width].reshape(devices, depth, turns, width)
        w_src, w_src_spec = w_src.transpose(0, 2, 1, 3).reshape(hidden, width), fixed((hidden, width), (0, 0))

    at_pos = at_back + turns * width
    at_vec = at_pos + length
    w_qkv_spec = fixed((width, 3 * width), (0, 0))
    w_out_spec = column(3)
    w_in_spec = fixed((width, hidden), (0, 4 * width // hidden))
    w_back_spec = fixed((hidden, width), (0, 0))
    vec_spec = fixed((16, width), (0, 0))

    x, hin, qkv, vec = call(
        when_live(first_kernel), 1, (BLOCKS,),
        [
            row(1), row(1), fixed(back.shape, (0, 0)), row(width), w_qkv_spec,
            fixed((width, length), (0, at_pos // length)), fixed((width, 128), (0, at_vec // 128)),
        ],
        [row(width), row(width), row(3 * width), whole_out(16, width)],
        [shape((rows, width), f32), shape((rows, width), bf), shape((rows, 3 * width), bf), shape((16, width), f32)],
        "first",
    )(plan, slots[:, None], spots[:, None], back, extra, full, full, full)

    block = lambda part, start=0: pl.BlockSpec((rows, GROUP), lambda p, *_: (0, part * pairs + start + p))
    mixed = call(
        attend_kernel, 1, (pairs,), [block(0), block(1), block(2)], block(0), shape((rows, width), bf), "attend"
    )(plan, qkv, qkv, qkv)

    vec_ff = vec[7 : 7 + turns].reshape(1, hidden)
    z1, h1, act, slope, z2, pooled, w_back = call(
        when_live(functools.partial(middle_kernel, staged, depth, turns)), 1, (BLOCKS,),
        [row(width), row(width), w_out_spec, w_in_spec, w_src_spec, vec_spec, fixed((1, hidden), (0, 0))],
        [row(width), row(width), row(hidden), row(hidden), row(width), whole_out(8, width), whole_out(hidden, width)],
        [
            shape((rows, width), f32), shape((rows, width), bf), shape((rows, hidden), bf), shape((rows, hidden), bf),
            shape((rows, width), f32), shape((8, width), f32), shape((hidden, width), bf),
        ],
        "middle",
    )(plan, x, mixed, full, full, w_src, vec, vec_ff)

    holders, facts, goal = meet
    all_pooled = exchange(jnp.broadcast_to(jnp.concatenate([pooled[:2], goal], axis=0)[None], (devices, 3, width)))
    d_y, d_f, d_r1, d_a, d_o, sums, sums_ff, loss = call(
        when_live(back_kernel), 3, (BLOCKS,),
        [
            fixed((8, width), (0, 0)), fixed((devices, 3, width), (0, 0, 0)), row(width), row(hidden), row(width), w_out_spec, w_in_spec,
            w_back_spec, vec_spec,
        ],
        [
            row(width), row(hidden), row(width), row(width), row(width), whole_out(8, width), whole_out(turns, width),
            whole_out(8, 128),
        ],
        [
            shape((rows, width), bf), shape((rows, hidden), bf), shape((rows, width), f32), shape((rows, width), bf), shape((rows, width), bf),
            shape((8, width), f32), shape((turns, width), f32), shape((8, 128), f32),
        ],
        "back",
    )(plan, facts, holders, pooled, all_pooled, z1, slope, z2, full, full, w_back, vec)

    part = width // 2
    halves = lambda cols: pl.BlockSpec((rows, cols), lambda i, *_: (0, i))
    live = (jnp.arange(rows) < plan[3] * ROWS)[:, None]
    clean = lambda v: jnp.where(live, v, 0)

    def split_call(kernel, in_specs, streams, name):
        specs, shapes = [], []
        for order, kinds in streams:
            at = order.index("z")
            dims = tuple(4 if axis == "z" else 2 for axis in order) + (kinds, depth, width)
            index = lambda i, *_, at=at: tuple(i if axis == at else 0 for axis in range(6))
            specs += [pl.BlockSpec((2, 2, 2, kinds, depth, width), index)] * 2
            shapes += [shape(dims, bf)] * 2
        return call(kernel, 1, (2,), in_specs, specs, shapes, name)

    if staged:
        z, y, x_at = place_in_slice()
        dense_out = split_call(
            functools.partial(out_grads_kernel, depth, turns),
            [halves(hidden // 2), fixed((rows, width), (0, 0)), halves(part), fixed((rows, hidden // 2), (0, 0))],
            [("xyz", turns + turns // 2)],
            "out_grads",
        )(plan, act, d_y, h1, d_f)
        dense_out = over_cores(*dense_out)
        dense_in = split_call(
            functools.partial(in_grads_kernel, depth, turns),
            [halves(part), fixed((rows, hidden // 2), (0, 1)), halves(part), fixed((rows, width), (0, 0))],
            [("yxz", turns // 2 + 1)],
            "in_grads",
        )(plan, h1, d_f, mixed, d_a)
        d_o, dense_out, dense_in = lax.optimization_barrier((d_o, dense_out, dense_in))
        dense_in = over_cores(*dense_in)
        dense_out = halve(dense_out, x_at, 2)
    else:
        dense_out = dot_tn(clean(act), clean(d_y)).astype(bf)
        dense_in = jnp.concatenate([dot_tn(clean(h1), clean(d_f)), dot_tn(clean(mixed), clean(d_a))], axis=1).astype(bf)

    def attend_back(start, count, total):
        more = () if total is None else (total,)
        return call(
            attend_back_kernel, 1, (count,),
            [block(0, start), block(1, start), block(2, start), block(0, start)] + [pl.BlockSpec(memory_space=pl.ANY)] * len(more),
            pl.BlockSpec((3, rows, GROUP), lambda p, *_: (0, 0, start + p)),
            shape((3, rows, width), bf),
            "attend_back",
            input_output_aliases={5: 0} if more else {},
        )(plan, qkv, qkv, qkv, d_o, *more)

    d_proj = attend_back(0, pairs, None)
    if staged:
        d_proj, dense_in = lax.optimization_barrier((d_proj, dense_in))
        in_sums = two_sums(dense_in, y)
        d_proj, in_sums = lax.optimization_barrier((d_proj, in_sums))
        dense_in = in_sums[0], swap(in_sums[1], 4, 32)
    if staged:
        first_rest = split_call(
            functools.partial(query_key_grads_kernel, depth),
            [halves(part), pl.BlockSpec((2, rows, width), lambda i, *_: (0, 0, 0), pipeline_mode=pl.Buffered(1))],
            [("xyz", 2)],
            "query_key_grads",
        )(plan, hin, d_proj)
        d_proj, dense_out, first_rest = lax.optimization_barrier((d_proj, dense_out, first_rest))
        first_rest = over_cores(*first_rest)

    d_xb, sums_0, give_rows = call(
        when_live(last_kernel), 1, (BLOCKS,),
        [
            row(1), row(width), row(width), pl.BlockSpec((3, ROWS, width), lambda i, plan: (0, at_row(i, plan), 0)), w_qkv_spec, vec_spec,
        ],
        [row(width), whole_out(8, width), whole_out(*back.shape)],
        [shape((rows, width), bf), shape((8, width), f32), shape(back.shape, bf)],
        "last",
        scratch=[pltpu.VMEM(back.shape, f32)],
    )(plan, slots[:, None], x, d_r1, d_proj, full, vec)

    if staged:
        give_rows, dense_in = lax.optimization_barrier((give_rows, dense_in))
        out_sums, in_sums = two_sums(dense_out, y), two_sums(dense_in, x_at)
        d_xb, out_sums, in_sums = lax.optimization_barrier((d_xb, out_sums, in_sums))
        dense_out = out_sums[0], swap(out_sums[1], 4, 32)
        dense_in = in_sums[0], swap(in_sums[1], 2, 32)
        cols = lambda count: pl.BlockSpec((count, part), lambda i, *_: (0, i))
        rest = split_call(
            functools.partial(rest_grads_kernel, depth, length),
            [
                fixed((rows, 1), (0, 0)), halves(part), pl.BlockSpec((1, rows, width), lambda i, *_: (2, 0, 0), pipeline_mode=pl.Buffered(1)),
                halves(part), cols(8), cols(8), cols(turns),
            ],
            [("yxz", 2)],
            "rest_grads",
        )(plan, spots[:, None], hin, d_proj, d_xb, sums_0, sums, sums_ff)
        rest = first_rest, over_cores(*rest)
    else:
        g_vec = jnp.concatenate([sums_0[:4], sums[:3], sums_ff, sums[3:6]], axis=0)
        g_pos = dot_tn(clean(d_xb), one_hot(spots, length))
        spare = jnp.zeros((width, width - length - g_vec.shape[0]), f32)
        rest = [dot_tn(clean(hin), clean(d_proj[i])) for i in range(3)] + [jnp.concatenate([g_pos, g_vec.T, spare], axis=1)]
        rest = jnp.concatenate(rest, axis=1).astype(bf)
    return loss[0, 0], dense_out, dense_in, rest, clean(d_xb), give_rows


def swap(v, bit, devices):
    return lax.ppermute(v, AXES, [(i, i ^ bit) for i in range(devices)])


def add(a, b):
    return (a.astype(f32) + b.astype(f32)).astype(bf)


def spot(v, axis, index):
    return lax.dynamic_index_in_dim(v, index, axis, keepdims=False)


def place_in_slice():
    row = lax.axis_index("dp")
    return row // 2, lax.rem(row, 2), lax.axis_index("seq") // 2


def over_cores(keep, send):
    return keep, swap(send, 1, 32)


def part_sum(pair, index):
    return add(spot(pair[0], 0, index), spot(pair[1], 0, index))


def two_sums(pair, index):
    return part_sum(pair, index), part_sum(pair, 1 - index)


def halve(pair, index, bit):
    return part_sum(pair, index), swap(part_sum(pair, 1 - index), bit, 32)


def over_long(pair, z):
    return [part_sum(pair, z)] + [swap(part_sum(pair, z ^ step), 8 * step, 32) for step in range(1, 4)]


def z_parts(one, two, z):
    return [jnp.concatenate([part_sum(one, z ^ step), part_sum(two, z ^ step)], axis=0) for step in range(4)]


def z_swaps(parts):
    return parts[:1] + [swap(parts[step], 8 * step, 32) for step in range(1, 4)]


def over_long_both(one, two, z):
    part = lambda step: jnp.concatenate([part_sum(one, z ^ step), part_sum(two, z ^ step)], axis=0)
    return [part(0)] + [swap(part(step), 8 * step, 32) for step in range(1, 4)]


def total_of(parts):
    return sum(p.astype(f32) for p in parts)


def body(
    token_ids, lengths, labeled, gold,
    embed, position, attn_in, attn_out, ff_in, ff_out, vectors,
    mom_embed, mom_position, mom_attn_in, mom_attn_out, mom_ff_in, mom_ff_out, mom_vectors,
    avg_embed, avg_position, avg_attn_in, avg_attn_out, avg_ff_in, avg_ff_out, avg_vectors,
):
    pairs_here, _, local = token_ids.shape
    seq = lax.axis_size("seq")
    devices = lax.axis_size("dp") * seq
    length = local * seq
    per_owner, width = embed.shape
    depth = attn_in.shape[0]
    hidden = ff_in.shape[1]
    nvec = vectors.shape[0]
    turns = ff_out.shape[0] // depth
    rows = BLOCKS * ROWS
    room = slots_of(devices)
    spare = 128 - nvec

    shard = jnp.concatenate(
        [attn_in, attn_out, ff_in]
        + [ff_out[i * depth : (i + 1) * depth] for i in range(turns)]
        + [position.T, vectors.T, jnp.zeros((depth, spare), f32)],
        axis=1,
    ).astype(bf)
    full = lax.all_gather(shard, AXES, axis=0, tiled=True)

    group = 2 * pairs_here
    info = jnp.concatenate([lengths.reshape(1, group), labeled.reshape(1, pairs_here)], axis=1)
    info = jnp.pad(info, ((0, 0), (0, local - group - pairs_here)))
    news = jnp.concatenate([token_ids.reshape(group, local), info], axis=0)
    news = exchange(jnp.broadcast_to(news[None], (devices,) + news.shape)).reshape(devices // seq, seq, group + 1, local)
    lens = news[:, 0, group, :group].reshape(2 * devices)
    lab = news[:, 0, group, group : group + pairs_here].reshape(devices)
    live = jnp.where(jnp.repeat(lab, 2) > 0, lens, 0)
    index = jnp.arange(2 * devices, dtype=jnp.int32)
    ahead = (live[None, :] > live[:, None]) | ((live[None, :] == live[:, None]) & (index[None, :] < index[:, None]))
    order = jnp.sum(ahead.astype(jnp.int32), axis=1)
    me = lax.axis_index("dp") * seq + lax.axis_index("seq")
    ranks = jnp.stack([me, 2 * devices - 1 - me])
    picked = order[None, :] == ranks[:, None]
    take = lambda values, i: jnp.sum(jnp.where(index[: values.shape[0]] == i, values, 0))
    chosen = list(jnp.sum(jnp.where(picked, index[None, :], 0), axis=1))
    count = jnp.maximum(jnp.sum(lab).astype(f32), 1.0)
    size = list(jnp.sum(jnp.where(picked, live[None, :], 0), axis=1))
    start = (size[0] + 15) // 16 * 16
    among = picked.reshape(2, devices // seq, 1, group, 1)
    two_ids = jnp.sum(jnp.where(among, news[None, :, :, :group, :], 0), axis=(1, 3)).reshape(2, length)
    ids = lax.dynamic_update_slice(jnp.pad(two_ids[0], (0, rows - length)), two_ids[1], (start,))
    line = jnp.arange(rows, dtype=jnp.int32)
    in_first, in_second = line < size[0], (line >= start) & (line < start + size[1])
    used = in_first | in_second
    spots = jnp.where(in_first, line, jnp.where(in_second, line - start, -1))
    total = jnp.where(size[1] > 0, start + size[1], size[0])
    core = lax.rem(lax.axis_index("seq"), 2)
    plan = jnp.stack([size[0], size[1], start, jnp.clip((total + ROWS - 1) // ROWS, 2, BLOCKS), core])
    owner, place, first, rank = route(ids, used, per_owner)
    most = jnp.max(jnp.where(used, rank + 1, 0))
    asked = requests(owner, place, first, rank, 0, devices).reshape(devices, room)
    note = jnp.broadcast_to(most, (devices, 1))
    got = exchange(jnp.concatenate([asked, note, jnp.zeros((devices, 127 - room), jnp.int32)], axis=1))
    rounds = (jnp.max(got[:, room]) + room - 1) // room

    table = embed.astype(bf)
    slots = token_slots(owner, used, rank, 0, room)
    wanted_first = got[:, :room].reshape(-1)

    def pick(wanted):
        picked = mm(one_hot(wanted, per_owner), table).astype(bf).reshape(devices, room, width)
        return exchange(picked).reshape(devices * room, width)

    back = pick(wanted_first)

    def ask_again(start):
        return exchange(requests(owner, place, first, rank, start, devices).reshape(devices, room)).reshape(-1)

    def more(state):
        step, total = state
        start = step * room
        there = one_hot(token_slots(owner, used, rank, start, room), devices * room)
        return step + 1, total + mm(there, pick(ask_again(start))).astype(bf)

    _, extra = lax.while_loop(lambda state: state[0] < rounds, more, (jnp.int32(1), jnp.zeros((rows, width), bf)))

    holders, facts = [], []
    for i in chosen:
        other, pair = i ^ 1, i // 2
        rank = take(order, other)
        late = rank >= devices
        holders += [jnp.where(late, 2 * devices - 1 - rank, rank), late.astype(jnp.int32), pair // pairs_here * seq, lax.rem(pair, pairs_here)]
        weight = take(lab, pair).astype(f32)
        own = jnp.where(lax.rem(i, 2) == 0, weight, 0.0)
        facts += [weight, take(lens, i).astype(f32), take(lens, other).astype(f32), own]
    goal = jnp.pad(gold[None, :], ((0, 0), (0, width - pairs_here)))
    holders, facts, goal, plan, slots = lax.optimization_barrier((jnp.stack(holders), jnp.stack(facts + [count]), goal, plan, slots))
    meet = holders, facts, goal

    staged = (seq, devices) == (4, 32) and depth == 24
    loss, dense_out, dense_in, rest, d_xb, give_rows = run_forward_backward(
        full, back, extra, slots, spots, plan, meet, staged, devices, depth, length, hidden
    )

    give_rows = exchange(give_rows.reshape(devices, room, width))
    if staged:
        z, y, x = place_in_slice()
        parts = z_parts(dense_out, dense_in, z)
        parts, rest = lax.optimization_barrier((parts, rest))
        dense = z_swaps(parts)
        rest = halve(rest[0], x, 2), halve(rest[1], y, 4)
        rest = halve(rest[0], y, 4), halve(rest[1], x, 2)
        dense, rest, give_rows = lax.optimization_barrier((dense, rest, give_rows))
        rest = over_long_both(*rest, z)
        dense, rest = total_of(dense), total_of(rest)
        dense_out, dense_in = dense[:turns], dense[turns:]
    else:
        sum_up = lambda parts: lax.psum_scatter(parts, AXES, scatter_dimension=0, tiled=True).astype(f32)
        kinds = lambda v: v.reshape(depth, -1, width).transpose(1, 0, 2)
        dense_out, dense_in, rest = sum_up(dense_out).reshape(turns, depth, width), kinds(sum_up(dense_in)), kinds(sum_up(rest))
    g_position = rest[3, :, :length]
    g_vectors = rest[3, :, length : length + nvec].T

    def give(wanted, there):
        return mm_left(one_hot(wanted, per_owner), there.reshape(devices * room, width))

    def more_back(state):
        step, total = state
        start = step * room
        sums = mm_left(one_hot(token_slots(owner, used, rank, start, room), devices * room), d_xb).astype(bf)
        return step + 1, total + give(ask_again(start), exchange(sums.reshape(devices, room, width)))

    _, g_embed = lax.while_loop(lambda state: state[0] < rounds, more_back, (jnp.int32(1), give(wanted_first, give_rows)))

    squares = sum(jnp.sum(g * g) for g in (g_embed, dense_out, dense_in, rest))
    sums = exchange(jnp.broadcast_to(jnp.stack([squares, loss])[None, :], (devices, 2)))
    sums = jnp.sum(sums, axis=0)
    norm = jnp.sqrt(sums[0])
    loss_sum = sums[1]
    scale = jnp.minimum(1.0, CLIP / (norm + 1e-06))
    state = (
        embed, position.T, attn_in, attn_out, ff_in, ff_out, vectors,
        mom_embed, mom_position.T, mom_attn_in, mom_attn_out, mom_ff_in, mom_ff_out, mom_vectors,
        avg_embed, avg_position.T, avg_attn_in, avg_attn_out, avg_ff_in, avg_ff_out, avg_vectors,
    )
    steps = next(n for n in (2, 5, 4, 3, 1) if per_owner % (8 * n) == 0 or n == 1)
    strip = pl.BlockSpec((per_owner // steps, width), lambda i, *_: (i, 0))
    whole = lambda v: strip if v.shape == embed.shape else fixed(v.shape, (0,) * v.ndim)
    whole_out = lambda v: strip if v.shape == embed.shape else pl.BlockSpec(v.shape, lambda *_: (0,) * v.ndim)
    inputs = (g_embed, dense_out, dense_in, rest, g_position, g_vectors) + state
    done = pl.pallas_call(
        functools.partial(update_kernel, turns),
        grid_spec=pltpu.PrefetchScalarGridSpec(
            num_scalar_prefetch=1, grid=(steps,), in_specs=[whole(v) for v in inputs], out_specs=[whole_out(v) for v in state]
        ),
        out_shape=[jax.ShapeDtypeStruct(v.shape, f32) for v in state],
        compiler_params=params(60),
        name="update",
    )(scale[None], *inputs)
    done = [v.T if i % 7 == 1 else v for i, v in enumerate(done)]
    return (loss_sum, count, norm, *done)


def solution(mesh):
    whole = (
        P(AXES, None),
        P(None, AXES),
        P(AXES, None),
        P(AXES, None),
        P(AXES, None),
        P(AXES, None),
        P(None, AXES),
    )
    return jax.shard_map(
        body,
        mesh=mesh,
        in_specs=(P("dp", None, "seq"), P("dp", None), P("dp"), P("dp")) + whole * 3,
        out_specs=(P(), P(), P()) + whole * 3,
        check_vma=False,
    )
```
